32 devices in a mesh: dp: 16 (over z, y, x), rep: 2 (over core).
Axes of the slice: x: 2, y: 2, z: 4, core: 2. Of those that a mesh axis runs over, the one named last changes fastest.
Arguments:
- tokens: bfloat16 [14336, 768], P(('dp', 'rep')), may hold values from -6 to 6
- project_in: bfloat16 [768, 2304], P('dp'), may hold values from -0.21875 to 0.21875
- project_out: bfloat16 [768, 768], P('dp'), may hold values from -0.875 to 0.875
- expand_weight: bfloat16 [768, 3072], P('dp'), may hold values from -0.21875 to 0.21875
- reduce_weight: bfloat16 [3072, 768], P('dp'), may hold values from -0.109375 to 0.109375
- first_gain: float32 [768], replicated, may hold values from 0.5 to 1.5
- first_shift: float32 [768], replicated, may hold values from -3 to 3
- query_value_bias: float32 [2, 768], replicated, may hold values from -3 to 3
- output_bias: float32 [768], replicated, may hold values from -3 to 3
- mixer_scale: float32 [768], replicated, may hold values from 0.3 to 1.5
- second_gain: float32 [768], replicated, may hold values from 0.5 to 1.5
- second_shift: float32 [768], replicated, may hold values from -3 to 3
- hidden_bias: float32 [3072], replicated, may hold values from -3 to 3
- return_bias: float32 [768], replicated, may hold values from -3 to 3
- feed_scale: float32 [768], replicated, may hold values from 0.3 to 1.5
- position_table: float32 [2, 127, 12], replicated, may hold values from -3 to 3
- image_sizes: int32 [32, 2], P(('dp', 'rep')), may hold values from 1 to 64, as said below
- cotangent: bfloat16 [14336, 768], P(('dp', 'rep')), may hold values from -6 to 6
Outputs:
- outputs: bfloat16 [14336, 768], P(('dp', 'rep'))
- input_grad: float32 [14336, 768], P(('dp', 'rep'))
- grad_project_in: float32 [768, 2304], P('dp')
- grad_project_out: float32 [768, 768], P('dp')
- grad_expand: float32 [768, 3072], P('dp')
- grad_reduce: float32 [3072, 768], P('dp')
- grad_first_gain: float32 [768], replicated
- grad_first_shift: float32 [768], replicated
- grad_query_value_bias: float32 [2, 768], replicated
- grad_output_bias: float32 [768], replicated
- grad_mixer_scale: float32 [768], replicated
- grad_second_gain: float32 [768], replicated
- grad_second_shift: float32 [768], replicated
- grad_hidden_bias: float32 [3072], replicated
- grad_return_bias: float32 [768], replicated
- grad_feed_scale: float32 [768], replicated
- grad_position_table: float32 [2, 127, 12], replicated
The draws below stay inside these ranges and needn't reach their ends.
Inputs may be any that keep to these rules, and one draw needn't show every extreme that they name: `image_sizes`: row i holds image i's height and width in patches. The width is at least 7, height times width is at most 448, and some image has exactly 448 patches.
All inputs are finite; a program needn't handle non-finite values.
Results may differ from the reference program's by a relative error of at most 0.011.
Values may be sent and summed in bfloat16 or wider, within the bound.
A program may use at most 192 MiB of HBM per device.

```python
import math
import jax
import jax.numpy as jnp
from jax import lax

D = 768
HEADS = 12
HEAD = 64
FF = 3072
GRID = 64
TOK_DEV = 448
IMAGES = 32
TOKENS = 14336


def draw_image_sizes(key, part):
    key = jax.random.fold_in(key, 11)
    first_key, second_key, third_key = jax.random.split(key, 3)
    widths = jax.random.randint(first_key, (IMAGES,), TOK_DEV // GRID, GRID + 1)
    tallest = TOK_DEV // widths
    halvings = jax.random.randint(second_key, (IMAGES,), 0, 6)
    heights = jnp.maximum(tallest // 2 ** halvings, 1)
    chosen = jax.random.randint(third_key, (), 0, IMAGES)
    places = jnp.arange(IMAGES, dtype=jnp.int32)
    widths = jnp.where(places == chosen, GRID, widths)
    heights = jnp.where(places == chosen, TOK_DEV // GRID, heights)
    return jnp.stack([heights, widths], axis=1).astype(jnp.int32)


def level_of(own_key, shape, shards, low, largest):
    level, own = 1.0, jax.random.fold_in(own_key, 6)
    for position, parts in shards:
        steps = jnp.exp(jax.random.uniform(jax.random.fold_in(own, position), (parts,), jnp.float32, low / len(shards), largest / len(shards)))
        level = level * jnp.repeat(steps, shape[position] // parts).reshape([-1 if axis == position else 1 for axis in range(len(shape))])
    return level


def scatter_about(key, shape, deviation, limit, cuts=(), kind=jnp.bfloat16):
    level = level_of(key, shape, cuts, -0.22, 0.18) if cuts else 1.0
    entries = jax.random.normal(key, shape, jnp.float32) * deviation * level
    return jnp.minimum(jnp.maximum(entries, -limit), limit).astype(kind)


def setup_inputs(seed: int = 0) -> dict:
    seeds = jax.random.split(jax.random.key(seed), 19)
    tokens = scatter_about(seeds[0], (TOKENS, D), 1.0, 6.0, ((0, 32),))
    project_in = scatter_about(seeds[1], (D, 3 * D), D ** -0.5, 0.21875, ((0, 16),))
    project_out = scatter_about(seeds[2], (D, D), (D // 16) ** -0.5, 0.875, ((0, 16),))
    expand_weight = scatter_about(seeds[3], (D, FF), D ** -0.5, 0.21875, ((0, 16),))
    reduce_weight = scatter_about(seeds[4], (FF, D), FF ** -0.5, 0.109375, ((0, 16),))
    first_gain = jnp.clip(jax.random.uniform(seeds[5], (D,), jnp.float32, 0.5, 1.5), 0.5, 1.5)
    first_shift = scatter_about(seeds[6], (D,), 0.5, 3.0, (), jnp.float32)
    query_value_bias = scatter_about(seeds[7], (2, D), 0.5, 3.0, (), jnp.float32)
    output_bias = scatter_about(seeds[8], (D,), 0.5, 3.0, (), jnp.float32)
    mixer_scale = jnp.clip(jnp.exp(jax.random.uniform(seeds[9], (D,), jnp.float32, math.log(0.3), math.log(1.5))), 0.3, 1.5)
    second_gain = jnp.clip(jax.random.uniform(seeds[10], (D,), jnp.float32, 0.5, 1.5), 0.5, 1.5)
    second_shift = scatter_about(seeds[11], (D,), 0.5, 3.0, (), jnp.float32)
    hidden_bias = scatter_about(seeds[12], (FF,), 0.5, 3.0, (), jnp.float32)
    return_bias = scatter_about(seeds[13], (D,), 0.5, 3.0, (), jnp.float32)
    feed_scale = jnp.clip(jnp.exp(jax.random.uniform(seeds[14], (D,), jnp.float32, math.log(0.3), math.log(1.5))), 0.3, 1.5)
    position_table = scatter_about(seeds[15], (2, 2 * GRID - 1, HEADS), 0.6, 3.0, (), jnp.float32)
    image_sizes = draw_image_sizes(jax.random.fold_in(seeds[18], 71), 0)
    cotangent = scatter_about(seeds[17], (TOKENS, D), 1.0, 6.0, ((0, 32),))
    return dict(tokens=tokens, project_in=project_in, project_out=project_out, expand_weight=expand_weight, reduce_weight=reduce_weight, first_gain=first_gain, first_shift=first_shift, query_value_bias=query_value_bias, output_bias=output_bias, mixer_scale=mixer_scale, second_gain=second_gain, second_shift=second_shift, hidden_bias=hidden_bias, return_bias=return_bias, feed_scale=feed_scale, position_table=position_table, image_sizes=image_sizes, cotangent=cotangent)


EPS = 1e-06
MASKED = -1000000000.0

@jax.custom_vjp
def low(v):
    return lax.optimization_barrier(v.astype(jnp.bfloat16)).astype(jnp.float32)

@jax.custom_vjp
def low_back(v):
    return v

def low_keep(v):
    return (low(v), None)

def low_pass(kept, grad):
    return (grad,)

def back_keep(v):
    return (v, None)

def back_low(kept, grad):
    return (low(grad),)
low.defvjp(low_keep, low_pass)
low_back.defvjp(back_keep, back_low)

def layer_norm(values, gain, shift):
    centre = values - lax.optimization_barrier(jnp.mean(values, axis=-1, keepdims=True))
    spread = lax.optimization_barrier(jnp.mean(centre * centre, axis=-1, keepdims=True))
    return centre * lax.rsqrt(spread + EPS) * gain + shift

def matmul(left, right):
    return jnp.dot(left, right, precision=lax.Precision.HIGHEST)

def attend(queries, keys, values, tables, extent):
    places = jnp.arange(TOK_DEV, dtype=jnp.int32)
    height = extent[0]
    width_image = extent[1]
    row_of = places // width_image
    col_of = places % width_image
    usable = places < height * width_image
    row_index = (row_of[:, None] - row_of[None, :] + GRID - 1).astype(jnp.int32)
    col_index = (col_of[:, None] - col_of[None, :] + GRID - 1).astype(jnp.int32)
    offset_bias = tables[0][row_index] + tables[1][col_index]
    scores = jnp.einsum('qhd,khd->hqk', queries, keys, precision=lax.Precision.HIGHEST)
    scores = low_back(scores + jnp.transpose(offset_bias, (2, 0, 1)))
    scores = jnp.where(usable[None, None, :], scores, MASKED)
    chances = jax.nn.softmax(scores, axis=-1)
    blended = jnp.einsum('hqk,khd->qhd', low(chances), values, precision=lax.Precision.HIGHEST)
    return blended.reshape(TOK_DEV, D)

def forward(tokens, project_in, project_out, expand_weight, reduce_weight, first_gain, first_shift, query_value_bias, output_bias, mixer_scale, second_gain, second_shift, hidden_bias, return_bias, feed_scale, position_table, image_sizes):
    tables = low(position_table)

    def one_image(packed):
        inputs, extent = packed
        normed_a = low(layer_norm(inputs, first_gain, first_shift))
        projected = matmul(normed_a, project_in)
        queries = low_back(low((projected[:, :D] + query_value_bias[0]) * HEAD ** (-0.5)))
        keys = low_back(low(projected[:, D:2 * D]))
        values = low_back(low(projected[:, 2 * D:] + query_value_bias[1]))
        blended = attend(queries.reshape(TOK_DEV, HEADS, HEAD), keys.reshape(TOK_DEV, HEADS, HEAD), values.reshape(TOK_DEV, HEADS, HEAD), tables, extent)
        blended = low_back(low(blended))
        branch = low_back(matmul(blended, project_out) + output_bias)
        middle = inputs + mixer_scale * branch
        normed_b = low(layer_norm(middle, second_gain, second_shift))
        preact = low_back(matmul(normed_b, expand_weight) + hidden_bias)
        activated = low(jax.nn.gelu(preact, approximate=False))
        returned = low_back(matmul(activated, reduce_weight) + return_bias)
        return middle + feed_scale * returned
    images = tokens.reshape(IMAGES, TOK_DEV, D)
    result = lax.map(jax.checkpoint(one_image), (images, image_sizes))
    return result.reshape(IMAGES * TOK_DEV, D)

def reference(tokens, project_in, project_out, expand_weight, reduce_weight, first_gain, first_shift, query_value_bias, output_bias, mixer_scale, second_gain, second_shift, hidden_bias, return_bias, feed_scale, position_table, image_sizes, cotangent):
    floats = [member.astype(jnp.float32) for member in (tokens, project_in, project_out, expand_weight, reduce_weight, first_gain, first_shift, query_value_bias, output_bias, mixer_scale, second_gain, second_shift, hidden_bias, return_bias, feed_scale, position_table)]

    def wrapped(*params):
        return forward(*params, image_sizes)
    outputs, pullback = jax.vjp(wrapped, *floats)
    gradients = pullback(cotangent.astype(jnp.float32))
    return (outputs.astype(jnp.bfloat16), gradients[0], gradients[1], gradients[2], gradients[3], gradients[4], gradients[5], gradients[6], gradients[7], gradients[8], gradients[9], gradients[10], gradients[11], gradients[12], gradients[13], gradients[14], gradients[15])
```

```python
import jax
import jax.numpy as jnp
from jax import lax
from jax.experimental import pallas as pl
from jax.experimental.pallas import tpu as pltpu
from jax.sharding import PartitionSpec as P

HEADS = 12
HEAD = 64
GRID = 64


EPS = 1e-06
MASKED = -1000000000.0


def layer_norm(values, gain, shift):
    centre = values - jnp.mean(values, axis=-1, keepdims=True)
    spread = jnp.mean(centre * centre, axis=-1, keepdims=True)
    return centre * lax.rsqrt(spread + EPS) * gain + shift


def gelu_exact(values):
    return jax.nn.gelu(values, approximate=False)


def shift_onehot(side):
    first_axis = lax.broadcasted_iota(jnp.int32, (side, side, 2 * side - 1), 0)
    second_axis = lax.broadcasted_iota(jnp.int32, (side, side, 2 * side - 1), 1)
    third_axis = lax.broadcasted_iota(jnp.int32, (side, side, 2 * side - 1), 2)
    return (first_axis - second_axis + side - 1 == third_axis).astype(jnp.float32)


def position_bias(shift_part, picks):
    between = jnp.einsum("tijh,tkj->tihk", shift_part, picks, preferred_element_type=jnp.float32)
    return jnp.einsum(
        "tqi,tihk->hqk", picks, between.astype(jnp.bfloat16), preferred_element_type=jnp.float32
    )


def group_scores(query_part, key_part, shift_part, picks, usable):
    scores = jnp.einsum("qhd,khd->hqk", query_part, key_part, preferred_element_type=jnp.float32)
    scores = scores + position_bias(shift_part, picks)
    return jnp.where(usable[None, None, :], scores, MASKED)


def attend_group(packed, picks, usable):
    query_part, key_part, value_part, shift_part = packed
    scores = group_scores(query_part, key_part, shift_part, picks, usable)
    highest = jnp.max(scores, axis=-1, keepdims=True)
    weights_raw = jnp.exp(scores - highest)
    totals = jnp.sum(weights_raw, axis=-1, keepdims=True)
    chances = (weights_raw / totals).astype(jnp.bfloat16)
    blended = jnp.einsum("hqk,khd->qhd", chances, value_part, preferred_element_type=jnp.float32)
    return (blended.astype(jnp.bfloat16), (highest + jnp.log(totals))[..., 0])


def attend_back(packed, picks, usable):
    query_part, key_part, value_part, grad_part, logsums, shift_part = packed
    scores = group_scores(query_part, key_part, shift_part, picks, usable)
    chances = jnp.exp(scores - logsums[..., None])
    grad_chance = jnp.einsum(
        "qhd,khd->hqk", grad_part, value_part, preferred_element_type=jnp.float32
    )
    row_dot = jnp.sum(chances * grad_chance, axis=-1, keepdims=True)
    grad_scores = (chances * (grad_chance - row_dot)).astype(jnp.bfloat16)
    grad_query = jnp.einsum(
        "hqk,khd->qhd", grad_scores, key_part, preferred_element_type=jnp.float32
    )
    grad_key = jnp.einsum(
        "hqk,qhd->khd", grad_scores, query_part, preferred_element_type=jnp.float32
    )
    grad_value = jnp.einsum(
        "hqk,qhd->khd", chances.astype(jnp.bfloat16), grad_part, preferred_element_type=jnp.float32
    )
    across = jnp.einsum("hqk,tkj->thqj", grad_scores, picks, preferred_element_type=jnp.float32)
    grad_shift = jnp.einsum(
        "tqi,thqj->tijh", picks.astype(jnp.float32), across, precision=lax.Precision.HIGHEST
    )
    return (
        grad_query.astype(jnp.bfloat16),
        grad_key.astype(jnp.bfloat16),
        grad_value.astype(jnp.bfloat16),
        grad_shift,
    )


def shards(
    tokens,
    project_in,
    project_out,
    expand_weight,
    reduce_weight,
    first_gain,
    first_shift,
    query_value_bias,
    output_bias,
    mixer_scale,
    second_gain,
    second_shift,
    hidden_bias,
    return_bias,
    feed_scale,
    position_table,
    image_sizes,
    cotangent,
):
    length = tokens.shape[0]
    width_model = tokens.shape[1]
    head_count = HEADS
    per_group = 4
    groups = head_count // per_group
    full_in, full_out, full_expand, full_reduce = (
        lax.all_gather(project_in, "dp", axis=0, tiled=True),
        lax.all_gather(project_out, "dp", axis=0, tiled=True),
        lax.all_gather(expand_weight, "dp", axis=0, tiled=True),
        lax.all_gather(reduce_weight, "dp", axis=0, tiled=True),
    )
    inputs = tokens.astype(jnp.float32)
    normed_a, first_back = jax.vjp(layer_norm, inputs, first_gain, first_shift)
    normed_a_low = normed_a.astype(jnp.bfloat16)
    projected = jnp.dot(normed_a_low, full_in, preferred_element_type=jnp.float32)
    queries = ((projected[:, :width_model] + query_value_bias[0]) * HEAD ** (-0.5)).astype(
        jnp.bfloat16
    )
    keys_low = projected[:, width_model : 2 * width_model].astype(jnp.bfloat16)
    values_low = (projected[:, 2 * width_model :] + query_value_bias[1]).astype(jnp.bfloat16)
    shift_table = shift_onehot(GRID)
    shifts = jnp.einsum(
        "ija,tah->tijh",
        shift_table.astype(jnp.bfloat16),
        position_table.astype(jnp.bfloat16),
        preferred_element_type=jnp.float32,
    ).astype(jnp.bfloat16)
    shifts_grouped = shifts.reshape(2, GRID, GRID, groups, per_group).transpose(3, 0, 1, 2, 4)
    places = jnp.arange(length, dtype=jnp.int32)
    height = image_sizes[0, 0]
    width_image = image_sizes[0, 1]
    grid_iota = jnp.arange(GRID, dtype=jnp.int32)
    picks = jnp.stack(
        [
            (places // width_image)[:, None] == grid_iota[None, :],
            (places % width_image)[:, None] == grid_iota[None, :],
        ]
    ).astype(jnp.bfloat16)
    usable = places < height * width_image

    def split_heads(matrix):
        return matrix.reshape(length, groups, per_group, HEAD).transpose(1, 0, 2, 3)

    def join_heads(blocks):
        return blocks.transpose(1, 0, 2, 3).reshape(length, width_model)

    query_groups = split_heads(queries)
    key_groups = split_heads(keys_low)
    value_groups = split_heads(values_low)
    blended_groups, logsums = lax.map(
        lambda packed: attend_group(packed, picks, usable),
        (query_groups, key_groups, value_groups, shifts_grouped),
    )
    blended = join_heads(blended_groups)
    branch = jnp.dot(blended, full_out, preferred_element_type=jnp.float32) + output_bias
    middle = inputs + mixer_scale * branch
    normed_b, second_back = jax.vjp(layer_norm, middle, second_gain, second_shift)
    normed_b_low = normed_b.astype(jnp.bfloat16)
    preact = jnp.dot(normed_b_low, full_expand, preferred_element_type=jnp.float32) + hidden_bias
    activated, gelu_back = jax.vjp(gelu_exact, preact)
    activated_low = activated.astype(jnp.bfloat16)
    returned = jnp.dot(activated_low, full_reduce, preferred_element_type=jnp.float32) + return_bias
    outputs = middle + feed_scale * returned
    back_in, back_out, back_expand, back_reduce = (
        lax.all_gather(project_in, "dp", axis=0, tiled=True),
        lax.all_gather(project_out, "dp", axis=0, tiled=True),
        lax.all_gather(expand_weight, "dp", axis=0, tiled=True),
        lax.all_gather(reduce_weight, "dp", axis=0, tiled=True),
    )
    upstream = cotangent.astype(jnp.float32)
    grad_feed_scale = jnp.sum(upstream * returned, axis=0)
    grad_returned = (upstream * feed_scale).astype(jnp.bfloat16)
    grad_return_bias = jnp.sum(grad_returned.astype(jnp.float32), axis=0)
    grad_reduce = jnp.einsum(
        "tf,td->fd", activated_low, grad_returned, preferred_element_type=jnp.float32
    )
    grad_activated = jnp.einsum(
        "td,fd->tf", grad_returned, back_reduce, preferred_element_type=jnp.float32
    )
    grad_preact = gelu_back(grad_activated)[0].astype(jnp.bfloat16)
    grad_hidden_bias = jnp.sum(grad_preact.astype(jnp.float32), axis=0)
    grad_expand = jnp.einsum(
        "td,tf->df", normed_b_low, grad_preact, preferred_element_type=jnp.float32
    )
    grad_normed_b = jnp.einsum(
        "tf,df->td", grad_preact, back_expand, preferred_element_type=jnp.float32
    )
    grad_from_norm, grad_second_gain, grad_second_shift = second_back(grad_normed_b)
    grad_middle = upstream + grad_from_norm
    grad_mixer_scale = jnp.sum(grad_middle * branch, axis=0)
    grad_branch = (grad_middle * mixer_scale).astype(jnp.bfloat16)
    grad_output_bias = jnp.sum(grad_branch.astype(jnp.float32), axis=0)
    grad_project_out = jnp.einsum(
        "td,te->de", blended, grad_branch, preferred_element_type=jnp.float32
    )
    grad_blended = jnp.einsum(
        "te,de->td", grad_branch, back_out, preferred_element_type=jnp.float32
    ).astype(jnp.bfloat16)
    grad_query_groups, grad_key_groups, grad_value_groups, grad_shift_groups = lax.map(
        lambda packed: attend_back(packed, picks, usable),
        (
            query_groups,
            key_groups,
            value_groups,
            split_heads(grad_blended),
            logsums,
            shifts_grouped,
        ),
    )
    grad_queries = join_heads(grad_query_groups) * HEAD ** (-0.5)
    grad_keys = join_heads(grad_key_groups)
    grad_values = join_heads(grad_value_groups)
    grad_projected = jnp.concatenate([grad_queries, grad_keys, grad_values], axis=1)
    grad_query_value_bias = jnp.stack(
        [
            jnp.sum(grad_queries.astype(jnp.float32), axis=0),
            jnp.sum(grad_values.astype(jnp.float32), axis=0),
        ]
    )
    grad_project_in = jnp.einsum(
        "td,te->de", normed_a_low, grad_projected, preferred_element_type=jnp.float32
    )
    grad_normed_a = jnp.einsum(
        "te,de->td", grad_projected, back_in, preferred_element_type=jnp.float32
    )
    grad_from_first, grad_first_gain, grad_first_shift = first_back(grad_normed_a)
    input_grad = grad_middle + grad_from_first
    grad_shift = grad_shift_groups.transpose(1, 2, 3, 0, 4).reshape(2, GRID, GRID, head_count)
    grad_position_table = jnp.einsum(
        "ija,tijh->tah", shift_table, grad_shift, precision=lax.Precision.HIGHEST
    )
    weight_grads = (
        lax.psum_scatter(grad_project_in, "dp", scatter_dimension=0, tiled=True),
        lax.psum_scatter(grad_project_out, "dp", scatter_dimension=0, tiled=True),
        lax.psum_scatter(grad_expand, "dp", scatter_dimension=0, tiled=True),
        lax.psum_scatter(grad_reduce, "dp", scatter_dimension=0, tiled=True),
    )
    weight_grads = lax.psum(
        (weight_grads[0], weight_grads[1], weight_grads[2], weight_grads[3]), "rep"
    )
    small_sums = lax.psum(
        (
            grad_first_gain,
            grad_first_shift,
            grad_query_value_bias,
            grad_output_bias,
            grad_mixer_scale,
            grad_second_gain,
            grad_second_shift,
            grad_hidden_bias,
            grad_return_bias,
            grad_feed_scale,
            grad_position_table,
        ),
        ("dp", "rep"),
    )
    return (
        outputs.astype(jnp.bfloat16),
        input_grad,
        weight_grads[0],
        weight_grads[1],
        weight_grads[2],
        weight_grads[3],
        small_sums[0],
        small_sums[1],
        small_sums[2],
        small_sums[3],
        small_sums[4],
        small_sums[5],
        small_sums[6],
        small_sums[7],
        small_sums[8],
        small_sums[9],
        small_sums[10],
    )


FEATURES = 768
HIDDEN = 3072
SLOTS = 448
MESH = pl.DeviceIdType.MESH
LOW = jnp.bfloat16
FULL = jnp.float32

W_IN = (48, 2304, False, "A")
W_OUT = (48, 768, False, "A")
W_EXPAND = (48, 3072, False, "A")
W_REDUCE = (192, 768, True, "B")
WEIGHTS = (W_IN, W_OUT, W_EXPAND, W_REDUCE)

CHUNK = 384
CHUNKS = (
    (3, 0, "B"), (3, 1, "A"),
    (2, 0, "A"), (2, 1, "B"), (2, 2, "A"), (2, 3, "A"),
    (1, 0, "B"),
    (0, 0, "A"), (0, 1, "B"), (0, 2, "A"),
)


def aligned(index, step):
    return pl.multiple_of(index, step)


class Net:
    def __init__(self):
        dp, c = lax.axis_index("dp"), lax.axis_index("rep")
        z, y, x = dp // 4, lax.rem(dp // 2, 2), lax.rem(dp, 2)
        self.dp, self.c, self.z, self.y, self.x = dp, c, z, y, x
        self.ma = y * (1 - c) + x * c
        self.mb = x * (1 - c) + y * c
        self.wa, self.wb = 2 - c, 1 + c
        self.to_a = (dp + self.wa * (1 - 2 * self.ma), c)
        self.to_b = (dp + self.wb * (1 - 2 * self.mb), c)
        self.to_z = (lax.rem(dp + 4, 16), c)
        self.from_z = (lax.rem(dp + 12, 16), c)
        self.far_z = (lax.rem(dp + 8, 16), c)
        self.sib = (dp, 1 - c)

    def barrier(self):
        sem = pltpu.get_barrier_semaphore()
        for target in (self.to_a, self.to_b, self.to_z, self.from_z, self.far_z, self.sib):
            pl.semaphore_signal(sem, inc=1, device_id=target, device_id_type=MESH)
        pl.semaphore_wait(sem, 6)

    def back(self, steps):
        return lax.rem(self.z + 4 - steps, 4)

    def owner(self, z, a, b):
        return 4 * z + self.wa * a + self.wb * b


class Transfers:
    def __init__(self, net, send, recv):
        self.net, self.send, self.recv, self.sent = net, send, recv, []

    def push(self, src, dst, slot, to):
        copy = pltpu.make_async_remote_copy(
            src, dst, self.send.at[len(self.sent)], self.recv.at[slot], device_id=to, device_id_type=MESH
        )
        copy.start()
        self.sent.append(copy)

    def landed(self, dst, slot):
        pltpu.make_async_remote_copy(
            dst, dst, self.send.at[0], self.recv.at[slot], device_id=self.net.sib, device_id_type=MESH
        ).wait_recv()

    def finish(self):
        for copy in self.sent:
            copy.wait_send()


class Gather(Transfers):
    def __init__(self, net, spec, buf, send, recv, name):
        super().__init__(net, send, recv)
        self.buf, self.name = buf, name
        self.rows, self.cols, self.by_rows, self.order = spec

    def load(self, src, sem):
        c = self.net.c
        if self.by_rows:
            part = src.at[pl.ds(aligned(c * (self.rows // 2), 16), self.rows // 2), :]
        else:
            part = src.at[:, pl.ds(aligned(c * (self.cols // 2), 128), self.cols // 2)]
        self.copy = pltpu.make_async_copy(part, self.block(self.net.dp), sem)
        self.copy.start()

    def block(self, owner):
        c = self.net.c
        if self.by_rows:
            half = self.rows // 2
            return self.buf.at[pl.ds(aligned(owner * self.rows + c * half, 16), half), :]
        half = self.cols // 2
        return self.buf.at[pl.ds(aligned(owner * self.rows, 16), self.rows), pl.ds(aligned(c * half, 128), half)]

    def group(self, z, c):
        if self.by_rows:
            return self.buf.reshape(4, 4, 2, self.rows // 2, self.cols).at[z, :, c]
        half, rows = self.cols // 2, 4 * self.rows
        return self.buf.at[pl.ds(aligned(z * rows, 16), rows), pl.ds(aligned(c * half, 128), half)]

    def events(self):
        net = self.net
        ma, mb = net.ma, net.mb

        def near(back, other):
            return self.block(net.owner(net.back(back), ma, mb + other * (1 - 2 * mb)))

        def far(back, other):
            return self.block(net.owner(net.back(back), 1 - ma, mb + other * (1 - 2 * mb)))

        def own():
            self.copy.wait()
            ref = near(0, 0)
            self.push(ref, ref, 2, net.to_z)
            self.push(ref, ref, 1, net.to_b)
            self.push(ref, ref, 8, net.to_a)

        def relay(back, other):
            def run():
                ref = near(back, other)
                self.landed(ref, back * 2 + other)
                if back < 3 and (other == 0 or self.order == "A"):
                    self.push(ref, ref, (back + 1) * 2 + other, net.to_z)
                if self.order == "B" and other == 0:
                    self.push(ref, ref, back * 2 + 1, net.to_b)
                self.push(ref, ref, 8 + back * 2 + other, net.to_a)

            return run

        def tail(back):
            def run():
                for other in (0, 1):
                    self.landed(far(back, other), 8 + back * 2 + other)
                ref = self.group(net.back(back), net.c)
                self.push(ref, ref, 16 + back, net.sib)

            return run

        def complete():
            for back in range(4):
                self.landed(self.group(net.back(back), 1 - net.c), 16 + back)

        events = [(self.name + "own", own), (self.name, relay(0, 1))]
        for back in (1, 2, 3):
            events += [(self.name, relay(back, 0)), (self.name, relay(back, 1))]
        events += [(self.name, tail(back)) for back in range(4)]
        events.append((self.name + "all", complete))
        return events


class Scatter(Transfers):
    def __init__(self, net, weight, column, order, refs, stage, send, recv, name):
        super().__init__(net, send, recv)
        self.order, self.name = order, name
        self.rows, self.cols, self.by_rows, _ = WEIGHTS[weight]
        self.g, self.ra, self.rb, self.rz = refs
        self.stage, self.column = stage, column
        self.rh = self.rows // 2 if self.by_rows else self.rows

    def produced(self, back):
        net = self.net
        self.push(self.g.at[net.back(back), 1 - net.ma], self.ra.at[back], back, net.to_a)

    def add_into(self, dst, terms, pair):
        def body(i, carry):
            rows = pl.ds(aligned(i * 16, 16), 16)
            for index in ((0, rows), (1, rows)) if pair else ((rows,),):
                total = dst[(*index, slice(None))].astype(FULL)
                for term in terms:
                    total += term[(*index, slice(None))].astype(FULL)
                dst[(*index, slice(None))] = total.astype(LOW)
            return carry

        lax.fori_loop(0, self.rh // 16, body, 0)

    def part_of_stage(self, c):
        if self.by_rows:
            return self.stage.at[pl.ds(aligned(c * self.rh, 16), self.rh), pl.ds(self.column * CHUNK, CHUNK)]
        return self.stage.at[:, pl.ds(aligned(c * (self.cols // 2) + self.column * CHUNK, 128), CHUNK)]

    def last(self, terms):
        mine = self.part_of_stage(self.net.c)

        def body(i, carry):
            rows = pl.ds(aligned(i * 16, 16), 16)
            total = terms[0][rows, :].astype(FULL)
            for term in terms[1:]:
                total += term[rows, :].astype(FULL)
            mine[rows, :] = total
            return carry

        lax.fori_loop(0, self.rh // 16, body, 0)
        self.push(mine, mine, 11, self.net.sib)

    def got(self):
        self.landed(self.part_of_stage(1 - self.net.c), 11)

    def events(self):
        net, g, ra, rb, rz = self.net, self.g, self.ra, self.rb, self.rz
        ma, mb = net.ma, net.mb

        def step_a(s):
            def run():
                back = (s + 1) % 4
                self.landed(ra.at[back], back)
                terms = [ra.at[back]]
                if s > 0:
                    self.landed(rz.at[s - 1], 8 + s - 1)
                    terms.append(rz.at[s - 1])
                dst = g.at[net.back(back), ma]
                self.add_into(dst, terms, True)
                if s < 3:
                    self.push(dst, rz.at[s], 8 + s, net.to_z)
                else:
                    self.push(dst.at[1 - mb], rb.at[0], 4, net.to_b)

            return run

        def final_a():
            self.landed(rb.at[0], 4)
            self.last([g.at[net.z, ma, mb], rb.at[0]])

        def first_b(back):
            def run():
                self.landed(ra.at[back], back)
                dst = g.at[net.back(back), ma]
                self.add_into(dst, [ra.at[back]], True)
                self.push(dst.at[1 - mb], rb.at[back], 4 + back, net.to_b)

            return run

        def step_b(s):
            def run():
                back = (s + 1) % 4
                self.landed(rb.at[back], 4 + back)
                terms = [rb.at[back]]
                if s > 0:
                    self.landed(rz.at[s - 1], 8 + s - 1)
                    terms.append(rz.at[s - 1])
                dst = g.at[net.back(back), ma, mb]
                if s < 3:
                    self.add_into(dst, terms, False)
                    self.push(dst, rz.at[s], 8 + s, net.to_z)
                else:
                    self.last([dst] + terms)

            return run

        if self.order == "A":
            steps = [step_a(s) for s in range(4)] + [final_a]
        else:
            steps = [first_b(back) for back in (1, 2, 3, 0)] + [step_b(s) for s in range(4)]
        return [(self.name, step) for step in steps] + [(self.name + "all", self.got)]

    @staticmethod
    def shapes(weight, order):
        rows, _, by_rows, _ = WEIGHTS[weight]
        block = (rows // 2 if by_rows else rows, CHUNK)
        relay = (3, 2) if order == "A" else (3,)
        return [
            pltpu.VMEM((4, 2, 2) + block, LOW),
            pltpu.VMEM((4, 2) + block, LOW),
            pltpu.VMEM((1 if order == "A" else 4,) + block, LOW),
            pltpu.VMEM(relay + block, LOW),
        ]


class SmallSum(Transfers):
    def __init__(self, net, buf, landing, send, recv):
        super().__init__(net, send, recv)
        self.buf, self.landing = buf, landing
        place, z = lax.rem(net.dp, 4), net.z
        near_z = z + 1 - 2 * lax.rem(z, 2)
        self.partners = [
            net.sib,
            (net.dp + 1 - 2 * net.x, net.c),
            (net.dp + 2 - 4 * net.y, net.c),
            (near_z * 4 + place, net.c),
            net.far_z,
        ]

    def events(self):
        def start(i):
            def run():
                self.push(self.buf.at[i], self.landing.at[i], i, self.partners[i])

            return run

        def add(i):
            def run():
                self.landed(self.landing.at[i], i)
                self.buf[i + 1] = self.buf[i] + self.landing[i]
                if i < 4:
                    start(i + 1)()

            return run

        return [("small", start(0))] + [("small", add(i)) for i in range(5)]


def dot(left, right):
    return jnp.dot(left, right, preferred_element_type=FULL)


def dot_rows(left, right):
    return lax.dot_general(left, right, (((1,), (1,)), ((), ())), preferred_element_type=FULL)


def fold(values):
    return jnp.sum(values.reshape(values.shape[0] // 8, 8, values.shape[1]), axis=0)


def normalised(values):
    centre = values - jnp.mean(values, axis=-1, keepdims=True)
    inverse = lax.rsqrt(jnp.mean(centre * centre, axis=-1, keepdims=True) + EPS)
    return centre * inverse, inverse


BLOCK = 64
ROOT_HALF = 0.7071067811865476
DENSITY = 0.3989422804014327


def layer_kernel(
    sizes, tokens_hbm, w_in_hbm, w_out_hbm, w_expand_hbm, w_reduce_hbm, cotangent_hbm,
    first_gain, first_shift, query_value_bias, output_bias, mixer_scale, second_gain, second_shift,
    hidden_bias, return_bias, feed_scale, table,
    outputs_hbm, input_grad_hbm, g_in_hbm, g_out_hbm, g_expand_hbm, g_reduce_hbm, small_out,
    w_in, w_out, w_expand, w_reduce,
    stage_in, stage_out, stage_expand, stage_reduce,
    tok, cot, normed, normed_a_t, normed_b_t, blended_t, qkv, place_q, place_k, place_t,
    chances, mixed, branch, middle, act, act_t, act_t_far, slope, g_ret, g_ret_far, g_pre_far,
    g_branch_far, g_qkv_far, work, small, small_landing,
    load_sem, out_sem, gather_send, gather_recv, scatter_send, scatter_recv, swap_send, swap_recv,
    small_send, small_recv, *scatter_refs,
):
    net = Net()
    g_branch = normed
    c = net.c
    sibling = 1 - c

    weights = [w_in, w_out, w_expand, w_reduce]
    gathers = []
    for i, source in enumerate((w_in_hbm, w_out_hbm, w_expand_hbm, w_reduce_hbm)):
        gather = Gather(net, WEIGHTS[i], weights[i], gather_send.at[i], gather_recv.at[i], "g%d" % i)
        gather.load(source, load_sem.at[i])
        gathers.append(gather)
    load_tok = pltpu.make_async_copy(tokens_hbm, tok, load_sem.at[4])
    load_cot = pltpu.make_async_copy(cotangent_hbm, cot, load_sem.at[5])
    load_tok.start()
    load_cot.start()
    net.barrier()

    stages = [stage_in, stage_out, stage_expand, stage_reduce]
    scatters = []
    for i, (weight, column, order) in enumerate(CHUNKS):
        scatters.append(
            Scatter(net, weight, column, order, scatter_refs[4 * i : 4 * i + 4], stages[weight],
                    scatter_send.at[i], scatter_recv.at[i], "s%d" % i)
        )
    swaps = Transfers(net, swap_send, swap_recv)
    sums = SmallSum(net, small, small_landing, small_send, small_recv)
    queue = []

    def pump(count):
        for _ in range(min(count, len(queue))):
            queue.pop(0)[1]()

    def pump_to(name):
        while any(entry[0] == name for entry in queue):
            queue.pop(0)[1]()

    def weave(lists, lag):
        lists = [list(entries) for entries in lists]
        step = 0
        while any(lists):
            for i, entries in enumerate(lists):
                if entries and step >= i * lag:
                    queue.append(entries.pop(0))
            step += 1

    weave([gather.events() for gather in gathers], GATHER_LAG)
    pump_to("g3own")

    load_tok.wait()
    load_cot.wait()

    def first_rows(i, carry):
        rows = pl.ds(aligned(i * BLOCK, BLOCK), BLOCK)
        unit, _ = normalised(tok[rows, :].astype(FULL))
        normed[rows, :] = (unit * first_gain[...] + first_shift[...]).astype(LOW)
        returned_grad = (cot[rows, :].astype(FULL) * feed_scale[...]).astype(LOW)
        g_ret[rows, :] = returned_grad
        return carry + fold(returned_grad.astype(FULL))

    total = lax.fori_loop(0, SLOTS // BLOCK, first_rows, jnp.zeros((8, FEATURES), FULL))
    small[0] = jnp.zeros_like(small[0])
    small[0, 12:13, :] = jnp.sum(total, axis=0, keepdims=True)
    swaps.push(g_ret, g_ret_far, 0, net.sib)
    pump(2)

    def turn(source, target):
        for j in range(FEATURES // 128):
            target[0, j * 128 : (j + 1) * 128, :] = source[:, j * 128 : (j + 1) * 128].T

    turn(normed, normed_a_t)
    swaps.push(normed_a_t.at[0], normed_a_t.at[1], 1, net.sib)
    pump(2)

    height, width = sizes[0, 0], sizes[0, 1]
    width_f = width.astype(FULL)
    live = (height * width).astype(FULL)

    def grid_place(slot):
        row = jnp.floor((slot + 0.5) / width_f)
        return row, slot - row * width_f

    slot = lax.broadcasted_iota(jnp.int32, (SLOTS, 128), 0).astype(FULL)
    lane = lax.broadcasted_iota(jnp.int32, (SLOTS, 128), 1).astype(FULL)
    row, col = grid_place(slot)
    hit = jnp.where(lane < GRID, row, col + GRID) == lane
    place_q[...] = jnp.where(hit, 1.0, 0.0).astype(LOW)
    place_k[...] = jnp.where(slot < live, jnp.where(hit, 1.0, 0.0), jnp.where(lane == GRID - 1, 1.0, 0.0)).astype(LOW)
    slot = lax.broadcasted_iota(jnp.int32, (128, SLOTS), 1).astype(FULL)
    lane = lax.broadcasted_iota(jnp.int32, (128, SLOTS), 0).astype(FULL)
    row, col = grid_place(slot)
    hit = jnp.where(lane < GRID, GRID - 1 - row, 2 * GRID - 1 - col) == lane
    place_t[...] = jnp.where(hit, 1.0, 0.0).astype(LOW)

    pump_to("g0all")
    for j in range(6):
        cols = slice(j * CHUNK, (j + 1) * CHUNK)
        part = dot(normed[...], w_in[:, cols])
        inner = slice((j % 2) * CHUNK, (j % 2 + 1) * CHUNK)
        if j < 2:
            part = (part + query_value_bias[0:1, inner]) * 0.125
        elif j >= 4:
            part = part + query_value_bias[1:2, inner]
        qkv[:, cols] = part.astype(LOW)
        pump(1)

    lane128 = lax.broadcasted_iota(jnp.int32, (128, 128), 1)
    row128 = lax.broadcasted_iota(jnp.int32, (128, 128), 0)
    half_lane = lax.broadcasted_iota(jnp.int32, (SLOTS, 128), 1)
    no_key = (lane128 == GRID - 1) & (row128 < GRID) & (jnp.full((128, 128), live) < SLOTS)
    spans = ((0, 256), (256, SLOTS))

    def only(values, e):
        keep = half_lane < 64 if e == 0 else half_lane >= 64
        return jnp.where(keep, values, jnp.zeros_like(values))

    def bias_table(head):
        rows_part = jnp.broadcast_to(table[head : head + 1, :], (GRID, 128))
        cols_part = jnp.broadcast_to(table[12 + head : 13 + head, :], (GRID, 128))
        both = jnp.concatenate(
            [
                pltpu.roll(rows_part, 65, 1, stride=1, stride_axis=0),
                pltpu.roll(cols_part, 1, 1, stride=1, stride_axis=0),
            ],
            axis=0,
        )
        both = jnp.where(lane128 // GRID == row128 // GRID, both, 0.0)
        return jnp.where(no_key, MASKED, both).astype(LOW)

    def attend(pair):
        cols = slice(pair * 128, (pair + 1) * 128)
        q_pair = qkv[:, cols]
        keys = jnp.concatenate([qkv[:, 768 + pair * 128 : 896 + pair * 128], place_k[...]], axis=1)
        v_turned = qkv[:, 1536 + pair * 128 : 1664 + pair * 128].T
        for e in (0, 1):
            head = 2 * pair + e
            bias = dot(place_q[...], bias_table(head)).astype(LOW)
            asks = jnp.concatenate([only(q_pair, e), bias], axis=1)
            v_head = v_turned[e * 64 : (e + 1) * 64, :]
            for lo, hi in spans:
                scores = dot_rows(keys, asks[lo:hi, :])
                raised = jnp.exp(scores - jnp.max(scores, axis=0, keepdims=True))
                share = (raised * (1.0 / jnp.sum(raised, axis=0, keepdims=True))).astype(LOW)
                chances[head, :, lo:hi] = share
                blended_t[0, head * 64 : (head + 1) * 64, lo:hi] = dot(v_head, share).astype(LOW)
        mixed[:, cols] = blended_t[0, cols, :].T

    for pair in range(6):
        attend(pair)
        pump(FORWARD_PUMP)
    swaps.push(blended_t.at[0], blended_t.at[1], 2, net.sib)

    pump_to("g1all")
    for j in range(2):
        cols = slice(j * CHUNK, (j + 1) * CHUNK)
        branch[:, cols] = dot(mixed[...], w_out[:, cols]) + output_bias[:, cols]
    pump(2)

    def middle_rows(i, carry):
        rows = pl.ds(aligned(i * BLOCK, BLOCK), BLOCK)
        mid = tok[rows, :].astype(FULL) + mixer_scale[...] * branch[rows, :]
        middle[rows, :] = mid
        unit, _ = normalised(mid)
        normed[rows, :] = (unit * second_gain[...] + second_shift[...]).astype(LOW)
        return carry

    lax.fori_loop(0, SLOTS // BLOCK, middle_rows, 0)
    turn(normed, normed_b_t)
    swaps.push(normed_b_t.at[0], normed_b_t.at[1], 3, net.sib)

    pump_to("g2all")
    for j in range(8):
        cols = slice(j * CHUNK, (j + 1) * CHUNK)
        pre = dot(normed[...], w_expand[:, cols]) + hidden_bias[:, cols]
        share = 0.5 + 0.5 * lax.erf(pre * ROOT_HALF)
        active = (pre * share).astype(LOW)
        act[:, cols] = active
        slope[:, cols] = (share + pre * (DENSITY * jnp.exp(-0.5 * pre * pre))).astype(LOW)
        for k in range(3):
            act_t[j * CHUNK + k * 128 : j * CHUNK + (k + 1) * 128, :] = active[:, k * 128 : (k + 1) * 128].T
        pump(1)
    act_blocks = act_t.reshape(16, 2, 96, SLOTS)
    swaps.push(act_blocks.at[:, sibling], act_t_far, 4, net.sib)

    def place_of(owner):
        oy, ox = owner // 2, owner % 2
        return oy * (1 - c) + ox * c, ox * (1 - c) + oy * c

    def weight_grad(index, left, left_far, right, right_far):
        scatter = scatters[index]
        for back in (1, 2, 3, 0):
            z = net.back(back)
            tile = dot(left(z), right) + dot(left_far(z), right_far)
            tile = tile.astype(LOW)
            for owner in range(4):
                pa, pb = place_of(owner)
                scatter.g[z, pa, pb] = tile[owner * scatter.rh : (owner + 1) * scatter.rh, :]
            scatter.produced(back)
        queue.extend(scatter.events())

    def rows_of(ref, slot):
        return lambda z: ref[slot, pl.ds(aligned(z * 192, 64), 192), :]

    swaps.landed(g_ret_far, 0)
    swaps.landed(act_t_far, 4)
    for j in range(2):
        cols = slice(j * CHUNK, (j + 1) * CHUNK)
        weight_grad(
            j,
            lambda z: act_blocks[pl.ds(4 * z, 4), c].reshape(384, SLOTS),
            lambda z: act_t_far[pl.ds(4 * z, 4)].reshape(384, SLOTS),
            g_ret[:, cols], g_ret_far[:, cols],
        )

    pump_to("g3all")
    for j in range(8):
        half = sibling if j < 4 else c
        cols = pl.ds(aligned(half * 1536 + (j % 4) * CHUNK, 128), CHUNK)
        rows = pl.ds(aligned(half * 1536 + (j % 4) * CHUNK, 128), CHUNK)
        part = (dot_rows(g_ret[...], w_reduce[rows, :]) * slope[:, cols].astype(FULL)).astype(LOW)
        slope[:, cols] = part
        summed = jnp.sum(part.astype(FULL), axis=0, keepdims=True)
        small[0, pl.ds(8 + 2 * half + (j % 4) // 2, 1), (j % 2) * CHUNK : (j % 2 + 1) * CHUNK] = summed
        if j == 3:
            swaps.push(slope.at[:, pl.ds(aligned(sibling * 1536, 128), 1536)], g_pre_far, 5, net.sib)
        pump(BACK_PUMP)
    swaps.landed(normed_b_t.at[1], 3)
    swaps.landed(g_pre_far, 5)
    for j in range(4):
        cols = slice(j * CHUNK, (j + 1) * CHUNK)
        weight_grad(
            2 + j, rows_of(normed_b_t, 0), rows_of(normed_b_t, 1),
            slope[:, pl.ds(aligned(c * 1536 + j * CHUNK, 128), CHUNK)], g_pre_far[:, cols],
        )
        pump(BACK_PUMP)

    for j in range(2):
        cols = slice(j * CHUNK, (j + 1) * CHUNK)
        work[:, cols] = dot_rows(slope[...], w_expand[cols, :])
        pump(BACK_PUMP)

    def second_back(i, carry):
        gain_sum, shift_sum, mixer_sum, bias_sum = carry
        rows = pl.ds(aligned(i * BLOCK, BLOCK), BLOCK)
        unit, inverse = normalised(middle[rows, :])
        grad = work[rows, :]
        gain_sum += fold(grad * unit)
        shift_sum += fold(grad)
        scaled = grad * second_gain[...]
        moved = scaled - jnp.mean(scaled, axis=-1, keepdims=True)
        moved -= unit * jnp.mean(scaled * unit, axis=-1, keepdims=True)
        grad_middle = cot[rows, :].astype(FULL) + inverse * moved
        work[rows, :] = grad_middle
        mixer_sum += fold(grad_middle * branch[rows, :])
        grad_branch = (grad_middle * mixer_scale[...]).astype(LOW)
        g_branch[rows, :] = grad_branch
        bias_sum += fold(grad_branch.astype(FULL))
        return gain_sum, shift_sum, mixer_sum, bias_sum

    zero = jnp.zeros((8, FEATURES), FULL)
    for line, total in zip((6, 7, 5, 4), lax.fori_loop(0, SLOTS // BLOCK, second_back, (zero,) * 4)):
        small[0, line : line + 1, :] = jnp.sum(total, axis=0, keepdims=True)
    swaps.push(g_branch.at[:, pl.ds(aligned(sibling * CHUNK, 128), CHUNK)], g_branch_far, 6, net.sib)
    pump(BACK_PUMP)

    for j in range(2):
        cols = slice(j * CHUNK, (j + 1) * CHUNK)
        mixed[:, cols] = dot_rows(g_branch[...], w_out[cols, :]).astype(LOW)
    swaps.landed(blended_t.at[1], 2)
    swaps.landed(g_branch_far, 6)
    weight_grad(
        6, rows_of(blended_t, 0), rows_of(blended_t, 1),
        g_branch[:, pl.ds(aligned(c * CHUNK, 128), CHUNK)], g_branch_far[...],
    )
    pump(BACK_PUMP)

    lane64 = lax.broadcasted_iota(jnp.int32, (GRID, 128), 1)

    def attend_back(pair):
        cols = slice(pair * 128, (pair + 1) * 128)
        key_cols = slice(768 + pair * 128, 896 + pair * 128)
        value_cols = slice(1536 + pair * 128, 1664 + pair * 128)
        q_pair, k_pair, v_pair, g_pair = qkv[:, cols], qkv[:, key_cols], qkv[:, value_cols], mixed[:, cols]
        k_turned = k_pair.T
        grad_keys = grad_values = None
        grad_queries = []
        for e in (0, 1):
            head = 2 * pair + e
            g_head = only(g_pair, e)
            asks = jnp.concatenate([only(q_pair, e), place_q[...]], axis=1)
            k_head = k_turned[e * 64 : (e + 1) * 64, :]
            across = None
            pieces = []
            for lo, hi in spans:
                low_share = chances[head, :, lo:hi]
                share = low_share.astype(FULL)
                weighed = share * dot_rows(v_pair, g_head[lo:hi, :])
                grad = (weighed - share * jnp.sum(weighed, axis=0, keepdims=True)).astype(LOW)
                pieces.append(dot(k_head, grad).astype(LOW).astype(FULL) * 0.125)
                part = dot(grad, asks[lo:hi, :])
                across = part if across is None else across + part
                part = dot(low_share, g_head[lo:hi, :])
                grad_values = part if grad_values is None else grad_values + part
            grad_keys = across[:, :128] if grad_keys is None else grad_keys + across[:, :128]
            grad_queries.append(jnp.concatenate(pieces, axis=1))
            marks = across[:, 128:]
            high = marks.astype(LOW)
            low = (marks - high.astype(FULL)).astype(LOW)
            pairs = dot(place_t[...], jnp.concatenate([high, low], axis=1))
            pairs = pairs[:, :128] + pairs[:, 128:]
            rows_part = jnp.where(lane64 < GRID, pairs[:GRID, :], 0.0)
            cols_part = jnp.where(lane64 >= GRID, pairs[GRID:, :], 0.0)
            rows_part = pltpu.roll(rows_part, 0, 1, stride=1, stride_axis=0)
            cols_part = pltpu.roll(cols_part, 64, 1, stride=1, stride_axis=0)
            for line, part in ((head, rows_part), (12 + head, cols_part)):
                spot = (line % 6) * 128
                small[0, 14 + line // 6 : 15 + line // 6, spot : spot + 128] = jnp.sum(part, axis=0, keepdims=True)
        grad_queries = jnp.concatenate(grad_queries, axis=0).T.astype(LOW)
        grad_values = grad_values.astype(LOW)
        qkv[:, cols] = grad_queries
        qkv[:, key_cols] = grad_keys.astype(LOW)
        qkv[:, value_cols] = grad_values
        small[0, 2:3, cols] = jnp.sum(grad_queries.astype(FULL), axis=0, keepdims=True)
        small[0, 3:4, cols] = jnp.sum(grad_values.astype(FULL), axis=0, keepdims=True)

    for pair in range(6):
        attend_back(pair)
        pump(BACK_PUMP)
    swaps.push(qkv.at[:, pl.ds(aligned(sibling * 1152, 128), 1152)], g_qkv_far, 7, net.sib)

    swaps.landed(normed_a_t.at[1], 1)
    swaps.landed(g_qkv_far, 7)
    for j in range(3):
        cols = slice(j * CHUNK, (j + 1) * CHUNK)
        weight_grad(
            7 + j, rows_of(normed_a_t, 0), rows_of(normed_a_t, 1),
            qkv[:, pl.ds(aligned(c * 1152 + j * CHUNK, 128), CHUNK)], g_qkv_far[:, cols],
        )
        pump(BACK_PUMP)

    for j in range(2):
        cols = slice(j * CHUNK, (j + 1) * CHUNK)
        branch[:, cols] = dot_rows(qkv[...], w_in[cols, :])
        pump(BACK_PUMP)

    def first_back(i, carry):
        gain_sum, shift_sum = carry
        rows = pl.ds(aligned(i * BLOCK, BLOCK), BLOCK)
        unit, inverse = normalised(tok[rows, :].astype(FULL))
        grad = branch[rows, :]
        gain_sum += fold(grad * unit)
        shift_sum += fold(grad)
        scaled = grad * first_gain[...]
        moved = scaled - jnp.mean(scaled, axis=-1, keepdims=True)
        moved -= unit * jnp.mean(scaled * unit, axis=-1, keepdims=True)
        work[rows, :] = work[rows, :] + inverse * moved
        return gain_sum, shift_sum

    for line, total in zip((0, 1), lax.fori_loop(0, SLOTS // BLOCK, first_back, (zero,) * 2)):
        small[0, line : line + 1, :] = jnp.sum(total, axis=0, keepdims=True)
    save_grad = pltpu.make_async_copy(work, input_grad_hbm, out_sem.at[0])
    save_grad.start()
    pump(BACK_PUMP)

    for j in range(2):
        cols = slice(j * CHUNK, (j + 1) * CHUNK)
        returned = dot(act[...], w_reduce[:, cols]) + return_bias[:, cols]
        mixed[:, cols] = (middle[:, cols] + feed_scale[:, cols] * returned).astype(LOW)
        small[0, 13:14, cols] = jnp.sum(cot[:, cols].astype(FULL) * returned, axis=0, keepdims=True)
        pump(BACK_PUMP)
    save_out = pltpu.make_async_copy(mixed, outputs_hbm, out_sem.at[1])
    save_out.start()

    rest = queue[:]
    queue.clear()
    weave([rest, sums.events()], 0)
    pump(len(queue))
    small_out[...] = small[5]
    saves = []
    for i, (stage, target) in enumerate(zip(stages, (g_in_hbm, g_out_hbm, g_expand_hbm, g_reduce_hbm))):
        saves.append(pltpu.make_async_copy(stage, target, out_sem.at[2 + i]))
        saves[-1].start()
    for group in gathers + scatters + [swaps, sums]:
        group.finish()
    for save in [save_grad, save_out] + saves:
        save.wait()


GATHER_LAG = 0
FORWARD_PUMP = 2
BACK_PUMP = 2


def one_kernel(
    tokens, project_in, project_out, expand_weight, reduce_weight, first_gain, first_shift, query_value_bias,
    output_bias, mixer_scale, second_gain, second_shift, hidden_bias, return_bias, feed_scale, position_table,
    image_sizes, cotangent,
):
    vector = lambda v: v.reshape(1, -1)
    table = jnp.transpose(position_table[:, ::-1, :], (0, 2, 1)).reshape(24, 127)
    table = jnp.pad(table.astype(LOW).astype(FULL), ((0, 0), (0, 1)))
    anywhere = pl.BlockSpec(memory_space=pl.ANY)
    vmem = pl.BlockSpec(memory_space=pltpu.VMEM)
    low = lambda *shape: pltpu.VMEM(shape, LOW)
    full = lambda *shape: pltpu.VMEM(shape, FULL)
    dma = lambda *shape: pltpu.SemaphoreType.DMA(shape)
    like = jax.ShapeDtypeStruct
    scratch = [low(16 * w[0], w[1]) for w in WEIGHTS]
    scratch += [full(w[0], w[1]) for w in WEIGHTS]
    T, D, F = SLOTS, FEATURES, HIDDEN
    scratch += [
        low(T, D), low(T, D), low(T, D), low(2, D, T), low(2, D, T), low(2, D, T), low(T, 3 * D),
        low(T, 128), low(T, 128), low(128, T), low(HEADS, T, T), low(T, D), full(T, D), full(T, D),
        low(T, F), low(F, T), low(16, 96, T), low(T, F), low(T, D), low(T, D), low(T, F // 2),
        low(T, D // 2), low(T, 3 * D // 2), full(T, D), full(6, 24, D), full(5, 24, D),
        dma(6), dma(6), dma(4, 20), dma(4, 20), dma(len(CHUNKS), 12), dma(len(CHUNKS), 12), dma(8), dma(8),
        dma(5), dma(5),
    ]
    for weight, _, order in CHUNKS:
        scratch += Scatter.shapes(weight, order)
    results = pl.pallas_call(
        layer_kernel,
        out_shape=[
            like((T, D), LOW), like((T, D), FULL), like((48, 3 * D), FULL), like((48, D), FULL), like((48, F), FULL),
            like((192, D), FULL), like((24, D), FULL),
        ],
        in_specs=[pl.BlockSpec(memory_space=pltpu.SMEM)] + [anywhere] * 6 + [vmem] * 11,
        out_specs=[anywhere] * 6 + [vmem],
        scratch_shapes=scratch,
        compiler_params=pltpu.CompilerParams(
            collective_id=0, has_side_effects=True, vmem_limit_bytes=VMEM_BYTES
        ),
    )(
        image_sizes, tokens, project_in, project_out, expand_weight, reduce_weight, cotangent, vector(first_gain),
        vector(first_shift), query_value_bias, vector(output_bias), vector(mixer_scale), vector(second_gain),
        vector(second_shift), vector(hidden_bias), vector(return_bias), vector(feed_scale), table,
    )
    small = results[6]
    grad_table = small[14:18].reshape(2, 12, 128)[:, :, :127].transpose(0, 2, 1)
    return (
        *results[:6], small[0], small[1], small[2:4], small[4], small[5], small[6], small[7],
        small[8:12].reshape(-1), small[12], small[13], grad_table,
    )


VMEM_BYTES = 64 * 2**20


def solution(mesh):
    placed = (
        P(("dp", "rep"), None),
        P("dp", None),
        P("dp", None),
        P("dp", None),
        P("dp", None),
        P(),
        P(),
        P(),
        P(),
        P(),
        P(),
        P(),
        P(),
        P(),
        P(),
        P(),
        P(("dp", "rep"), None),
        P(("dp", "rep"), None),
    )
    return jax.shard_map(
        one_kernel if tuple(mesh.shape.values()) == (16, 2) else shards,
        mesh=mesh,
        in_specs=placed,
        out_specs=(
            P(("dp", "rep"), None),
            P(("dp", "rep"), None),
            P("dp", None),
            P("dp", None),
            P("dp", None),
            P("dp", None),
            P(),
            P(),
            P(),
            P(),
            P(),
            P(),
            P(),
            P(),
            P(),
            P(),
            P(),
        ),
        check_vma=False,
    )
```

```python
import functools

import jax
import jax.numpy as jnp
from jax import lax
from jax.experimental import pallas as pl
from jax.experimental.pallas import tpu as pltpu
from jax.sharding import PartitionSpec as P

HEADS = 12
HEAD = 64
GRID = 64


EPS = 1e-06
MASKED = -1000000000.0


def layer_norm(values, gain, shift):
    centre = values - jnp.mean(values, axis=-1, keepdims=True)
    spread = jnp.mean(centre * centre, axis=-1, keepdims=True)
    return centre * lax.rsqrt(spread + EPS) * gain + shift


def gelu_exact(values):
    return jax.nn.gelu(values, approximate=False)


def shift_onehot(side):
    first_axis = lax.broadcasted_iota(jnp.int32, (side, side, 2 * side - 1), 0)
    second_axis = lax.broadcasted_iota(jnp.int32, (side, side, 2 * side - 1), 1)
    third_axis = lax.broadcasted_iota(jnp.int32, (side, side, 2 * side - 1), 2)
    return (first_axis - second_axis + side - 1 == third_axis).astype(jnp.float32)


def position_bias(shift_part, picks):
    between = jnp.einsum("tijh,tkj->tihk", shift_part, picks, preferred_element_type=jnp.float32)
    return jnp.einsum(
        "tqi,tihk->hqk", picks, between.astype(jnp.bfloat16), preferred_element_type=jnp.float32
    )


def group_scores(query_part, key_part, shift_part, picks, usable):
    scores = jnp.einsum("qhd,khd->hqk", query_part, key_part, preferred_element_type=jnp.float32)
    scores = scores + position_bias(shift_part, picks)
    return jnp.where(usable[None, None, :], scores, MASKED)


def attend_group(packed, picks, usable):
    query_part, key_part, value_part, shift_part = packed
    scores = group_scores(query_part, key_part, shift_part, picks, usable)
    highest = jnp.max(scores, axis=-1, keepdims=True)
    weights_raw = jnp.exp(scores - highest)
    totals = jnp.sum(weights_raw, axis=-1, keepdims=True)
    chances = (weights_raw / totals).astype(jnp.bfloat16)
    blended = jnp.einsum("hqk,khd->qhd", chances, value_part, preferred_element_type=jnp.float32)
    return (blended.astype(jnp.bfloat16), (highest + jnp.log(totals))[..., 0])


def attend_back(packed, picks, usable):
    query_part, key_part, value_part, grad_part, logsums, shift_part = packed
    scores = group_scores(query_part, key_part, shift_part, picks, usable)
    chances = jnp.exp(scores - logsums[..., None])
    grad_chance = jnp.einsum(
        "qhd,khd->hqk", grad_part, value_part, preferred_element_type=jnp.float32
    )
    row_dot = jnp.sum(chances * grad_chance, axis=-1, keepdims=True)
    grad_scores = (chances * (grad_chance - row_dot)).astype(jnp.bfloat16)
    grad_query = jnp.einsum(
        "hqk,khd->qhd", grad_scores, key_part, preferred_element_type=jnp.float32
    )
    grad_key = jnp.einsum(
        "hqk,qhd->khd", grad_scores, query_part, preferred_element_type=jnp.float32
    )
    grad_value = jnp.einsum(
        "hqk,qhd->khd", chances.astype(jnp.bfloat16), grad_part, preferred_element_type=jnp.float32
    )
    across = jnp.einsum("hqk,tkj->thqj", grad_scores, picks, preferred_element_type=jnp.float32)
    grad_shift = jnp.einsum(
        "tqi,thqj->tijh", picks.astype(jnp.float32), across, precision=lax.Precision.HIGHEST
    )
    return (
        grad_query.astype(jnp.bfloat16),
        grad_key.astype(jnp.bfloat16),
        grad_value.astype(jnp.bfloat16),
        grad_shift,
    )


def shards(
    tokens,
    project_in,
    project_out,
    expand_weight,
    reduce_weight,
    first_gain,
    first_shift,
    query_value_bias,
    output_bias,
    mixer_scale,
    second_gain,
    second_shift,
    hidden_bias,
    return_bias,
    feed_scale,
    position_table,
    image_sizes,
    cotangent,
):
    length = tokens.shape[0]
    width_model = tokens.shape[1]
    head_count = HEADS
    per_group = 4
    groups = head_count // per_group
    full_in, full_out, full_expand, full_reduce = (
        lax.all_gather(project_in, "dp", axis=0, tiled=True),
        lax.all_gather(project_out, "dp", axis=0, tiled=True),
        lax.all_gather(expand_weight, "dp", axis=0, tiled=True),
        lax.all_gather(reduce_weight, "dp", axis=0, tiled=True),
    )
    inputs = tokens.astype(jnp.float32)
    normed_a, first_back = jax.vjp(layer_norm, inputs, first_gain, first_shift)
    normed_a_low = normed_a.astype(jnp.bfloat16)
    projected = jnp.dot(normed_a_low, full_in, preferred_element_type=jnp.float32)
    queries = ((projected[:, :width_model] + query_value_bias[0]) * HEAD ** (-0.5)).astype(
        jnp.bfloat16
    )
    keys_low = projected[:, width_model : 2 * width_model].astype(jnp.bfloat16)
    values_low = (projected[:, 2 * width_model :] + query_value_bias[1]).astype(jnp.bfloat16)
    shift_table = shift_onehot(GRID)
    shifts = jnp.einsum(
        "ija,tah->tijh",
        shift_table.astype(jnp.bfloat16),
        position_table.astype(jnp.bfloat16),
        preferred_element_type=jnp.float32,
    ).astype(jnp.bfloat16)
    shifts_grouped = shifts.reshape(2, GRID, GRID, groups, per_group).transpose(3, 0, 1, 2, 4)
    places = jnp.arange(length, dtype=jnp.int32)
    height = image_sizes[0, 0]
    width_image = image_sizes[0, 1]
    grid_iota = jnp.arange(GRID, dtype=jnp.int32)
    picks = jnp.stack(
        [
            (places // width_image)[:, None] == grid_iota[None, :],
            (places % width_image)[:, None] == grid_iota[None, :],
        ]
    ).astype(jnp.bfloat16)
    usable = places < height * width_image

    def split_heads(matrix):
        return matrix.reshape(length, groups, per_group, HEAD).transpose(1, 0, 2, 3)

    def join_heads(blocks):
        return blocks.transpose(1, 0, 2, 3).reshape(length, width_model)

    query_groups = split_heads(queries)
    key_groups = split_heads(keys_low)
    value_groups = split_heads(values_low)
    blended_groups, logsums = lax.map(
        lambda packed: attend_group(packed, picks, usable),
        (query_groups, key_groups, value_groups, shifts_grouped),
    )
    blended = join_heads(blended_groups)
    branch = jnp.dot(blended, full_out, preferred_element_type=jnp.float32) + output_bias
    middle = inputs + mixer_scale * branch
    normed_b, second_back = jax.vjp(layer_norm, middle, second_gain, second_shift)
    normed_b_low = normed_b.astype(jnp.bfloat16)
    preact = jnp.dot(normed_b_low, full_expand, preferred_element_type=jnp.float32) + hidden_bias
    activated, gelu_back = jax.vjp(gelu_exact, preact)
    activated_low = activated.astype(jnp.bfloat16)
    returned = jnp.dot(activated_low, full_reduce, preferred_element_type=jnp.float32) + return_bias
    outputs = middle + feed_scale * returned
    back_in, back_out, back_expand, back_reduce = (
        lax.all_gather(project_in, "dp", axis=0, tiled=True),
        lax.all_gather(project_out, "dp", axis=0, tiled=True),
        lax.all_gather(expand_weight, "dp", axis=0, tiled=True),
        lax.all_gather(reduce_weight, "dp", axis=0, tiled=True),
    )
    upstream = cotangent.astype(jnp.float32)
    grad_feed_scale = jnp.sum(upstream * returned, axis=0)
    grad_returned = (upstream * feed_scale).astype(jnp.bfloat16)
    grad_return_bias = jnp.sum(grad_returned.astype(jnp.float32), axis=0)
    grad_reduce = jnp.einsum(
        "tf,td->fd", activated_low, grad_returned, preferred_element_type=jnp.float32
    )
    grad_activated = jnp.einsum(
        "td,fd->tf", grad_returned, back_reduce, preferred_element_type=jnp.float32
    )
    grad_preact = gelu_back(grad_activated)[0].astype(jnp.bfloat16)
    grad_hidden_bias = jnp.sum(grad_preact.astype(jnp.float32), axis=0)
    grad_expand = jnp.einsum(
        "td,tf->df", normed_b_low, grad_preact, preferred_element_type=jnp.float32
    )
    grad_normed_b = jnp.einsum(
        "tf,df->td", grad_preact, back_expand, preferred_element_type=jnp.float32
    )
    grad_from_norm, grad_second_gain, grad_second_shift = second_back(grad_normed_b)
    grad_middle = upstream + grad_from_norm
    grad_mixer_scale = jnp.sum(grad_middle * branch, axis=0)
    grad_branch = (grad_middle * mixer_scale).astype(jnp.bfloat16)
    grad_output_bias = jnp.sum(grad_branch.astype(jnp.float32), axis=0)
    grad_project_out = jnp.einsum(
        "td,te->de", blended, grad_branch, preferred_element_type=jnp.float32
    )
    grad_blended = jnp.einsum(
        "te,de->td", grad_branch, back_out, preferred_element_type=jnp.float32
    ).astype(jnp.bfloat16)
    grad_query_groups, grad_key_groups, grad_value_groups, grad_shift_groups = lax.map(
        lambda packed: attend_back(packed, picks, usable),
        (
            query_groups,
            key_groups,
            value_groups,
            split_heads(grad_blended),
            logsums,
            shifts_grouped,
        ),
    )
    grad_queries = join_heads(grad_query_groups) * HEAD ** (-0.5)
    grad_keys = join_heads(grad_key_groups)
    grad_values = join_heads(grad_value_groups)
    grad_projected = jnp.concatenate([grad_queries, grad_keys, grad_values], axis=1)
    grad_query_value_bias = jnp.stack(
        [
            jnp.sum(grad_queries.astype(jnp.float32), axis=0),
            jnp.sum(grad_values.astype(jnp.float32), axis=0),
        ]
    )
    grad_project_in = jnp.einsum(
        "td,te->de", normed_a_low, grad_projected, preferred_element_type=jnp.float32
    )
    grad_normed_a = jnp.einsum(
        "te,de->td", grad_projected, back_in, preferred_element_type=jnp.float32
    )
    grad_from_first, grad_first_gain, grad_first_shift = first_back(grad_normed_a)
    input_grad = grad_middle + grad_from_first
    grad_shift = grad_shift_groups.transpose(1, 2, 3, 0, 4).reshape(2, GRID, GRID, head_count)
    grad_position_table = jnp.einsum(
        "ija,tijh->tah", shift_table, grad_shift, precision=lax.Precision.HIGHEST
    )
    weight_grads = (
        lax.psum_scatter(grad_project_in, "dp", scatter_dimension=0, tiled=True),
        lax.psum_scatter(grad_project_out, "dp", scatter_dimension=0, tiled=True),
        lax.psum_scatter(grad_expand, "dp", scatter_dimension=0, tiled=True),
        lax.psum_scatter(grad_reduce, "dp", scatter_dimension=0, tiled=True),
    )
    weight_grads = lax.psum(
        (weight_grads[0], weight_grads[1], weight_grads[2], weight_grads[3]), "rep"
    )
    small_sums = lax.psum(
        (
            grad_first_gain,
            grad_first_shift,
            grad_query_value_bias,
            grad_output_bias,
            grad_mixer_scale,
            grad_second_gain,
            grad_second_shift,
            grad_hidden_bias,
            grad_return_bias,
            grad_feed_scale,
            grad_position_table,
        ),
        ("dp", "rep"),
    )
    return (
        outputs.astype(jnp.bfloat16),
        input_grad,
        weight_grads[0],
        weight_grads[1],
        weight_grads[2],
        weight_grads[3],
        small_sums[0],
        small_sums[1],
        small_sums[2],
        small_sums[3],
        small_sums[4],
        small_sums[5],
        small_sums[6],
        small_sums[7],
        small_sums[8],
        small_sums[9],
        small_sums[10],
    )


FEATURES = 768
HIDDEN = 3072
SLOTS = 448
MESH = pl.DeviceIdType.MESH
LOW = jnp.bfloat16
FULL = jnp.float32

W_IN = (48, 2304, False, "A")
W_OUT = (48, 768, False, "A")
W_EXPAND = (48, 3072, False, "A")
W_REDUCE = (192, 768, True, "B")
WEIGHTS = (W_IN, W_OUT, W_EXPAND, W_REDUCE)

PARTS = ((0, 0, 1, "A"), (1, 0, 1, "A"), (2, 0, 2, "A"), (2, 1, 2, "A"), (3, 0, 2, "B"), (3, 1, 2, "B"))

CHUNK = 384
CHUNKS = (
    (3, 0, "B"), (3, 1, "A"),
    (2, 0, "A"), (2, 1, "B"), (2, 2, "A"), (2, 3, "A"),
    (1, 0, "B"),
    (0, 0, "A"), (0, 1, "B"), (0, 2, "A"),
)


def aligned(index, step):
    return pl.multiple_of(index, step)


class Net:
    def __init__(self):
        dp, c = lax.axis_index("dp"), lax.axis_index("rep")
        z, y, x = dp // 4, lax.rem(dp // 2, 2), lax.rem(dp, 2)
        self.dp, self.c, self.z, self.y, self.x = dp, c, z, y, x
        self.ma = y * (1 - c) + x * c
        self.mb = x * (1 - c) + y * c
        self.wa, self.wb = 2 - c, 1 + c
        self.to_a = (dp + self.wa * (1 - 2 * self.ma), c)
        self.to_b = (dp + self.wb * (1 - 2 * self.mb), c)
        self.to_z = (lax.rem(dp + 4, 16), c)
        self.from_z = (lax.rem(dp + 12, 16), c)
        self.far_z = (lax.rem(dp + 8, 16), c)
        self.sib = (dp, 1 - c)

    def barrier(self):
        sem = pltpu.get_barrier_semaphore()
        for target in (self.to_a, self.to_b, self.to_z, self.from_z, self.far_z, self.sib):
            pl.semaphore_signal(sem, inc=1, device_id=target, device_id_type=MESH)
        pl.semaphore_wait(sem, 6)

    def back(self, steps):
        return lax.rem(self.z + 4 - steps, 4)

    def owner(self, z, a, b):
        return 4 * z + self.wa * a + self.wb * b


class Transfers:
    def __init__(self, net, send, recv):
        self.net, self.send, self.recv, self.sent = net, send, recv, []

    def push(self, src, dst, slot, to):
        copy = pltpu.make_async_remote_copy(
            src, dst, self.send.at[len(self.sent)], self.recv.at[slot], device_id=to, device_id_type=MESH
        )
        copy.start()
        self.sent.append(copy)

    def landed(self, dst, slot):
        pltpu.make_async_remote_copy(
            dst, dst, self.send.at[0], self.recv.at[slot], device_id=self.net.sib, device_id_type=MESH
        ).wait_recv()

    def finish(self):
        for copy in self.sent:
            copy.wait_send()


class Gather(Transfers):
    def __init__(self, net, part, buf, send, recv, name):
        super().__init__(net, send, recv)
        weight, self.part, self.parts, self.order = part
        self.buf, self.name = buf, name
        self.rows, self.cols, self.by_rows, _ = WEIGHTS[weight]

    def span(self, c):
        half = (self.rows if self.by_rows else self.cols) // 2
        size = half // self.parts
        return c * half + self.part * size, size

    def block(self, owner):
        start, size = self.span(self.net.c)
        if self.by_rows:
            return self.buf.at[pl.ds(aligned(owner * self.rows + start, 16), size), :]
        return self.buf.at[pl.ds(aligned(owner * self.rows, 16), self.rows), pl.ds(aligned(start, 128), size)]

    def group(self, z, c):
        start, size = self.span(c)
        if self.by_rows:
            pieces = self.rows // size
            return self.buf.reshape(4, 4, pieces, size, self.cols).at[z, :, c * self.parts + self.part]
        rows = 4 * self.rows
        return self.buf.at[pl.ds(aligned(z * rows, 16), rows), pl.ds(aligned(start, 128), size)]

    def load(self, src, sem):
        start, size = self.span(self.net.c)
        if self.by_rows:
            part = src.at[pl.ds(aligned(start, 16), size), :]
        else:
            part = src.at[:, pl.ds(aligned(start, 128), size)]
        self.copy = pltpu.make_async_copy(part, self.block(self.net.dp), sem)
        self.copy.start()

    def jobs(self):
        net = self.net
        ma, mb = net.ma, net.mb

        def near(back, other):
            return self.block(net.owner(net.back(back), ma, mb + other * (1 - 2 * mb)))

        def far(back, other):
            return self.block(net.owner(net.back(back), 1 - ma, mb + other * (1 - 2 * mb)))

        def own():
            self.copy.wait()
            ref = near(0, 0)
            self.push(ref, ref, 2, net.to_z)
            self.push(ref, ref, 1, net.to_b)
            self.push(ref, ref, 8, net.to_a)

        def relay(back, other):
            def run():
                ref = near(back, other)
                self.landed(ref, back * 2 + other)
                if back < 3 and (other == 0 or self.order == "A"):
                    self.push(ref, ref, (back + 1) * 2 + other, net.to_z)
                if self.order == "B" and other == 0:
                    self.push(ref, ref, back * 2 + 1, net.to_b)
                self.push(ref, ref, 8 + back * 2 + other, net.to_a)

            return run

        def tail(back):
            def run():
                for other in (0, 1):
                    self.landed(far(back, other), 8 + back * 2 + other)
                ref = self.group(net.back(back), net.c)
                self.push(ref, ref, 16 + back, net.sib)

            return run

        def complete():
            for back in range(4):
                self.landed(self.group(net.back(back), 1 - net.c), 16 + back)

        table = {"own": own, "r01": relay(0, 1)}
        for back in (1, 2, 3):
            table["r%d0" % back], table["r%d1" % back] = relay(back, 0), relay(back, 1)
        for back in range(4):
            table["t%d" % back] = tail(back)
        table["all"] = complete
        return {self.name + key: job for key, job in table.items()}


class Scatter(Transfers):
    def __init__(self, net, weight, column, order, refs, stage, send, recv, name):
        super().__init__(net, send, recv)
        self.order, self.name = order, name
        self.rows, self.cols, self.by_rows, _ = WEIGHTS[weight]
        self.g, self.ra, self.rb, self.rz = refs
        self.stage, self.column = stage, column
        self.rh = self.rows // 2 if self.by_rows else self.rows

    def produced(self, back):
        net = self.net
        self.push(self.g.at[net.back(back), 1 - net.ma], self.ra.at[back], back, net.to_a)

    def add_into(self, dst, terms, pair):
        def body(i, carry):
            rows = pl.ds(aligned(i * 16, 16), 16)
            for index in ((0, rows), (1, rows)) if pair else ((rows,),):
                total = dst[(*index, slice(None))].astype(FULL)
                for term in terms:
                    total += term[(*index, slice(None))].astype(FULL)
                dst[(*index, slice(None))] = total.astype(LOW)
            return carry

        lax.fori_loop(0, self.rh // 16, body, 0)

    def part_of_stage(self, c):
        if self.by_rows:
            return self.stage.at[pl.ds(aligned(c * self.rh, 16), self.rh), pl.ds(self.column * CHUNK, CHUNK)]
        return self.stage.at[:, pl.ds(aligned(c * (self.cols // 2) + self.column * CHUNK, 128), CHUNK)]

    def last(self, terms):
        mine = self.part_of_stage(self.net.c)

        def body(i, carry):
            rows = pl.ds(aligned(i * 16, 16), 16)
            total = terms[0][rows, :].astype(FULL)
            for term in terms[1:]:
                total += term[rows, :].astype(FULL)
            mine[rows, :] = total
            return carry

        lax.fori_loop(0, self.rh // 16, body, 0)
        self.push(mine, mine, 11, self.net.sib)

    def got(self):
        self.landed(self.part_of_stage(1 - self.net.c), 11)

    def jobs(self):
        net, g, ra, rb, rz = self.net, self.g, self.ra, self.rb, self.rz
        ma, mb = net.ma, net.mb

        def step_a(s):
            def run():
                back = (s + 1) % 4
                self.landed(ra.at[back], back)
                terms = [ra.at[back]]
                if s > 0:
                    self.landed(rz.at[s - 1], 8 + s - 1)
                    terms.append(rz.at[s - 1])
                dst = g.at[net.back(back), ma]
                self.add_into(dst, terms, True)
                if s < 3:
                    self.push(dst, rz.at[s], 8 + s, net.to_z)
                else:
                    self.push(dst.at[1 - mb], rb.at[0], 4, net.to_b)

            return run

        def final_a():
            self.landed(rb.at[0], 4)
            self.last([g.at[net.z, ma, mb], rb.at[0]])

        def first_b(back):
            def run():
                self.landed(ra.at[back], back)
                dst = g.at[net.back(back), ma]
                self.add_into(dst, [ra.at[back]], True)
                self.push(dst.at[1 - mb], rb.at[back], 4 + back, net.to_b)

            return run

        def step_b(s):
            def run():
                back = (s + 1) % 4
                self.landed(rb.at[back], 4 + back)
                terms = [rb.at[back]]
                if s > 0:
                    self.landed(rz.at[s - 1], 8 + s - 1)
                    terms.append(rz.at[s - 1])
                dst = g.at[net.back(back), ma, mb]
                if s < 3:
                    self.add_into(dst, terms, False)
                    self.push(dst, rz.at[s], 8 + s, net.to_z)
                else:
                    self.last([dst] + terms)

            return run

        if self.order == "A":
            steps = [step_a(s) for s in range(4)] + [final_a]
        else:
            steps = [first_b(back) for back in (1, 2, 3, 0)] + [step_b(s) for s in range(4)]
        table = {"%se%d" % (self.name, i): step for i, step in enumerate(steps)}
        table[self.name + "all"] = self.got
        return table

    @staticmethod
    def shapes(weight, order):
        rows, _, by_rows, _ = WEIGHTS[weight]
        block = (rows // 2 if by_rows else rows, CHUNK)
        relay = (3, 2) if order == "A" else (3,)
        return [
            pltpu.VMEM((4, 2, 2) + block, LOW),
            pltpu.VMEM((4, 2) + block, LOW),
            pltpu.VMEM((1 if order == "A" else 4,) + block, LOW),
            pltpu.VMEM(relay + block, LOW),
        ]


class SmallSum(Transfers):
    def __init__(self, net, buf, landing, send, recv):
        super().__init__(net, send, recv)
        self.buf, self.landing = buf, landing
        place, z = lax.rem(net.dp, 4), net.z
        near_z = z + 1 - 2 * lax.rem(z, 2)
        self.partners = [
            net.sib,
            (net.dp + 1 - 2 * net.x, net.c),
            (net.dp + 2 - 4 * net.y, net.c),
            (near_z * 4 + place, net.c),
            net.far_z,
        ]

    def jobs(self):
        def start(i):
            def run():
                self.push(self.buf.at[i], self.landing.at[i], i, self.partners[i])

            return run

        def add(i):
            def run():
                self.landed(self.landing.at[i], i)
                self.buf[i + 1] = self.buf[i] + self.landing[i]
                if i < 4:
                    start(i + 1)()

            return run

        table = {"sum%d" % i: add(i) for i in range(5)}
        table["sum"] = start(0)
        return table


def dot(left, right):
    return jnp.dot(left, right, preferred_element_type=FULL)


def dot_rows(left, right):
    return lax.dot_general(left, right, (((1,), (1,)), ((), ())), preferred_element_type=FULL)


def fold(values):
    return jnp.sum(values.reshape(values.shape[0] // 8, 8, values.shape[1]), axis=0)


def normalised(values):
    centre = values - jnp.mean(values, axis=-1, keepdims=True)
    inverse = lax.rsqrt(jnp.mean(centre * centre, axis=-1, keepdims=True) + EPS)
    return centre * inverse, inverse


BLOCK = 64
ROOT_HALF = 0.7071067811865476
DENSITY = 0.3989422804014327


class Line:
    def __init__(self, ref):
        self.ref = ref

    def __getitem__(self, index):
        cols = slice(None) if index is Ellipsis else index[1]
        return self.ref[cols].reshape(1, -1)


def layer_kernel(
    sizes, tokens_hbm, w_in_hbm, w_out_hbm, w_expand_hbm, w_reduce_hbm, cotangent_hbm,
    first_gain, first_shift, query_value_bias, output_bias, mixer_scale, second_gain, second_shift,
    hidden_bias, return_bias, feed_scale, table,
    outputs_hbm, input_grad_hbm, g_in_hbm, g_out_hbm, g_expand_hbm, g_reduce_hbm, small_out,
    w_in, w_out, w_expand, w_reduce,
    stage_in, stage_out, stage_expand, stage_reduce,
    tok, cot, normed, normed_a_t, normed_b_t, blended_t, qkv, place_q, place_k, place_t,
    chances, mixed, branch, middle, act, act_t, act_t_far, slope, g_ret, g_ret_far, g_pre_far,
    g_branch_far, g_qkv_far, work, small, small_landing,
    load_sem, out_sem, gather_send, gather_recv, scatter_send, scatter_recv, swap_send, swap_recv,
    small_send, small_recv, *scatter_refs,
):
    net = Net()
    first_gain, first_shift, output_bias, mixer_scale, second_gain, second_shift, hidden_bias, return_bias, feed_scale = map(
        Line,
        (first_gain, first_shift, output_bias, mixer_scale, second_gain, second_shift, hidden_bias, return_bias, feed_scale),
    )
    g_branch = normed
    c = net.c
    sibling = 1 - c

    weights = [w_in, w_out, w_expand, w_reduce]
    sources = [w_in_hbm, w_out_hbm, w_expand_hbm, w_reduce_hbm]
    jobs = {}

    def job(name):
        def note(function):
            jobs[name] = function
            return function

        return note

    gathers = []
    for i, part in enumerate(PARTS):
        gather = Gather(net, part, weights[part[0]], gather_send.at[i], gather_recv.at[i], "g%d" % i)
        gather.load(sources[part[0]], load_sem.at[i])
        gathers.append(gather)
        jobs.update(gather.jobs())
    load_tok = pltpu.make_async_copy(tokens_hbm, tok, load_sem.at[len(PARTS)])
    load_cot = pltpu.make_async_copy(cotangent_hbm, cot, load_sem.at[len(PARTS) + 1])
    load_tok.start()
    load_cot.start()
    net.barrier()

    stages = [stage_in, stage_out, stage_expand, stage_reduce]
    scatters = []
    for i, (weight, column, order) in enumerate(CHUNKS):
        scatters.append(
            Scatter(net, weight, column, order, scatter_refs[4 * i : 4 * i + 4], stages[weight],
                    scatter_send.at[i], scatter_recv.at[i], "s%d" % i)
        )
    swaps = Transfers(net, swap_send, swap_recv)
    sums = SmallSum(net, small, small_landing, small_send, small_recv)
    for group in scatters + [sums]:
        jobs.update(group.jobs())

    @job("norm")
    def _():
        load_tok.wait()
        load_cot.wait()

        def first_rows(i, carry):
            rows = pl.ds(aligned(i * BLOCK, BLOCK), BLOCK)
            unit, _ = normalised(tok[rows, :].astype(FULL))
            normed[rows, :] = (unit * first_gain[...] + first_shift[...]).astype(LOW)
            returned_grad = (cot[rows, :].astype(FULL) * feed_scale[...]).astype(LOW)
            g_ret[rows, :] = returned_grad
            return carry + fold(returned_grad.astype(FULL))

        total = lax.fori_loop(0, SLOTS // BLOCK, first_rows, jnp.zeros((8, FEATURES), FULL))
        small[0] = jnp.zeros_like(small[0])
        small[0, 12:13, :] = jnp.sum(total, axis=0, keepdims=True)
        swaps.push(g_ret, g_ret_far, 0, net.sib)

    def turn(source, target):
        for j in range(FEATURES // 128):
            target[0, j * 128 : (j + 1) * 128, :] = source[:, j * 128 : (j + 1) * 128].T

    @job("turn")
    def _():
        turn(normed, normed_a_t)
        swaps.push(normed_a_t.at[0], normed_a_t.at[1], 1, net.sib)

    height, width = sizes[0, 0], sizes[0, 1]
    width_f = width.astype(FULL)
    live = (height * width).astype(FULL)

    def grid_place(slot):
        row = jnp.floor((slot + 0.5) / width_f)
        return row, slot - row * width_f

    @job("place")
    def _():
        slot = lax.broadcasted_iota(jnp.int32, (SLOTS, 128), 0).astype(FULL)
        lane = lax.broadcasted_iota(jnp.int32, (SLOTS, 128), 1).astype(FULL)
        row, col = grid_place(slot)
        hit = jnp.where(jnp.where(lane < GRID, row, col + GRID) == lane, 1.0, 0.0)
        place_q[...] = hit.astype(LOW)
        place_k[...] = jnp.where(slot < live, hit, jnp.where(lane == GRID - 1, 1.0, 0.0)).astype(LOW)
        slot = lax.broadcasted_iota(jnp.int32, (128, SLOTS), 1).astype(FULL)
        lane = lax.broadcasted_iota(jnp.int32, (128, SLOTS), 0).astype(FULL)
        row, col = grid_place(slot)
        hit = jnp.where(lane < GRID, GRID - 1 - row, 2 * GRID - 1 - col) == lane
        place_t[...] = jnp.where(hit, 1.0, 0.0).astype(LOW)

    def project(j):
        cols = slice(j * CHUNK, (j + 1) * CHUNK)
        part = dot(normed[...], w_in[:, cols])
        inner = slice((j % 2) * CHUNK, (j % 2 + 1) * CHUNK)
        if j < 2:
            part = (part + query_value_bias[0:1, inner]) * 0.125
        elif j >= 4:
            part = part + query_value_bias[1:2, inner]
        qkv[:, cols] = part.astype(LOW)

    for j in range(6):
        jobs["qkv%d" % j] = functools.partial(project, j)

    lane128 = lax.broadcasted_iota(jnp.int32, (128, 128), 1)
    row128 = lax.broadcasted_iota(jnp.int32, (128, 128), 0)
    half_lane = lax.broadcasted_iota(jnp.int32, (SLOTS, 128), 1)
    no_key = (lane128 == GRID - 1) & (row128 < GRID) & (jnp.full((128, 128), live) < SLOTS)
    spans = ((0, 256), (256, SLOTS))

    def only(values, e):
        keep = half_lane < 64 if e == 0 else half_lane >= 64
        return jnp.where(keep, values, jnp.zeros_like(values))

    def bias_table(head):
        rows_part = jnp.broadcast_to(table[head : head + 1, :], (GRID, 128))
        cols_part = jnp.broadcast_to(table[12 + head : 13 + head, :], (GRID, 128))
        both = jnp.concatenate(
            [
                pltpu.roll(rows_part, 65, 1, stride=1, stride_axis=0),
                pltpu.roll(cols_part, 1, 1, stride=1, stride_axis=0),
            ],
            axis=0,
        )
        both = jnp.where(lane128 // GRID == row128 // GRID, both, 0.0)
        return jnp.where(no_key, MASKED, both).astype(LOW)

    def attend(head):
        pair, e = head // 2, head % 2
        cols = slice(pair * 128, (pair + 1) * 128)
        keys = jnp.concatenate([qkv[:, 768 + pair * 128 : 896 + pair * 128], place_k[...]], axis=1)
        v_head = qkv[:, 1536 + pair * 128 : 1664 + pair * 128].T[e * 64 : (e + 1) * 64, :]
        bias = dot(place_q[...], bias_table(head)).astype(LOW)
        asks = jnp.concatenate([only(qkv[:, cols], e), bias], axis=1)
        for lo, hi in spans:
            scores = dot_rows(keys, asks[lo:hi, :])
            raised = jnp.exp(scores - jnp.max(scores, axis=0, keepdims=True))
            share = (raised * (1.0 / jnp.sum(raised, axis=0, keepdims=True))).astype(LOW)
            chances[head, :, lo:hi] = share
            blended_t[0, head * 64 : (head + 1) * 64, lo:hi] = dot(v_head, share).astype(LOW)
        if e == 1:
            mixed[:, cols] = blended_t[0, cols, :].T
        if head == HEADS - 1:
            swaps.push(blended_t.at[0], blended_t.at[1], 2, net.sib)

    for head in range(HEADS):
        jobs["att%d" % head] = functools.partial(attend, head)

    @job("mix")
    def _():
        for j in range(2):
            cols = slice(j * CHUNK, (j + 1) * CHUNK)
            branch[:, cols] = dot(mixed[...], w_out[:, cols]) + output_bias[:, cols]

    @job("middle")
    def _():
        def middle_rows(i, carry):
            rows = pl.ds(aligned(i * BLOCK, BLOCK), BLOCK)
            mid = tok[rows, :].astype(FULL) + mixer_scale[...] * branch[rows, :]
            middle[rows, :] = mid
            unit, _ = normalised(mid)
            normed[rows, :] = (unit * second_gain[...] + second_shift[...]).astype(LOW)
            return carry

        lax.fori_loop(0, SLOTS // BLOCK, middle_rows, 0)
        turn(normed, normed_b_t)
        swaps.push(normed_b_t.at[0], normed_b_t.at[1], 3, net.sib)

    act_blocks = act_t.reshape(16, 2, 96, SLOTS)

    def hidden(j):
        cols = slice(j * CHUNK, (j + 1) * CHUNK)
        pre = dot(normed[...], w_expand[:, cols]) + hidden_bias[:, cols]
        share = 0.5 + 0.5 * lax.erf(pre * ROOT_HALF)
        active = (pre * share).astype(LOW)
        act[:, cols] = active
        slope[:, cols] = (share + pre * (DENSITY * jnp.exp(-0.5 * pre * pre))).astype(LOW)
        for k in range(3):
            act_t[j * CHUNK + k * 128 : j * CHUNK + (k + 1) * 128, :] = active[:, k * 128 : (k + 1) * 128].T

    for i, j in enumerate((0, 1, 4, 5, 2, 3, 6, 7)):
        jobs["hid%d" % i] = functools.partial(hidden, j)

    @job("act")
    def _():
        swaps.push(act_blocks.at[:, sibling], act_t_far, 4, net.sib)

    def place_of(owner):
        oy, ox = owner // 2, owner % 2
        return oy * (1 - c) + ox * c, ox * (1 - c) + oy * c

    def weight_grad(index, order, left, left_far, right, right_far):
        scatter = scatters[index]
        back = (1, 2, 3, 0)[order]
        z = net.back(back)
        tile = (dot(left(z), right) + dot(left_far(z), right_far)).astype(LOW)
        for owner in range(4):
            pa, pb = place_of(owner)
            scatter.g[z, pa, pb] = tile[owner * scatter.rh : (owner + 1) * scatter.rh, :]
        scatter.produced(back)

    def rows_of(ref, slot):
        return lambda z: ref[slot, pl.ds(aligned(z * 192, 64), 192), :]

    def grad_reduce(j, order):
        cols = slice(j * CHUNK, (j + 1) * CHUNK)
        if (j, order) == (0, 0):
            swaps.landed(g_ret_far, 0)
            swaps.landed(act_t_far, 4)
        weight_grad(
            j, order,
            lambda z: act_blocks[pl.ds(4 * z, 4), c].reshape(384, SLOTS),
            lambda z: act_t_far[pl.ds(4 * z, 4)].reshape(384, SLOTS),
            g_ret[:, cols], g_ret_far[:, cols],
        )

    for j in range(2):
        for order in range(4):
            jobs["wr%d%d" % (j, order)] = functools.partial(grad_reduce, j, order)

    def grad_hidden(j):
        half = sibling if j < 4 else c
        cols = pl.ds(aligned(half * 1536 + (j % 4) * CHUNK, 128), CHUNK)
        part = (dot_rows(g_ret[...], w_reduce[cols, :]) * slope[:, cols].astype(FULL)).astype(LOW)
        slope[:, cols] = part
        summed = jnp.sum(part.astype(FULL), axis=0, keepdims=True)
        small[0, pl.ds(8 + 2 * half + (j % 4) // 2, 1), (j % 2) * CHUNK : (j % 2 + 1) * CHUNK] = summed
        if j == 3:
            swaps.push(slope.at[:, pl.ds(aligned(sibling * 1536, 128), 1536)], g_pre_far, 5, net.sib)

    for j in range(8):
        jobs["ga%d" % j] = functools.partial(grad_hidden, j)

    def grad_expand(j, order):
        if (j, order) == (0, 0):
            swaps.landed(normed_b_t.at[1], 3)
            swaps.landed(g_pre_far, 5)
        weight_grad(
            2 + j, order, rows_of(normed_b_t, 0), rows_of(normed_b_t, 1),
            slope[:, pl.ds(aligned(c * 1536 + j * CHUNK, 128), CHUNK)], g_pre_far[:, j * CHUNK : (j + 1) * CHUNK],
        )

    for j in range(4):
        for order in range(4):
            jobs["we%d%d" % (j, order)] = functools.partial(grad_expand, j, order)

    def grad_normed_b(j):
        cols = slice(j * CHUNK, (j + 1) * CHUNK)
        work[:, cols] = dot_rows(slope[...], w_expand[cols, :])

    for j in range(2):
        jobs["gnb%d" % j] = functools.partial(grad_normed_b, j)

    zero = jnp.zeros((8, FEATURES), FULL)

    @job("sback")
    def _():
        def second_back(i, carry):
            gain_sum, shift_sum, mixer_sum, bias_sum = carry
            rows = pl.ds(aligned(i * BLOCK, BLOCK), BLOCK)
            unit, inverse = normalised(middle[rows, :])
            grad = work[rows, :]
            gain_sum += fold(grad * unit)
            shift_sum += fold(grad)
            scaled = grad * second_gain[...]
            moved = scaled - jnp.mean(scaled, axis=-1, keepdims=True)
            moved -= unit * jnp.mean(scaled * unit, axis=-1, keepdims=True)
            grad_middle = cot[rows, :].astype(FULL) + inverse * moved
            work[rows, :] = grad_middle
            mixer_sum += fold(grad_middle * branch[rows, :])
            grad_branch = (grad_middle * mixer_scale[...]).astype(LOW)
            g_branch[rows, :] = grad_branch
            bias_sum += fold(grad_branch.astype(FULL))
            return gain_sum, shift_sum, mixer_sum, bias_sum

        for line, total in zip((6, 7, 5, 4), lax.fori_loop(0, SLOTS // BLOCK, second_back, (zero,) * 4)):
            small[0, line : line + 1, :] = jnp.sum(total, axis=0, keepdims=True)
        swaps.push(g_branch.at[:, pl.ds(aligned(sibling * CHUNK, 128), CHUNK)], g_branch_far, 6, net.sib)

    @job("gbl")
    def _():
        for j in range(2):
            cols = slice(j * CHUNK, (j + 1) * CHUNK)
            mixed[:, cols] = dot_rows(g_branch[...], w_out[cols, :]).astype(LOW)

    def grad_out(order):
        if order == 0:
            swaps.landed(blended_t.at[1], 2)
            swaps.landed(g_branch_far, 6)
        weight_grad(
            6, order, rows_of(blended_t, 0), rows_of(blended_t, 1),
            g_branch[:, pl.ds(aligned(c * CHUNK, 128), CHUNK)], g_branch_far[...],
        )

    for order in range(4):
        jobs["wo%d" % order] = functools.partial(grad_out, order)

    lane64 = lax.broadcasted_iota(jnp.int32, (GRID, 128), 1)

    def attend_back(pair):
        cols = slice(pair * 128, (pair + 1) * 128)
        key_cols = slice(768 + pair * 128, 896 + pair * 128)
        value_cols = slice(1536 + pair * 128, 1664 + pair * 128)
        q_pair, k_pair, v_pair, g_pair = qkv[:, cols], qkv[:, key_cols], qkv[:, value_cols], mixed[:, cols]
        k_turned = k_pair.T
        grad_keys = grad_values = None
        grad_queries = []
        for e in (0, 1):
            head = 2 * pair + e
            g_head = only(g_pair, e)
            asks = jnp.concatenate([only(q_pair, e), place_q[...]], axis=1)
            k_head = k_turned[e * 64 : (e + 1) * 64, :]
            across = None
            pieces = []
            for lo, hi in spans:
                low_share = chances[head, :, lo:hi]
                share = low_share.astype(FULL)
                weighed = share * dot_rows(v_pair, g_head[lo:hi, :])
                grad = (weighed - share * jnp.sum(weighed, axis=0, keepdims=True)).astype(LOW)
                pieces.append(dot(k_head, grad).astype(LOW).astype(FULL) * 0.125)
                part = dot(grad, asks[lo:hi, :])
                across = part if across is None else across + part
                part = dot(low_share, g_head[lo:hi, :])
                grad_values = part if grad_values is None else grad_values + part
            grad_keys = across[:, :128] if grad_keys is None else grad_keys + across[:, :128]
            grad_queries.append(jnp.concatenate(pieces, axis=1))
            marks = across[:, 128:]
            high = marks.astype(LOW)
            low = (marks - high.astype(FULL)).astype(LOW)
            pairs = dot(place_t[...], jnp.concatenate([high, low], axis=1))
            pairs = pairs[:, :128] + pairs[:, 128:]
            rows_part = jnp.where(lane64 < GRID, pairs[:GRID, :], 0.0)
            cols_part = jnp.where(lane64 >= GRID, pairs[GRID:, :], 0.0)
            rows_part = pltpu.roll(rows_part, 0, 1, stride=1, stride_axis=0)
            cols_part = pltpu.roll(cols_part, 64, 1, stride=1, stride_axis=0)
            for line, part in ((head, rows_part), (12 + head, cols_part)):
                spot = (line % 6) * 128
                small[0, 14 + line // 6 : 15 + line // 6, spot : spot + 128] = jnp.sum(part, axis=0, keepdims=True)
        grad_queries = jnp.concatenate(grad_queries, axis=0).T.astype(LOW)
        grad_values = grad_values.astype(LOW)
        qkv[:, cols] = grad_queries
        qkv[:, key_cols] = grad_keys.astype(LOW)
        qkv[:, value_cols] = grad_values
        small[0, 2:3, cols] = jnp.sum(grad_queries.astype(FULL), axis=0, keepdims=True)
        small[0, 3:4, cols] = jnp.sum(grad_values.astype(FULL), axis=0, keepdims=True)
        if pair == HEADS // 2 - 1:
            swaps.push(qkv.at[:, pl.ds(aligned(sibling * 1152, 128), 1152)], g_qkv_far, 7, net.sib)

    for pair in range(6):
        jobs["ab%d" % pair] = functools.partial(attend_back, pair)

    def grad_in(j, order):
        if (j, order) == (0, 0):
            swaps.landed(normed_a_t.at[1], 1)
            swaps.landed(g_qkv_far, 7)
        weight_grad(
            7 + j, order, rows_of(normed_a_t, 0), rows_of(normed_a_t, 1),
            qkv[:, pl.ds(aligned(c * 1152 + j * CHUNK, 128), CHUNK)], g_qkv_far[:, j * CHUNK : (j + 1) * CHUNK],
        )

    for j in range(3):
        for order in range(4):
            jobs["wi%d%d" % (j, order)] = functools.partial(grad_in, j, order)

    def grad_normed_a(j):
        cols = slice(j * CHUNK, (j + 1) * CHUNK)
        branch[:, cols] = dot_rows(qkv[...], w_in[cols, :])

    for j in range(2):
        jobs["gna%d" % j] = functools.partial(grad_normed_a, j)

    save_grad = pltpu.make_async_copy(work, input_grad_hbm, out_sem.at[0])
    save_out = pltpu.make_async_copy(mixed, outputs_hbm, out_sem.at[1])

    @job("fback")
    def _():
        def first_back(i, carry):
            gain_sum, shift_sum = carry
            rows = pl.ds(aligned(i * BLOCK, BLOCK), BLOCK)
            unit, inverse = normalised(tok[rows, :].astype(FULL))
            grad = branch[rows, :]
            gain_sum += fold(grad * unit)
            shift_sum += fold(grad)
            scaled = grad * first_gain[...]
            moved = scaled - jnp.mean(scaled, axis=-1, keepdims=True)
            moved -= unit * jnp.mean(scaled * unit, axis=-1, keepdims=True)
            work[rows, :] = work[rows, :] + inverse * moved
            return gain_sum, shift_sum

        for line, total in zip((0, 1), lax.fori_loop(0, SLOTS // BLOCK, first_back, (zero,) * 2)):
            small[0, line : line + 1, :] = jnp.sum(total, axis=0, keepdims=True)
        save_grad.start()

    def finish_rows(j):
        cols = slice(j * CHUNK, (j + 1) * CHUNK)
        returned = dot(act[...], w_reduce[:, cols]) + return_bias[:, cols]
        mixed[:, cols] = (middle[:, cols] + feed_scale[:, cols] * returned).astype(LOW)
        small[0, 13:14, cols] = jnp.sum(cot[:, cols].astype(FULL) * returned, axis=0, keepdims=True)
        if j == 1:
            save_out.start()

    for j in range(2):
        jobs["ret%d" % j] = functools.partial(finish_rows, j)

    for key in PLAN:
        jobs.pop(key)()
    assert not jobs, sorted(jobs)
    small_out[...] = small[5]
    saves = []
    for i, (stage, target) in enumerate(zip(stages, (g_in_hbm, g_out_hbm, g_expand_hbm, g_reduce_hbm))):
        saves.append(pltpu.make_async_copy(stage, target, out_sem.at[2 + i]))
        saves[-1].start()
    for group in gathers + scatters + [swaps, sums]:
        group.finish()
    for save in [save_grad, save_out] + saves:
        save.wait()


PLAN = (
    "g0own", "norm", "turn", "place", "g0r01", "g0r10", "g1own", "g0t0", "g0r11", "g1r01", "g0r20", "g0t1", "g1r10",
    "g1t0", "g2own", "g0r21", "g1r11", "g2r01", "g0t2", "g0r30", "g1t1", "g3own", "g1r20", "g2t0", "g2r10", "g3r01",
    "g0r31", "g1r21", "g4own", "g3t0", "g2r11", "g0t3", "g1t2", "g3r10", "g4r01", "g0all", "qkv0", "g1r30", "qkv1",
    "qkv2", "g2t1", "qkv3", "qkv4", "g2r20", "qkv5", "att0", "g4t0", "g3r11", "g5own", "att1", "g1r31", "att2",
    "g4r10", "g3t1", "att3", "g5r01", "att4", "g1t3", "g2r21", "att5", "g1all", "g3r20", "g4r11", "att6", "g2r30",
    "g5t0", "g2t2", "att7", "g3r21", "att8", "g4t1", "att9", "g5r10", "att10", "g3t2", "g4r20", "att11", "mix",
    "g2r31", "g5r11", "middle", "g3r30", "g4r21", "g3r31", "g2t3", "g5t1", "g5r20", "g2all", "hid0", "g4t2", "g4r30",
    "hid1", "g3t3", "hid2", "g5r21", "hid3", "g3all", "hid4", "g4r31", "g5r30", "hid5", "hid6", "hid7", "g5t2", "act",
    "g4t3", "g5r31", "g5t3", "wr00", "wr01", "g4all", "wr02", "g5all", "wr03", "wr10", "wr11", "wr12", "wr13", "ga0",
    "s0e0", "ga1", "ga2", "s0e1", "ga3", "ga4", "s0e2", "ga5", "ga6", "s0e3", "ga7", "s1e0", "gnb0", "gnb1", "sback",
    "gbl", "s0e4", "s1e1", "wo0", "wo1", "wo2", "wo3", "we00", "we01", "we02", "we03", "we10", "we11", "s6e0", "we12",
    "s6e1", "s0e5", "we13", "s6e2", "we20", "s6e3", "we21", "we22", "s2e0", "we23", "we30", "s1e2", "we31", "we32",
    "we33", "s0e6", "ab0", "s2e1", "s3e0", "s3e1", "s3e2", "s3e3", "s6e4", "ab1", "s0e7", "s1e3", "s4e0", "s2e2",
    "s0all", "s5e0", "s6e5", "ab2", "s3e4", "ab3", "s1e4", "s2e3", "s4e1", "ab4", "s1all", "s2e4", "s3e5", "s5e1",
    "s6e6", "ab5", "s2all", "s4e2", "s3e6", "gna0", "s5e2", "gna1", "s6e7", "wi00", "wi01", "wi02", "s4e3", "s6all",
    "wi03", "s3e7", "wi10", "wi11", "wi12", "s7e0", "s3all", "wi13", "s5e3", "wi20", "wi21", "wi22", "s4e4", "wi23",
    "fback", "s4all", "s8e0", "ret0", "s7e1", "s8e1", "s8e2", "s5e4", "s8e3", "s9e0", "ret1", "s5all", "sum", "s8e4",
    "s7e2", "sum0", "s9e1", "sum1", "s8e5", "s7e3", "sum2", "s9e2", "s7e4", "s8e6", "s7all", "sum3", "s9e3", "s8e7",
    "s8all", "s9e4", "sum4", "s9all",
)


def one_kernel(
    tokens, project_in, project_out, expand_weight, reduce_weight, first_gain, first_shift, query_value_bias,
    output_bias, mixer_scale, second_gain, second_shift, hidden_bias, return_bias, feed_scale, position_table,
    image_sizes, cotangent,
):
    vector = lambda v: v
    table = jnp.transpose(position_table[:, ::-1, :], (0, 2, 1)).reshape(24, 127)
    table = jnp.pad(table.astype(LOW).astype(FULL), ((0, 0), (0, 1)))
    anywhere = pl.BlockSpec(memory_space=pl.ANY)
    vmem = pl.BlockSpec(memory_space=pltpu.VMEM)
    low = lambda *shape: pltpu.VMEM(shape, LOW)
    full = lambda *shape: pltpu.VMEM(shape, FULL)
    dma = lambda *shape: pltpu.SemaphoreType.DMA(shape)
    like = jax.ShapeDtypeStruct
    scratch = [low(16 * w[0], w[1]) for w in WEIGHTS]
    scratch += [full(w[0], w[1]) for w in WEIGHTS]
    T, D, F = SLOTS, FEATURES, HIDDEN
    scratch += [
        low(T, D), low(T, D), low(T, D), low(2, D, T), low(2, D, T), low(2, D, T), low(T, 3 * D),
        low(T, 128), low(T, 128), low(128, T), low(HEADS, T, T), low(T, D), full(T, D), full(T, D),
        low(T, F), low(F, T), low(16, 96, T), low(T, F), low(T, D), low(T, D), low(T, F // 2),
        low(T, D // 2), low(T, 3 * D // 2), full(T, D), full(6, 24, D), full(5, 24, D),
        dma(len(PARTS) + 2), dma(6), dma(len(PARTS), 20), dma(len(PARTS), 20), dma(len(CHUNKS), 12), dma(len(CHUNKS), 12), dma(8), dma(8),
        dma(5), dma(5),
    ]
    for weight, _, order in CHUNKS:
        scratch += Scatter.shapes(weight, order)
    results = pl.pallas_call(
        layer_kernel,
        out_shape=[
            like((T, D), LOW), like((T, D), FULL), like((48, 3 * D), FULL), like((48, D), FULL), like((48, F), FULL),
            like((192, D), FULL), like((24, D), FULL),
        ],
        in_specs=[pl.BlockSpec(memory_space=pltpu.SMEM)] + [anywhere] * 6 + [vmem] * 11,
        out_specs=[anywhere] * 6 + [vmem],
        scratch_shapes=scratch,
        compiler_params=pltpu.CompilerParams(
            collective_id=0, has_side_effects=True, vmem_limit_bytes=VMEM_BYTES
        ),
    )(
        image_sizes, tokens, project_in, project_out, expand_weight, reduce_weight, cotangent, vector(first_gain),
        vector(first_shift), query_value_bias, vector(output_bias), vector(mixer_scale), vector(second_gain),
        vector(second_shift), vector(hidden_bias), vector(return_bias), vector(feed_scale), table,
    )
    vectors = [(D,), (D,), (2, D), (D,), (D,), (D,), (D,), (F,), (D,), (D,), (2, 2 * GRID - 1, HEADS)]
    return pl.pallas_call(
        handout,
        out_shape=[like(r.shape, r.dtype) for r in results[:6]] + [like(v, FULL) for v in vectors],
        in_specs=[anywhere] * 6 + [vmem],
        out_specs=[anywhere] * 6 + [vmem] * 11,
        scratch_shapes=[pltpu.VMEM(r.shape, r.dtype) for r in results[:6]] + [dma(2, 6)],
    )(*results)


def handout(*refs):
    large, small, saved, outs, held, sems = refs[:6], refs[6], refs[7:13], refs[13:24], refs[24:30], refs[30]
    loads = [pltpu.make_async_copy(large[i], held[i], sems.at[0, i]) for i in range(6)]
    copies = [pltpu.make_async_copy(held[i], saved[i], sems.at[1, i]) for i in range(6)]
    for load in loads:
        load.start()
    for load, copy in zip(loads, copies):
        load.wait()
        copy.start()
    for line, out in ((0, 0), (1, 1), (4, 3), (5, 4), (6, 5), (7, 6), (12, 8), (13, 9)):
        outs[out][...] = small[line, :]
    outs[2][...] = small[2:4, :]
    for k in range(4):
        outs[7][k * FEATURES : (k + 1) * FEATURES] = small[8 + k, :]
    for part in range(2):
        lines = [small[14 + n // 6 : 15 + n // 6, (n % 6) * 128 : (n % 6 + 1) * 128] for n in range(12 * part, 12 * part + 12)]
        turned = jnp.concatenate(lines + [jnp.zeros((4, 128), FULL)], axis=0).T
        outs[10][part] = turned[: 2 * GRID - 1, :HEADS]
    for copy in copies:
        copy.wait()


VMEM_BYTES = 64 * 2**20


def solution(mesh):
    placed = (
        P(("dp", "rep"), None),
        P("dp", None),
        P("dp", None),
        P("dp", None),
        P("dp", None),
        P(),
        P(),
        P(),
        P(),
        P(),
        P(),
        P(),
        P(),
        P(),
        P(),
        P(),
        P(("dp", "rep"), None),
        P(("dp", "rep"), None),
    )
    return jax.shard_map(
        one_kernel if tuple(mesh.shape.values()) == (16, 2) else shards,
        mesh=mesh,
        in_specs=placed,
        out_specs=(
            P(("dp", "rep"), None),
            P(("dp", "rep"), None),
            P("dp", None),
            P("dp", None),
            P("dp", None),
            P("dp", None),
            P(),
            P(),
            P(),
            P(),
            P(),
            P(),
            P(),
            P(),
            P(),
            P(),
            P(),
        ),
        check_vma=False,
    )
```

```python
import functools

import jax
import jax.numpy as jnp
from jax import lax
from jax.experimental import pallas as pl
from jax.experimental.pallas import tpu as pltpu
from jax.sharding import PartitionSpec as P

HEADS = 12
HEAD = 64
GRID = 64


EPS = 1e-06
MASKED = -1000000000.0


def layer_norm(values, gain, shift):
    centre = values - jnp.mean(values, axis=-1, keepdims=True)
    spread = jnp.mean(centre * centre, axis=-1, keepdims=True)
    return centre * lax.rsqrt(spread + EPS) * gain + shift


def gelu_exact(values):
    return jax.nn.gelu(values, approximate=False)


def shift_onehot(side):
    first_axis = lax.broadcasted_iota(jnp.int32, (side, side, 2 * side - 1), 0)
    second_axis = lax.broadcasted_iota(jnp.int32, (side, side, 2 * side - 1), 1)
    third_axis = lax.broadcasted_iota(jnp.int32, (side, side, 2 * side - 1), 2)
    return (first_axis - second_axis + side - 1 == third_axis).astype(jnp.float32)


def position_bias(shift_part, picks):
    between = jnp.einsum("tijh,tkj->tihk", shift_part, picks, preferred_element_type=jnp.float32)
    return jnp.einsum(
        "tqi,tihk->hqk", picks, between.astype(jnp.bfloat16), preferred_element_type=jnp.float32
    )


def group_scores(query_part, key_part, shift_part, picks, usable):
    scores = jnp.einsum("qhd,khd->hqk", query_part, key_part, preferred_element_type=jnp.float32)
    scores = scores + position_bias(shift_part, picks)
    return jnp.where(usable[None, None, :], scores, MASKED)


def attend_group(packed, picks, usable):
    query_part, key_part, value_part, shift_part = packed
    scores = group_scores(query_part, key_part, shift_part, picks, usable)
    highest = jnp.max(scores, axis=-1, keepdims=True)
    weights_raw = jnp.exp(scores - highest)
    totals = jnp.sum(weights_raw, axis=-1, keepdims=True)
    chances = (weights_raw / totals).astype(jnp.bfloat16)
    blended = jnp.einsum("hqk,khd->qhd", chances, value_part, preferred_element_type=jnp.float32)
    return (blended.astype(jnp.bfloat16), (highest + jnp.log(totals))[..., 0])


def attend_back(packed, picks, usable):
    query_part, key_part, value_part, grad_part, logsums, shift_part = packed
    scores = group_scores(query_part, key_part, shift_part, picks, usable)
    chances = jnp.exp(scores - logsums[..., None])
    grad_chance = jnp.einsum(
        "qhd,khd->hqk", grad_part, value_part, preferred_element_type=jnp.float32
    )
    row_dot = jnp.sum(chances * grad_chance, axis=-1, keepdims=True)
    grad_scores = (chances * (grad_chance - row_dot)).astype(jnp.bfloat16)
    grad_query = jnp.einsum(
        "hqk,khd->qhd", grad_scores, key_part, preferred_element_type=jnp.float32
    )
    grad_key = jnp.einsum(
        "hqk,qhd->khd", grad_scores, query_part, preferred_element_type=jnp.float32
    )
    grad_value = jnp.einsum(
        "hqk,qhd->khd", chances.astype(jnp.bfloat16), grad_part, preferred_element_type=jnp.float32
    )
    across = jnp.einsum("hqk,tkj->thqj", grad_scores, picks, preferred_element_type=jnp.float32)
    grad_shift = jnp.einsum(
        "tqi,thqj->tijh", picks.astype(jnp.float32), across, precision=lax.Precision.HIGHEST
    )
    return (
        grad_query.astype(jnp.bfloat16),
        grad_key.astype(jnp.bfloat16),
        grad_value.astype(jnp.bfloat16),
        grad_shift,
    )


def shards(
    tokens,
    project_in,
    project_out,
    expand_weight,
    reduce_weight,
    first_gain,
    first_shift,
    query_value_bias,
    output_bias,
    mixer_scale,
    second_gain,
    second_shift,
    hidden_bias,
    return_bias,
    feed_scale,
    position_table,
    image_sizes,
    cotangent,
):
    length = tokens.shape[0]
    width_model = tokens.shape[1]
    head_count = HEADS
    per_group = 4
    groups = head_count // per_group
    full_in, full_out, full_expand, full_reduce = (
        lax.all_gather(project_in, "dp", axis=0, tiled=True),
        lax.all_gather(project_out, "dp", axis=0, tiled=True),
        lax.all_gather(expand_weight, "dp", axis=0, tiled=True),
        lax.all_gather(reduce_weight, "dp", axis=0, tiled=True),
    )
    inputs = tokens.astype(jnp.float32)
    normed_a, first_back = jax.vjp(layer_norm, inputs, first_gain, first_shift)
    normed_a_low = normed_a.astype(jnp.bfloat16)
    projected = jnp.dot(normed_a_low, full_in, preferred_element_type=jnp.float32)
    queries = ((projected[:, :width_model] + query_value_bias[0]) * HEAD ** (-0.5)).astype(
        jnp.bfloat16
    )
    keys_low = projected[:, width_model : 2 * width_model].astype(jnp.bfloat16)
    values_low = (projected[:, 2 * width_model :] + query_value_bias[1]).astype(jnp.bfloat16)
    shift_table = shift_onehot(GRID)
    shifts = jnp.einsum(
        "ija,tah->tijh",
        shift_table.astype(jnp.bfloat16),
        position_table.astype(jnp.bfloat16),
        preferred_element_type=jnp.float32,
    ).astype(jnp.bfloat16)
    shifts_grouped = shifts.reshape(2, GRID, GRID, groups, per_group).transpose(3, 0, 1, 2, 4)
    places = jnp.arange(length, dtype=jnp.int32)
    height = image_sizes[0, 0]
    width_image = image_sizes[0, 1]
    grid_iota = jnp.arange(GRID, dtype=jnp.int32)
    picks = jnp.stack(
        [
            (places // width_image)[:, None] == grid_iota[None, :],
            (places % width_image)[:, None] == grid_iota[None, :],
        ]
    ).astype(jnp.bfloat16)
    usable = places < height * width_image

    def split_heads(matrix):
        return matrix.reshape(length, groups, per_group, HEAD).transpose(1, 0, 2, 3)

    def join_heads(blocks):
        return blocks.transpose(1, 0, 2, 3).reshape(length, width_model)

    query_groups = split_heads(queries)
    key_groups = split_heads(keys_low)
    value_groups = split_heads(values_low)
    blended_groups, logsums = lax.map(
        lambda packed: attend_group(packed, picks, usable),
        (query_groups, key_groups, value_groups, shifts_grouped),
    )
    blended = join_heads(blended_groups)
    branch = jnp.dot(blended, full_out, preferred_element_type=jnp.float32) + output_bias
    middle = inputs + mixer_scale * branch
    normed_b, second_back = jax.vjp(layer_norm, middle, second_gain, second_shift)
    normed_b_low = normed_b.astype(jnp.bfloat16)
    preact = jnp.dot(normed_b_low, full_expand, preferred_element_type=jnp.float32) + hidden_bias
    activated, gelu_back = jax.vjp(gelu_exact, preact)
    activated_low = activated.astype(jnp.bfloat16)
    returned = jnp.dot(activated_low, full_reduce, preferred_element_type=jnp.float32) + return_bias
    outputs = middle + feed_scale * returned
    back_in, back_out, back_expand, back_reduce = (
        lax.all_gather(project_in, "dp", axis=0, tiled=True),
        lax.all_gather(project_out, "dp", axis=0, tiled=True),
        lax.all_gather(expand_weight, "dp", axis=0, tiled=True),
        lax.all_gather(reduce_weight, "dp", axis=0, tiled=True),
    )
    upstream = cotangent.astype(jnp.float32)
    grad_feed_scale = jnp.sum(upstream * returned, axis=0)
    grad_returned = (upstream * feed_scale).astype(jnp.bfloat16)
    grad_return_bias = jnp.sum(grad_returned.astype(jnp.float32), axis=0)
    grad_reduce = jnp.einsum(
        "tf,td->fd", activated_low, grad_returned, preferred_element_type=jnp.float32
    )
    grad_activated = jnp.einsum(
        "td,fd->tf", grad_returned, back_reduce, preferred_element_type=jnp.float32
    )
    grad_preact = gelu_back(grad_activated)[0].astype(jnp.bfloat16)
    grad_hidden_bias = jnp.sum(grad_preact.astype(jnp.float32), axis=0)
    grad_expand = jnp.einsum(
        "td,tf->df", normed_b_low, grad_preact, preferred_element_type=jnp.float32
    )
    grad_normed_b = jnp.einsum(
        "tf,df->td", grad_preact, back_expand, preferred_element_type=jnp.float32
    )
    grad_from_norm, grad_second_gain, grad_second_shift = second_back(grad_normed_b)
    grad_middle = upstream + grad_from_norm
    grad_mixer_scale = jnp.sum(grad_middle * branch, axis=0)
    grad_branch = (grad_middle * mixer_scale).astype(jnp.bfloat16)
    grad_output_bias = jnp.sum(grad_branch.astype(jnp.float32), axis=0)
    grad_project_out = jnp.einsum(
        "td,te->de", blended, grad_branch, preferred_element_type=jnp.float32
    )
    grad_blended = jnp.einsum(
        "te,de->td", grad_branch, back_out, preferred_element_type=jnp.float32
    ).astype(jnp.bfloat16)
    grad_query_groups, grad_key_groups, grad_value_groups, grad_shift_groups = lax.map(
        lambda packed: attend_back(packed, picks, usable),
        (
            query_groups,
            key_groups,
            value_groups,
            split_heads(grad_blended),
            logsums,
            shifts_grouped,
        ),
    )
    grad_queries = join_heads(grad_query_groups) * HEAD ** (-0.5)
    grad_keys = join_heads(grad_key_groups)
    grad_values = join_heads(grad_value_groups)
    grad_projected = jnp.concatenate([grad_queries, grad_keys, grad_values], axis=1)
    grad_query_value_bias = jnp.stack(
        [
            jnp.sum(grad_queries.astype(jnp.float32), axis=0),
            jnp.sum(grad_values.astype(jnp.float32), axis=0),
        ]
    )
    grad_project_in = jnp.einsum(
        "td,te->de", normed_a_low, grad_projected, preferred_element_type=jnp.float32
    )
    grad_normed_a = jnp.einsum(
        "te,de->td", grad_projected, back_in, preferred_element_type=jnp.float32
    )
    grad_from_first, grad_first_gain, grad_first_shift = first_back(grad_normed_a)
    input_grad = grad_middle + grad_from_first
    grad_shift = grad_shift_groups.transpose(1, 2, 3, 0, 4).reshape(2, GRID, GRID, head_count)
    grad_position_table = jnp.einsum(
        "ija,tijh->tah", shift_table, grad_shift, precision=lax.Precision.HIGHEST
    )
    weight_grads = (
        lax.psum_scatter(grad_project_in, "dp", scatter_dimension=0, tiled=True),
        lax.psum_scatter(grad_project_out, "dp", scatter_dimension=0, tiled=True),
        lax.psum_scatter(grad_expand, "dp", scatter_dimension=0, tiled=True),
        lax.psum_scatter(grad_reduce, "dp", scatter_dimension=0, tiled=True),
    )
    weight_grads = lax.psum(
        (weight_grads[0], weight_grads[1], weight_grads[2], weight_grads[3]), "rep"
    )
    small_sums = lax.psum(
        (
            grad_first_gain,
            grad_first_shift,
            grad_query_value_bias,
            grad_output_bias,
            grad_mixer_scale,
            grad_second_gain,
            grad_second_shift,
            grad_hidden_bias,
            grad_return_bias,
            grad_feed_scale,
            grad_position_table,
        ),
        ("dp", "rep"),
    )
    return (
        outputs.astype(jnp.bfloat16),
        input_grad,
        weight_grads[0],
        weight_grads[1],
        weight_grads[2],
        weight_grads[3],
        small_sums[0],
        small_sums[1],
        small_sums[2],
        small_sums[3],
        small_sums[4],
        small_sums[5],
        small_sums[6],
        small_sums[7],
        small_sums[8],
        small_sums[9],
        small_sums[10],
    )


FEATURES = 768
HIDDEN = 3072
SLOTS = 448
MESH = pl.DeviceIdType.MESH
LOW = jnp.bfloat16
FULL = jnp.float32

W_IN = (48, 2304, False, "A")
W_OUT = (48, 768, False, "A")
W_EXPAND = (48, 3072, False, "A")
W_REDUCE = (192, 768, True, "B")
WEIGHTS = (W_IN, W_OUT, W_EXPAND, W_REDUCE)

PARTS = ((0, 0, 1, "A"), (1, 0, 1, "A"), (2, 0, 2, "A"), (2, 1, 2, "A"), (3, 0, 2, "B"), (3, 1, 2, "B"))

CHUNK = 384
CHUNKS = (
    (3, 0, "B"), (3, 1, "A"),
    (2, 0, "A"), (2, 1, "B"), (2, 2, "A"), (2, 3, "A"),
    (1, 0, "B"),
    (0, 0, "A"), (0, 1, "B"), (0, 2, "A"),
)
IN_COLUMNS = ((0, 4), (2, 3), (1, 5))


def aligned(index, step):
    return pl.multiple_of(index, step)


class Net:
    def __init__(self):
        dp, c = lax.axis_index("dp"), lax.axis_index("rep")
        z, y, x = dp // 4, lax.rem(dp // 2, 2), lax.rem(dp, 2)
        self.dp, self.c, self.z, self.y, self.x = dp, c, z, y, x
        self.ma = y * (1 - c) + x * c
        self.mb = x * (1 - c) + y * c
        self.wa, self.wb = 2 - c, 1 + c
        self.to_a = (dp + self.wa * (1 - 2 * self.ma), c)
        self.to_b = (dp + self.wb * (1 - 2 * self.mb), c)
        self.to_z = (lax.rem(dp + 4, 16), c)
        self.from_z = (lax.rem(dp + 12, 16), c)
        self.far_z = (lax.rem(dp + 8, 16), c)
        self.sib = (dp, 1 - c)

    def barrier(self):
        sem = pltpu.get_barrier_semaphore()
        for target in (self.to_a, self.to_b, self.to_z, self.from_z, self.far_z, self.sib):
            pl.semaphore_signal(sem, inc=1, device_id=target, device_id_type=MESH)
        pl.semaphore_wait(sem, 6)

    def back(self, steps):
        return lax.rem(self.z + 4 - steps, 4)

    def owner(self, z, a, b):
        return 4 * z + self.wa * a + self.wb * b


class Transfers:
    def __init__(self, net, send, recv):
        self.net, self.send, self.recv, self.sent = net, send, recv, []
        self.waited = 0

    def push(self, src, dst, slot, to):
        copy = pltpu.make_async_remote_copy(
            src, dst, self.send.at[len(self.sent)], self.recv.at[slot], device_id=to, device_id_type=MESH
        )
        copy.start()
        self.sent.append(copy)

    def landed(self, dst, slot):
        pltpu.make_async_remote_copy(
            dst, dst, self.send.at[0], self.recv.at[slot], device_id=self.net.sib, device_id_type=MESH
        ).wait_recv()

    def finish(self):
        for copy in self.sent[self.waited :]:
            copy.wait_send()


class Gather(Transfers):
    def __init__(self, net, part, buf, send, recv):
        super().__init__(net, send, recv)
        weight, self.part, self.parts, self.order = part
        self.buf = buf
        self.rows, self.cols, self.by_rows, _ = WEIGHTS[weight]

    def span(self, c):
        half = (self.rows if self.by_rows else self.cols) // 2
        size = half // self.parts
        return c * half + self.part * size, size

    def block(self, owner):
        start, size = self.span(self.net.c)
        if self.by_rows:
            return self.buf.at[pl.ds(aligned(owner * self.rows + start, 16), size), :]
        return self.buf.at[pl.ds(aligned(owner * self.rows, 16), self.rows), pl.ds(aligned(start, 128), size)]

    def group(self, z, c):
        start, size = self.span(c)
        if self.by_rows:
            pieces = self.rows // size
            return self.buf.reshape(4, 4, pieces, size, self.cols).at[z, :, c * self.parts + self.part]
        rows = 4 * self.rows
        return self.buf.at[pl.ds(aligned(z * rows, 16), rows), pl.ds(aligned(start, 128), size)]

    def load(self, src, sem):
        start, size = self.span(self.net.c)
        if self.by_rows:
            part = src.at[pl.ds(aligned(start, 16), size), :]
        else:
            part = src.at[:, pl.ds(aligned(start, 128), size)]
        self.copy = pltpu.make_async_copy(part, self.block(self.net.dp), sem)
        self.copy.start()

    def along_z(self, ref, back, other):
        net = self.net
        if back == 0:
            self.push(ref, ref, 2 + other, net.to_z)
            self.push(ref, ref, 6 + other, net.from_z)
        elif back == 1:
            self.push(ref, ref, 4 + other, net.to_z)

    def jobs(self):
        net = self.net
        ma, mb = net.ma, net.mb

        def near(back, other):
            return self.block(net.owner(net.back(back), ma, mb + other * (1 - 2 * mb)))

        def far(back, other):
            return self.block(net.owner(net.back(back), 1 - ma, mb + other * (1 - 2 * mb)))

        def own():
            self.copy.wait()
            ref = near(0, 0)
            self.along_z(ref, 0, 0)
            self.push(ref, ref, 1, net.to_b)
            self.push(ref, ref, 8, net.to_a)

        def relay(back, other):
            def run():
                ref = near(back, other)
                self.landed(ref, back * 2 + other)
                if other == 0 or self.order != "B":
                    self.along_z(ref, back, other)
                if self.order == "B" and other == 0:
                    self.push(ref, ref, back * 2 + 1, net.to_b)
                self.push(ref, ref, 8 + back * 2 + other, net.to_a)

            return run

        def tail(back):
            def run():
                for other in (0, 1):
                    self.landed(far(back, other), 8 + back * 2 + other)
                ref = self.group(net.back(back), net.c)
                self.push(ref, ref, 16 + back, net.sib)

            return run

        def complete():
            for back in range(4):
                self.landed(self.group(net.back(back), 1 - net.c), 16 + back)

        relays = [relay(0, 1)] + [relay(back, other) for back in (1, 3, 2) for other in (0, 1)]
        return [own, *relays, *[tail(back) for back in (0, 1, 3, 2)], complete]


STEPS = (2, 1, 3, 0)


class Scatter(Transfers):
    def __init__(self, net, weight, column, order, refs, stage, send, recv):
        super().__init__(net, send, recv)
        self.order = order
        self.rows, self.cols, self.by_rows, _ = WEIGHTS[weight]
        self.g, self.ra, self.rb, self.rz = refs
        self.stage, self.column = stage, column
        self.rh = self.rows // 2 if self.by_rows else self.rows

    def produced(self, back):
        net = self.net
        self.push(self.g.at[net.back(back), 1 - net.ma], self.ra.at[back], back, net.to_a)

    def along_z(self, step, src):
        net = self.net
        self.push(src, self.rz.at[step], 8 + step, net.from_z if step == 1 else net.to_z)

    def add_into(self, dst, terms):
        total = dst[...].astype(FULL)
        for term in terms:
            total += term[...].astype(FULL)
        dst[...] = total.astype(LOW)

    def part_of_stage(self, c):
        if self.by_rows:
            return self.stage.at[pl.ds(aligned(c * self.rh, 16), self.rh), pl.ds(self.column * CHUNK, CHUNK)]
        return self.stage.at[:, pl.ds(aligned(self.first_column(c), 128), CHUNK)]

    def first_column(self, c):
        if self.cols == 3 * FEATURES:
            first, second = IN_COLUMNS[self.column]
            return (first + c * (second - first)) * CHUNK
        return c * (self.cols // 2) + self.column * CHUNK

    def last(self, terms):
        mine = self.part_of_stage(self.net.c)
        total = terms[0][...].astype(FULL)
        for term in terms[1:]:
            total += term[...].astype(FULL)
        mine[...] = total
        self.push(mine, mine, 11, self.net.sib)

    def got(self):
        self.landed(self.part_of_stage(1 - self.net.c), 11)

    def jobs(self):
        net, g, ra, rb, rz = self.net, self.g, self.ra, self.rb, self.rz
        ma, mb = net.ma, net.mb

        def step_a(s):
            def run():
                back = STEPS[s]
                self.landed(ra.at[back], back)
                terms = [ra.at[back]]
                for k in ((), (), (0,), (1, 2))[s]:
                    self.landed(rz.at[k], 8 + k)
                    terms.append(rz.at[k])
                dst = g.at[net.back(back), ma]
                self.add_into(dst, terms)
                if s < 3:
                    self.along_z(s, dst)
                else:
                    self.push(dst.at[1 - mb], rb.at[0], 4, net.to_b)

            return run

        def final_a():
            self.landed(rb.at[0], 4)
            self.last([g.at[net.z, ma, mb], rb.at[0]])

        def first_b(back):
            def run():
                self.landed(ra.at[back], back)
                dst = g.at[net.back(back), ma]
                self.add_into(dst, [ra.at[back]])
                self.push(dst.at[1 - mb], rb.at[back], 4 + back, net.to_b)

            return run

        def step_b(s):
            def run():
                back = STEPS[s]
                self.landed(rb.at[back], 4 + back)
                terms = [rb.at[back]]
                for k in ((), (), (0,), (1, 2))[s]:
                    self.landed(rz.at[k], 8 + k)
                    terms.append(rz.at[k])
                dst = g.at[net.back(back), ma, mb]
                if s < 3:
                    self.add_into(dst, terms)
                    self.along_z(s, dst)
                else:
                    self.last([dst] + terms)

            return run

        if self.order == "A":
            steps = [step_a(s) for s in range(4)] + [final_a]
        else:
            steps = [first_b(back) for back in STEPS] + [step_b(s) for s in range(4)]
        return steps + [self.got]

    @staticmethod
    def shapes(weight, order):
        rows, _, by_rows, _ = WEIGHTS[weight]
        block = (rows // 2 if by_rows else rows, CHUNK)
        relay = (3,) if order == "B" else (3, 2)
        return [
            pltpu.VMEM((4, 2, 2) + block, LOW),
            pltpu.VMEM((4, 2) + block, LOW),
            pltpu.VMEM((4 if order == "B" else 1,) + block, LOW),
            pltpu.VMEM(relay + block, LOW),
        ]


class SmallSum(Transfers):
    def __init__(self, net, buf, landing, send, recv):
        super().__init__(net, send, recv)
        self.buf, self.landing = buf, landing
        place, z = lax.rem(net.dp, 4), net.z
        near_z = z + 1 - 2 * lax.rem(z, 2)
        self.partners = [
            net.sib,
            (net.dp + 1 - 2 * net.x, net.c),
            (net.dp + 2 - 4 * net.y, net.c),
            (near_z * 4 + place, net.c),
            net.far_z,
        ]

    def jobs(self):
        def start(i):
            def run():
                self.push(self.buf.at[i], self.landing.at[i], i, self.partners[i])

            return run

        def add(i):
            def run():
                self.landed(self.landing.at[i], i)
                self.buf[i + 1] = self.buf[i] + self.landing[i]
                if i < 4:
                    start(i + 1)()

            return run

        return [start(0)] + [add(i) for i in range(5)]


def dot(left, right):
    return jnp.dot(left, right, preferred_element_type=FULL)


def dot_rows(left, right):
    return lax.dot_general(left, right, (((1,), (1,)), ((), ())), preferred_element_type=FULL)


def fold(values):
    return jnp.sum(values.reshape(values.shape[0] // 8, 8, values.shape[1]), axis=0)


def normalised(values):
    centre = values - jnp.mean(values, axis=-1, keepdims=True)
    inverse = lax.rsqrt(jnp.mean(centre * centre, axis=-1, keepdims=True) + EPS)
    return centre * inverse, inverse


BLOCK = 64
ROOT_HALF = 0.7071067811865476
DENSITY = 0.3989422804014327


class Line:
    def __init__(self, ref):
        self.ref = ref

    def __getitem__(self, index):
        cols = slice(None) if index is Ellipsis else index[1]
        return self.ref[cols].reshape(1, -1)


def layer_kernel(
    sizes, tokens_hbm, w_in_hbm, w_out_hbm, w_expand_hbm, w_reduce_hbm, cotangent_hbm,
    first_gain, first_shift, query_value_bias, output_bias, mixer_scale, second_gain, second_shift,
    hidden_bias, return_bias, feed_scale, position_table,
    outputs_hbm, input_grad_hbm, g_in_hbm, g_out_hbm, g_expand_hbm, g_reduce_hbm, small_out,
    w_in, w_out, w_expand, w_reduce,
    stage_in, stage_out, stage_expand, stage_reduce,
    tok, cot, normed_a_t, normed_b_t, blended_t, qkv, place_q, place_k, place_t,
    chances, mixed, branch, middle, act, act_t, act_t_far, slope, g_ret, g_ret_far, g_pre_far,
    g_branch_far, g_qkv_far, work, small, small_landing, table,
    load_sem, out_sem, gather_send, gather_recv, scatter_send, scatter_recv, swap_send, swap_recv,
    small_send, small_recv, *scatter_refs,
):
    net = Net()
    first_gain, first_shift, output_bias, mixer_scale, second_gain, second_shift, hidden_bias, return_bias, feed_scale = map(
        Line,
        (first_gain, first_shift, output_bias, mixer_scale, second_gain, second_shift, hidden_bias, return_bias, feed_scale),
    )
    g_branch = g_ret
    normed = mixed
    c = net.c
    sibling = 1 - c

    weights = [w_in, w_out, w_expand, w_reduce]
    sources = [w_in_hbm, w_out_hbm, w_expand_hbm, w_reduce_hbm]
    jobs = []

    gathers = []
    for i, part in enumerate(PARTS):
        gather = Gather(net, part, weights[part[0]], gather_send.at[i], gather_recv.at[i])
        gather.load(sources[part[0]], load_sem.at[i])
        gathers.append(gather)
        jobs += gather.jobs()
    load_tok = pltpu.make_async_copy(tokens_hbm, tok, load_sem.at[len(PARTS)])
    load_cot = pltpu.make_async_copy(cotangent_hbm, cot, load_sem.at[len(PARTS) + 1])
    load_tok.start()
    load_cot.start()
    net.barrier()

    stages = [stage_in, stage_out, stage_expand, stage_reduce]
    scatters = []
    for i, (weight, column, order) in enumerate(CHUNKS):
        scatters.append(
            Scatter(net, weight, column, order, scatter_refs[4 * i : 4 * i + 4], stages[weight],
                    scatter_send.at[i], scatter_recv.at[i])
        )
    swaps = Transfers(net, swap_send, swap_recv)
    sums = SmallSum(net, small, small_landing, small_send, small_recv)
    for group in scatters + [sums]:
        jobs += group.jobs()

    @jobs.append
    def _():
        load_tok.wait()
        load_cot.wait()

        def first_rows(i, carry):
            rows = pl.ds(aligned(i * BLOCK, BLOCK), BLOCK)
            unit, _ = normalised(tok[rows, :].astype(FULL))
            normed[rows, :] = (unit * first_gain[...] + first_shift[...]).astype(LOW)
            returned_grad = (cot[rows, :].astype(FULL) * feed_scale[...]).astype(LOW)
            g_ret[rows, :] = returned_grad
            return carry + fold(returned_grad.astype(FULL))

        total = lax.fori_loop(0, SLOTS // BLOCK, first_rows, jnp.zeros((8, FEATURES), FULL), unroll=True)
        small[0] = jnp.zeros_like(small[0])
        small[0, 12:13, :] = jnp.sum(total, axis=0, keepdims=True)
        swaps.push(g_ret, g_ret_far, 0, net.sib)

    def turn(source, target):
        for j in range(FEATURES // 128):
            target[0, j * 128 : (j + 1) * 128, :] = source[:, j * 128 : (j + 1) * 128].T

    @jobs.append
    def _():
        turn(normed, normed_a_t)
        swaps.push(normed_a_t.at[0], normed_a_t.at[1], 1, net.sib)

    lane128 = lax.broadcasted_iota(jnp.int32, (128, 128), 1)
    row128 = lax.broadcasted_iota(jnp.int32, (128, 128), 0)
    height, width = sizes[0, 0], sizes[0, 1]
    width_f = width.astype(FULL)
    live = (height * width).astype(FULL)

    def grid_place(slot):
        row = jnp.floor((slot + 0.5) / width_f)
        return row, slot - row * width_f

    @jobs.append
    def _():
        slot = lax.broadcasted_iota(jnp.int32, (SLOTS, 128), 0).astype(FULL)
        lane = lax.broadcasted_iota(jnp.int32, (SLOTS, 128), 1).astype(FULL)
        row, col = grid_place(slot)
        hit = jnp.where(jnp.where(lane < GRID, row, col + GRID) == lane, 1.0, 0.0)
        place_q[...] = hit.astype(LOW)
        place_k[...] = jnp.where(slot < live, hit, jnp.where(lane == GRID - 1, 1.0, 0.0)).astype(LOW)
        slot = lax.broadcasted_iota(jnp.int32, (128, SLOTS), 1).astype(FULL)
        lane = lax.broadcasted_iota(jnp.int32, (128, SLOTS), 0).astype(FULL)
        row, col = grid_place(slot)
        hit = jnp.where(lane < GRID, GRID - 1 - row, 2 * GRID - 1 - col) == lane
        place_t[...] = jnp.where(hit, 1.0, 0.0).astype(LOW)
        mirror = jnp.where(row128 + lane128 == 2 * GRID - 2, 1.0, 0.0).astype(LOW)
        for part in range(2):
            low_table = position_table[:, part, :].astype(LOW)
            table[12 * part : 12 * part + 12, :] = dot(low_table, mirror[: 2 * GRID - 1, :])

    def project(j):
        cols = slice(j * CHUNK, (j + 1) * CHUNK)
        part = dot(normed[...], w_in[:, cols])
        inner = slice((j % 2) * CHUNK, (j % 2 + 1) * CHUNK)
        if j < 2:
            part = (part + query_value_bias[0:1, inner]) * 0.125
        elif j >= 4:
            part = part + query_value_bias[1:2, inner]
        qkv[:, cols] = part.astype(LOW)

    for j in range(6):
        jobs.append(functools.partial(project, j))

    half_lane = lax.broadcasted_iota(jnp.int32, (SLOTS, 128), 1)
    no_key = (lane128 == GRID - 1) & (row128 < GRID) & (jnp.full((128, 128), live) < SLOTS)
    spans = ((0, 256), (256, SLOTS))

    def only(values, e):
        keep = half_lane < 64 if e == 0 else half_lane >= 64
        return jnp.where(keep, values, jnp.zeros_like(values))

    def bias_table(head):
        rows_part = jnp.broadcast_to(table[head : head + 1, :], (GRID, 128))
        cols_part = jnp.broadcast_to(table[12 + head : 13 + head, :], (GRID, 128))
        both = jnp.concatenate(
            [
                pltpu.roll(rows_part, 65, 1, stride=1, stride_axis=0),
                pltpu.roll(cols_part, 1, 1, stride=1, stride_axis=0),
            ],
            axis=0,
        )
        both = jnp.where(lane128 // GRID == row128 // GRID, both, 0.0)
        return jnp.where(no_key, MASKED, both).astype(LOW)

    def attend(head):
        pair, e = head // 2, head % 2
        cols = slice(pair * 128, (pair + 1) * 128)
        keys = jnp.concatenate([qkv[:, 768 + pair * 128 : 896 + pair * 128], place_k[...]], axis=1)
        v_head = qkv[:, 1536 + pair * 128 : 1664 + pair * 128].T[e * 64 : (e + 1) * 64, :]
        bias = dot(place_q[...], bias_table(head)).astype(LOW)
        asks = jnp.concatenate([only(qkv[:, cols], e), bias], axis=1)
        for lo, hi in spans:
            scores = dot_rows(keys, asks[lo:hi, :])
            raised = jnp.exp(scores - jnp.max(scores, axis=0, keepdims=True))
            share = (raised * (1.0 / jnp.sum(raised, axis=0, keepdims=True))).astype(LOW)
            chances[head, :, lo:hi] = share
            blended_t[0, head * 64 : (head + 1) * 64, lo:hi] = dot(v_head, share).astype(LOW)
        if e == 1:
            mixed[:, cols] = blended_t[0, cols, :].T
        if head == HEADS - 1:
            swaps.push(blended_t.at[0], blended_t.at[1], 2, net.sib)

    for head in range(HEADS):
        jobs.append(functools.partial(attend, head))

    @jobs.append
    def _():
        for j in range(2):
            cols = slice(j * CHUNK, (j + 1) * CHUNK)
            branch[:, cols] = dot(mixed[...], w_out[:, cols]) + output_bias[:, cols]

    @jobs.append
    def _():
        def middle_rows(i, carry):
            rows = pl.ds(aligned(i * BLOCK, BLOCK), BLOCK)
            mid = tok[rows, :].astype(FULL) + mixer_scale[...] * branch[rows, :]
            middle[rows, :] = mid
            unit, _ = normalised(mid)
            normed[rows, :] = (unit * second_gain[...] + second_shift[...]).astype(LOW)
            return carry

        lax.fori_loop(0, SLOTS // BLOCK, middle_rows, 0, unroll=True)
        turn(normed, normed_b_t)
        swaps.push(normed_b_t.at[0], normed_b_t.at[1], 3, net.sib)

    act_blocks = act_t.reshape(16, 2, 96, SLOTS)

    def hidden(j):
        cols = slice(j * CHUNK, (j + 1) * CHUNK)
        pre = dot(normed[...], w_expand[:, cols]) + hidden_bias[:, cols]
        share = 0.5 + 0.5 * lax.erf(pre * ROOT_HALF)
        active = (pre * share).astype(LOW)
        act[:, cols] = active
        slope[:, cols] = (share + pre * (DENSITY * jnp.exp(-0.5 * pre * pre))).astype(LOW)
        for k in range(3):
            act_t[j * CHUNK + k * 128 : j * CHUNK + (k + 1) * 128, :] = active[:, k * 128 : (k + 1) * 128].T

    for i, j in enumerate((0, 1, 4, 5, 2, 3, 6, 7)):
        jobs.append(functools.partial(hidden, j))

    @jobs.append
    def _():
        swaps.push(act_blocks.at[:, sibling], act_t_far, 4, net.sib)

    def place_of(owner):
        oy, ox = owner // 2, owner % 2
        return oy * (1 - c) + ox * c, ox * (1 - c) + oy * c

    def weight_grad(index, order, left, left_far, right, right_far):
        scatter = scatters[index]
        back = STEPS[order]
        z = net.back(back)
        tile = (dot(left(z), right) + dot(left_far(z), right_far)).astype(LOW)
        for owner in range(4):
            pa, pb = place_of(owner)
            scatter.g[z, pa, pb] = tile[owner * scatter.rh : (owner + 1) * scatter.rh, :]
        scatter.produced(back)

    def rows_of(ref, slot):
        return lambda z: ref[slot, pl.ds(aligned(z * 192, 64), 192), :]

    def grad_reduce(j, order):
        cols = slice(j * CHUNK, (j + 1) * CHUNK)
        if (j, order) == (0, 0):
            swaps.landed(g_ret_far, 0)
            swaps.landed(act_t_far, 4)
        weight_grad(
            j, order,
            lambda z: act_blocks[pl.ds(4 * z, 4), c].reshape(384, SLOTS),
            lambda z: act_t_far[pl.ds(4 * z, 4)].reshape(384, SLOTS),
            g_ret[:, cols], g_ret_far[:, cols],
        )

    for j in range(2):
        for order in range(4):
            jobs.append(functools.partial(grad_reduce, j, order))

    def grad_hidden(j):
        half = sibling if j < 4 else c
        cols = pl.ds(aligned(half * 1536 + (j % 4) * CHUNK, 128), CHUNK)
        part = (dot_rows(g_ret[...], w_reduce[cols, :]) * slope[:, cols].astype(FULL)).astype(LOW)
        slope[:, cols] = part
        summed = jnp.sum(part.astype(FULL), axis=0, keepdims=True)
        small[0, pl.ds(8 + 2 * half + (j % 4) // 2, 1), (j % 2) * CHUNK : (j % 2 + 1) * CHUNK] = summed
        if j == 3:
            swaps.push(slope.at[:, pl.ds(aligned(sibling * 1536, 128), 1536)], g_pre_far, 5, net.sib)

    for j in range(8):
        jobs.append(functools.partial(grad_hidden, j))

    def grad_expand(j, order):
        if (j, order) == (0, 0):
            swaps.landed(normed_b_t.at[1], 3)
            swaps.landed(g_pre_far, 5)
        weight_grad(
            2 + j, order, rows_of(normed_b_t, 0), rows_of(normed_b_t, 1),
            slope[:, pl.ds(aligned(c * 1536 + j * CHUNK, 128), CHUNK)], g_pre_far[:, j * CHUNK : (j + 1) * CHUNK],
        )

    for j in range(4):
        for order in range(4):
            jobs.append(functools.partial(grad_expand, j, order))

    def grad_normed_b(j):
        cols = slice(j * CHUNK, (j + 1) * CHUNK)
        work[:, cols] = dot_rows(slope[...], w_expand[cols, :])

    for j in range(2):
        jobs.append(functools.partial(grad_normed_b, j))

    zero = jnp.zeros((8, FEATURES), FULL)

    @jobs.append
    def _():
        swaps.sent[0].wait_send()
        swaps.waited = 1

        def second_back(i, carry):
            gain_sum, shift_sum, mixer_sum, bias_sum = carry
            rows = pl.ds(aligned(i * BLOCK, BLOCK), BLOCK)
            unit, inverse = normalised(middle[rows, :])
            grad = work[rows, :]
            gain_sum += fold(grad * unit)
            shift_sum += fold(grad)
            scaled = grad * second_gain[...]
            moved = scaled - jnp.mean(scaled, axis=-1, keepdims=True)
            moved -= unit * jnp.mean(scaled * unit, axis=-1, keepdims=True)
            grad_middle = cot[rows, :].astype(FULL) + inverse * moved
            work[rows, :] = grad_middle
            mixer_sum += fold(grad_middle * branch[rows, :])
            grad_branch = (grad_middle * mixer_scale[...]).astype(LOW)
            g_branch[rows, :] = grad_branch
            bias_sum += fold(grad_branch.astype(FULL))
            return gain_sum, shift_sum, mixer_sum, bias_sum

        for line, total in zip((6, 7, 5, 4), lax.fori_loop(0, SLOTS // BLOCK, second_back, (zero,) * 4, unroll=True)):
            small[0, line : line + 1, :] = jnp.sum(total, axis=0, keepdims=True)
        swaps.push(g_branch.at[:, pl.ds(aligned(sibling * CHUNK, 128), CHUNK)], g_branch_far, 6, net.sib)

    @jobs.append
    def _():
        for j in range(2):
            cols = slice(j * CHUNK, (j + 1) * CHUNK)
            mixed[:, cols] = dot_rows(g_branch[...], w_out[cols, :]).astype(LOW)

    def grad_out(order):
        if order == 0:
            swaps.landed(blended_t.at[1], 2)
            swaps.landed(g_branch_far, 6)
        weight_grad(
            6, order, rows_of(blended_t, 0), rows_of(blended_t, 1),
            g_branch[:, pl.ds(aligned(c * CHUNK, 128), CHUNK)], g_branch_far[...],
        )

    for order in range(4):
        jobs.append(functools.partial(grad_out, order))

    lane64 = lax.broadcasted_iota(jnp.int32, (GRID, 128), 1)

    def attend_back(pair):
        cols = slice(pair * 128, (pair + 1) * 128)
        key_cols = slice(768 + pair * 128, 896 + pair * 128)
        value_cols = slice(1536 + pair * 128, 1664 + pair * 128)
        q_pair, k_pair, v_pair, g_pair = qkv[:, cols], qkv[:, key_cols], qkv[:, value_cols], mixed[:, cols]
        k_turned = k_pair.T
        grad_keys = grad_values = None
        grad_queries = []
        for e in (0, 1):
            head = 2 * pair + e
            g_head = only(g_pair, e)
            asks = jnp.concatenate([only(q_pair, e), place_q[...]], axis=1)
            k_head = k_turned[e * 64 : (e + 1) * 64, :]
            across = None
            pieces = []
            for lo, hi in spans:
                low_share = chances[head, :, lo:hi]
                share = low_share.astype(FULL)
                weighed = share * dot_rows(v_pair, g_head[lo:hi, :])
                grad = (weighed - share * jnp.sum(weighed, axis=0, keepdims=True)).astype(LOW)
                pieces.append(dot(k_head, grad).astype(LOW).astype(FULL) * 0.125)
                part = dot(grad, asks[lo:hi, :])
                across = part if across is None else across + part
                part = dot(low_share, g_head[lo:hi, :])
                grad_values = part if grad_values is None else grad_values + part
            grad_keys = across[:, :128] if grad_keys is None else grad_keys + across[:, :128]
            grad_queries.append(jnp.concatenate(pieces, axis=1))
            marks = across[:, 128:]
            high = marks.astype(LOW)
            low = (marks - high.astype(FULL)).astype(LOW)
            pairs = dot(place_t[...], jnp.concatenate([high, low], axis=1))
            pairs = pairs[:, :128] + pairs[:, 128:]
            rows_part = jnp.where(lane64 < GRID, pairs[:GRID, :], 0.0)
            cols_part = jnp.where(lane64 >= GRID, pairs[GRID:, :], 0.0)
            rows_part = pltpu.roll(rows_part, 0, 1, stride=1, stride_axis=0)
            cols_part = pltpu.roll(cols_part, 64, 1, stride=1, stride_axis=0)
            for line, part in ((head, rows_part), (12 + head, cols_part)):
                spot = (line % 6) * 128
                small[0, 14 + line // 6 : 15 + line // 6, spot : spot + 128] = jnp.sum(part, axis=0, keepdims=True)
        grad_queries = jnp.concatenate(grad_queries, axis=0).T.astype(LOW)
        grad_values = grad_values.astype(LOW)
        qkv[:, cols] = grad_queries
        qkv[:, key_cols] = grad_keys.astype(LOW)
        qkv[:, value_cols] = grad_values
        small[0, 2:3, cols] = jnp.sum(grad_queries.astype(FULL), axis=0, keepdims=True)
        small[0, 3:4, cols] = jnp.sum(grad_values.astype(FULL), axis=0, keepdims=True)
        for part in (0,) if pair == 2 else (1, 2) if pair == 5 else ():
            first = aligned(scatters[7 + part].first_column(sibling), 128)
            swaps.push(qkv.at[:, pl.ds(first, CHUNK)], g_qkv_far.at[part], 7 + part, net.sib)

    for pair in range(6):
        jobs.append(functools.partial(attend_back, pair))

    def grad_in(j, order):
        if (j, order) == (0, 0):
            swaps.landed(normed_a_t.at[1], 1)
        if order == 0:
            swaps.landed(g_qkv_far.at[j], 7 + j)
        weight_grad(
            7 + j, order, rows_of(normed_a_t, 0), rows_of(normed_a_t, 1),
            qkv[:, pl.ds(aligned(scatters[7 + j].first_column(c), 128), CHUNK)], g_qkv_far[j],
        )

    for j in range(3):
        for order in range(4):
            jobs.append(functools.partial(grad_in, j, order))

    def grad_normed_a(j):
        cols = slice(j * CHUNK, (j + 1) * CHUNK)
        branch[:, cols] = dot_rows(qkv[...], w_in[cols, :])

    for j in range(2):
        jobs.append(functools.partial(grad_normed_a, j))

    save_grad = pltpu.make_async_copy(work, input_grad_hbm, out_sem.at[0])
    save_out = pltpu.make_async_copy(mixed, outputs_hbm, out_sem.at[1])

    @jobs.append
    def _():
        def first_back(i, carry):
            gain_sum, shift_sum = carry
            rows = pl.ds(aligned(i * BLOCK, BLOCK), BLOCK)
            unit, inverse = normalised(tok[rows, :].astype(FULL))
            grad = branch[rows, :]
            gain_sum += fold(grad * unit)
            shift_sum += fold(grad)
            scaled = grad * first_gain[...]
            moved = scaled - jnp.mean(scaled, axis=-1, keepdims=True)
            moved -= unit * jnp.mean(scaled * unit, axis=-1, keepdims=True)
            work[rows, :] = work[rows, :] + inverse * moved
            return gain_sum, shift_sum

        for line, total in zip((0, 1), lax.fori_loop(0, SLOTS // BLOCK, first_back, (zero,) * 2, unroll=True)):
            small[0, line : line + 1, :] = jnp.sum(total, axis=0, keepdims=True)
        save_grad.start()

    def finish_rows(j):
        cols = slice(j * CHUNK, (j + 1) * CHUNK)
        returned = dot(act[...], w_reduce[:, cols]) + return_bias[:, cols]
        mixed[:, cols] = (middle[:, cols] + feed_scale[:, cols] * returned).astype(LOW)
        small[0, 13:14, cols] = jnp.sum(cot[:, cols].astype(FULL) * returned, axis=0, keepdims=True)
        if j == 1:
            save_out.start()

    for j in range(2):
        jobs.append(functools.partial(finish_rows, j))

    for key in PLAN:
        jobs[key]()
    small_out[...] = small[5]
    saves = []
    for i, (stage, target) in enumerate(zip(stages, (g_in_hbm, g_out_hbm, g_expand_hbm, g_reduce_hbm))):
        saves.append(pltpu.make_async_copy(stage, target, out_sem.at[2 + i]))
        saves[-1].start()
    for group in gathers + scatters + [swaps, sums]:
        group.finish()
    for save in [save_grad, save_out] + saves:
        save.wait()


PLAN = (
    0, 156, 157, 158, 1, 2, 4, 8, 3, 13, 5, 9, 14, 26, 6, 10, 7, 21, 15, 27, 17, 16, 18, 39, 11, 28, 34, 22, 30, 12,
    159, 23, 160, 161, 19, 162, 40, 163, 164, 165, 29, 166, 31, 167, 20, 47, 168, 35, 41, 169, 36, 43, 52, 170, 24,
    32, 171, 25, 42, 172, 44, 53, 65, 173, 174, 33, 48, 175, 45, 49, 60, 176, 54, 66, 177, 37, 56, 178, 46, 55, 67,
    38, 179, 180, 73, 181, 69, 182, 57, 58, 50, 61, 71, 68, 51, 183, 184, 185, 70, 186, 187, 62, 59, 72, 74, 188, 75,
    189, 190, 63, 191, 76, 192, 193, 194, 64, 195, 77, 196, 78, 197, 198, 79, 199, 200, 201, 80, 202, 203, 220, 81,
    87, 221, 88, 204, 205, 206, 207, 208, 209, 210, 211, 212, 213, 214, 215, 216, 217, 82, 218, 219, 89, 83, 222, 93,
    94, 223, 228, 84, 99, 100, 101, 224, 225, 90, 102, 226, 227, 229, 95, 108, 109, 230, 114, 85, 115, 231, 86, 96,
    103, 104, 110, 120, 121, 234, 91, 235, 236, 237, 232, 92, 97, 116, 122, 123, 124, 125, 129, 233, 98, 105, 130,
    246, 111, 238, 117, 239, 240, 241, 126, 242, 243, 244, 245, 247, 112, 131, 248, 106, 113, 118, 127, 135, 136, 137,
    138, 144, 249, 107, 119, 128, 132, 145, 250, 139, 140, 150, 146, 133, 151, 134, 141, 152, 147, 142, 143, 153, 148,
    149, 154, 155,
)


def one_kernel(
    tokens, project_in, project_out, expand_weight, reduce_weight, first_gain, first_shift, query_value_bias,
    output_bias, mixer_scale, second_gain, second_shift, hidden_bias, return_bias, feed_scale, position_table,
    image_sizes, cotangent,
):
    vector = lambda v: v
    table = jnp.transpose(position_table, (2, 0, 1))
    anywhere = pl.BlockSpec(memory_space=pl.ANY)
    vmem = pl.BlockSpec(memory_space=pltpu.VMEM)
    low = lambda *shape: pltpu.VMEM(shape, LOW)
    full = lambda *shape: pltpu.VMEM(shape, FULL)
    dma = lambda *shape: pltpu.SemaphoreType.DMA(shape)
    like = jax.ShapeDtypeStruct
    scratch = [low(16 * w[0], w[1]) for w in WEIGHTS]
    scratch += [full(w[0], w[1]) for w in WEIGHTS]
    T, D, F = SLOTS, FEATURES, HIDDEN
    scratch += [
        low(T, D), low(T, D), low(2, D, T), low(2, D, T), low(2, D, T), low(T, 3 * D),
        low(T, 128), low(T, 128), low(128, T), low(HEADS, T, T), low(T, D), full(T, D), full(T, D),
        low(T, F), low(F, T), low(16, 96, T), low(T, F), low(T, D), low(T, D), low(T, F // 2),
        low(T, D // 2), low(3, T, CHUNK), full(T, D), full(6, 24, D), full(5, 24, D), full(24, 128),
        dma(len(PARTS) + 2), dma(6), dma(len(PARTS), 24), dma(len(PARTS), 20), dma(len(CHUNKS), 12), dma(len(CHUNKS), 12), dma(10), dma(10),
        dma(5), dma(5),
    ]
    for weight, _, order in CHUNKS:
        scratch += Scatter.shapes(weight, order)
    results = pl.pallas_call(
        layer_kernel,
        out_shape=[
            like((T, D), LOW), like((T, D), FULL), like((48, 3 * D), FULL), like((48, D), FULL), like((48, F), FULL),
            like((192, D), FULL), like((24, D), FULL),
        ],
        in_specs=[pl.BlockSpec(memory_space=pltpu.SMEM)] + [anywhere] * 6 + [vmem] * 11,
        out_specs=[anywhere] * 6 + [vmem],
        scratch_shapes=scratch,
        compiler_params=pltpu.CompilerParams(
            collective_id=0, has_side_effects=True, vmem_limit_bytes=VMEM_BYTES
        ),
    )(
        image_sizes, tokens, project_in, project_out, expand_weight, reduce_weight, cotangent, vector(first_gain),
        vector(first_shift), query_value_bias, vector(output_bias), vector(mixer_scale), vector(second_gain),
        vector(second_shift), vector(hidden_bias), vector(return_bias), vector(feed_scale), table,
    )
    vectors = [(D,), (D,), (2, D), (D,), (D,), (D,), (D,), (F,), (D,), (D,), (HEADS, 2, 2 * GRID - 1)]
    handed = pl.pallas_call(
        handout,
        out_shape=[like(r.shape, r.dtype) for r in results[:6]] + [like(v, FULL) for v in vectors],
        in_specs=[anywhere] * 6 + [vmem],
        out_specs=[anywhere] * 6 + [vmem] * 11,
        scratch_shapes=[pltpu.VMEM(r.shape, r.dtype) for r in results[:6]] + [dma(2, 6)],
    )(*results)
    return (*handed[:16], jnp.transpose(handed[16], (1, 2, 0)))


def handout(*refs):
    large, small, saved, outs, held, sems = refs[:6], refs[6], refs[7:13], refs[13:24], refs[24:30], refs[30]
    loads = [pltpu.make_async_copy(large[i], held[i], sems.at[0, i]) for i in range(6)]
    copies = [pltpu.make_async_copy(held[i], saved[i], sems.at[1, i]) for i in range(6)]
    for load in loads:
        load.start()
    for load, copy in zip(loads, copies):
        load.wait()
        copy.start()
    for line, out in ((0, 0), (1, 1), (4, 3), (5, 4), (6, 5), (7, 6), (12, 8), (13, 9)):
        outs[out][...] = small[line, :]
    outs[2][...] = small[2:4, :]
    for k in range(4):
        outs[7][k * FEATURES : (k + 1) * FEATURES] = small[8 + k, :]
    for n in range(24):
        line = small[14 + n // 6 : 15 + n // 6, (n % 6) * 128 : (n % 6) * 128 + 2 * GRID - 1]
        outs[10][n % 12, n // 12 : n // 12 + 1, :] = line
    for copy in copies:
        copy.wait()


VMEM_BYTES = 64 * 2**20


def solution(mesh):
    placed = (
        P(("dp", "rep"), None),
        P("dp", None),
        P("dp", None),
        P("dp", None),
        P("dp", None),
        P(),
        P(),
        P(),
        P(),
        P(),
        P(),
        P(),
        P(),
        P(),
        P(),
        P(),
        P(("dp", "rep"), None),
        P(("dp", "rep"), None),
    )
    return jax.shard_map(
        one_kernel if tuple(mesh.shape.values()) == (16, 2) else shards,
        mesh=mesh,
        in_specs=placed,
        out_specs=(
            P(("dp", "rep"), None),
            P(("dp", "rep"), None),
            P("dp", None),
            P("dp", None),
            P("dp", None),
            P("dp", None),
            P(),
            P(),
            P(),
            P(),
            P(),
            P(),
            P(),
            P(),
            P(),
            P(),
            P(),
        ),
        check_vma=False,
    )
```

```python
import functools

import jax
import jax.numpy as jnp
from jax import lax
from jax.experimental import pallas as pl
from jax.experimental.pallas import tpu as pltpu
from jax.sharding import PartitionSpec as P

HEADS = 12
HEAD = 64
GRID = 64


EPS = 1e-06
MASKED = -1000000000.0


def layer_norm(values, gain, shift):
    centre = values - jnp.mean(values, axis=-1, keepdims=True)
    spread = jnp.mean(centre * centre, axis=-1, keepdims=True)
    return centre * lax.rsqrt(spread + EPS) * gain + shift


def gelu_exact(values):
    return jax.nn.gelu(values, approximate=False)


def shift_onehot(side):
    first_axis = lax.broadcasted_iota(jnp.int32, (side, side, 2 * side - 1), 0)
    second_axis = lax.broadcasted_iota(jnp.int32, (side, side, 2 * side - 1), 1)
    third_axis = lax.broadcasted_iota(jnp.int32, (side, side, 2 * side - 1), 2)
    return (first_axis - second_axis + side - 1 == third_axis).astype(jnp.float32)


def position_bias(shift_part, picks):
    between = jnp.einsum("tijh,tkj->tihk", shift_part, picks, preferred_element_type=jnp.float32)
    return jnp.einsum(
        "tqi,tihk->hqk", picks, between.astype(jnp.bfloat16), preferred_element_type=jnp.float32
    )


def group_scores(query_part, key_part, shift_part, picks, usable):
    scores = jnp.einsum("qhd,khd->hqk", query_part, key_part, preferred_element_type=jnp.float32)
    scores = scores + position_bias(shift_part, picks)
    return jnp.where(usable[None, None, :], scores, MASKED)


def attend_group(packed, picks, usable):
    query_part, key_part, value_part, shift_part = packed
    scores = group_scores(query_part, key_part, shift_part, picks, usable)
    highest = jnp.max(scores, axis=-1, keepdims=True)
    weights_raw = jnp.exp(scores - highest)
    totals = jnp.sum(weights_raw, axis=-1, keepdims=True)
    chances = (weights_raw / totals).astype(jnp.bfloat16)
    blended = jnp.einsum("hqk,khd->qhd", chances, value_part, preferred_element_type=jnp.float32)
    return (blended.astype(jnp.bfloat16), (highest + jnp.log(totals))[..., 0])


def attend_back(packed, picks, usable):
    query_part, key_part, value_part, grad_part, logsums, shift_part = packed
    scores = group_scores(query_part, key_part, shift_part, picks, usable)
    chances = jnp.exp(scores - logsums[..., None])
    grad_chance = jnp.einsum(
        "qhd,khd->hqk", grad_part, value_part, preferred_element_type=jnp.float32
    )
    row_dot = jnp.sum(chances * grad_chance, axis=-1, keepdims=True)
    grad_scores = (chances * (grad_chance - row_dot)).astype(jnp.bfloat16)
    grad_query = jnp.einsum(
        "hqk,khd->qhd", grad_scores, key_part, preferred_element_type=jnp.float32
    )
    grad_key = jnp.einsum(
        "hqk,qhd->khd", grad_scores, query_part, preferred_element_type=jnp.float32
    )
    grad_value = jnp.einsum(
        "hqk,qhd->khd", chances.astype(jnp.bfloat16), grad_part, preferred_element_type=jnp.float32
    )
    across = jnp.einsum("hqk,tkj->thqj", grad_scores, picks, preferred_element_type=jnp.float32)
    grad_shift = jnp.einsum(
        "tqi,thqj->tijh", picks.astype(jnp.float32), across, precision=lax.Precision.HIGHEST
    )
    return (
        grad_query.astype(jnp.bfloat16),
        grad_key.astype(jnp.bfloat16),
        grad_value.astype(jnp.bfloat16),
        grad_shift,
    )


def shards(
    tokens,
    project_in,
    project_out,
    expand_weight,
    reduce_weight,
    first_gain,
    first_shift,
    query_value_bias,
    output_bias,
    mixer_scale,
    second_gain,
    second_shift,
    hidden_bias,
    return_bias,
    feed_scale,
    position_table,
    image_sizes,
    cotangent,
):
    length = tokens.shape[0]
    width_model = tokens.shape[1]
    head_count = HEADS
    per_group = 4
    groups = head_count // per_group
    full_in, full_out, full_expand, full_reduce = (
        lax.all_gather(project_in, "dp", axis=0, tiled=True),
        lax.all_gather(project_out, "dp", axis=0, tiled=True),
        lax.all_gather(expand_weight, "dp", axis=0, tiled=True),
        lax.all_gather(reduce_weight, "dp", axis=0, tiled=True),
    )
    inputs = tokens.astype(jnp.float32)
    normed_a, first_back = jax.vjp(layer_norm, inputs, first_gain, first_shift)
    normed_a_low = normed_a.astype(jnp.bfloat16)
    projected = jnp.dot(normed_a_low, full_in, preferred_element_type=jnp.float32)
    queries = ((projected[:, :width_model] + query_value_bias[0]) * HEAD ** (-0.5)).astype(
        jnp.bfloat16
    )
    keys_low = projected[:, width_model : 2 * width_model].astype(jnp.bfloat16)
    values_low = (projected[:, 2 * width_model :] + query_value_bias[1]).astype(jnp.bfloat16)
    shift_table = shift_onehot(GRID)
    shifts = jnp.einsum(
        "ija,tah->tijh",
        shift_table.astype(jnp.bfloat16),
        position_table.astype(jnp.bfloat16),
        preferred_element_type=jnp.float32,
    ).astype(jnp.bfloat16)
    shifts_grouped = shifts.reshape(2, GRID, GRID, groups, per_group).transpose(3, 0, 1, 2, 4)
    places = jnp.arange(length, dtype=jnp.int32)
    height = image_sizes[0, 0]
    width_image = image_sizes[0, 1]
    grid_iota = jnp.arange(GRID, dtype=jnp.int32)
    picks = jnp.stack(
        [
            (places // width_image)[:, None] == grid_iota[None, :],
            (places % width_image)[:, None] == grid_iota[None, :],
        ]
    ).astype(jnp.bfloat16)
    usable = places < height * width_image

    def split_heads(matrix):
        return matrix.reshape(length, groups, per_group, HEAD).transpose(1, 0, 2, 3)

    def join_heads(blocks):
        return blocks.transpose(1, 0, 2, 3).reshape(length, width_model)

    query_groups = split_heads(queries)
    key_groups = split_heads(keys_low)
    value_groups = split_heads(values_low)
    blended_groups, logsums = lax.map(
        lambda packed: attend_group(packed, picks, usable),
        (query_groups, key_groups, value_groups, shifts_grouped),
    )
    blended = join_heads(blended_groups)
    branch = jnp.dot(blended, full_out, preferred_element_type=jnp.float32) + output_bias
    middle = inputs + mixer_scale * branch
    normed_b, second_back = jax.vjp(layer_norm, middle, second_gain, second_shift)
    normed_b_low = normed_b.astype(jnp.bfloat16)
    preact = jnp.dot(normed_b_low, full_expand, preferred_element_type=jnp.float32) + hidden_bias
    activated, gelu_back = jax.vjp(gelu_exact, preact)
    activated_low = activated.astype(jnp.bfloat16)
    returned = jnp.dot(activated_low, full_reduce, preferred_element_type=jnp.float32) + return_bias
    outputs = middle + feed_scale * returned
    back_in, back_out, back_expand, back_reduce = (
        lax.all_gather(project_in, "dp", axis=0, tiled=True),
        lax.all_gather(project_out, "dp", axis=0, tiled=True),
        lax.all_gather(expand_weight, "dp", axis=0, tiled=True),
        lax.all_gather(reduce_weight, "dp", axis=0, tiled=True),
    )
    upstream = cotangent.astype(jnp.float32)
    grad_feed_scale = jnp.sum(upstream * returned, axis=0)
    grad_returned = (upstream * feed_scale).astype(jnp.bfloat16)
    grad_return_bias = jnp.sum(grad_returned.astype(jnp.float32), axis=0)
    grad_reduce = jnp.einsum(
        "tf,td->fd", activated_low, grad_returned, preferred_element_type=jnp.float32
    )
    grad_activated = jnp.einsum(
        "td,fd->tf", grad_returned, back_reduce, preferred_element_type=jnp.float32
    )
    grad_preact = gelu_back(grad_activated)[0].astype(jnp.bfloat16)
    grad_hidden_bias = jnp.sum(grad_preact.astype(jnp.float32), axis=0)
    grad_expand = jnp.einsum(
        "td,tf->df", normed_b_low, grad_preact, preferred_element_type=jnp.float32
    )
    grad_normed_b = jnp.einsum(
        "tf,df->td", grad_preact, back_expand, preferred_element_type=jnp.float32
    )
    grad_from_norm, grad_second_gain, grad_second_shift = second_back(grad_normed_b)
    grad_middle = upstream + grad_from_norm
    grad_mixer_scale = jnp.sum(grad_middle * branch, axis=0)
    grad_branch = (grad_middle * mixer_scale).astype(jnp.bfloat16)
    grad_output_bias = jnp.sum(grad_branch.astype(jnp.float32), axis=0)
    grad_project_out = jnp.einsum(
        "td,te->de", blended, grad_branch, preferred_element_type=jnp.float32
    )
    grad_blended = jnp.einsum(
        "te,de->td", grad_branch, back_out, preferred_element_type=jnp.float32
    ).astype(jnp.bfloat16)
    grad_query_groups, grad_key_groups, grad_value_groups, grad_shift_groups = lax.map(
        lambda packed: attend_back(packed, picks, usable),
        (
            query_groups,
            key_groups,
            value_groups,
            split_heads(grad_blended),
            logsums,
            shifts_grouped,
        ),
    )
    grad_queries = join_heads(grad_query_groups) * HEAD ** (-0.5)
    grad_keys = join_heads(grad_key_groups)
    grad_values = join_heads(grad_value_groups)
    grad_projected = jnp.concatenate([grad_queries, grad_keys, grad_values], axis=1)
    grad_query_value_bias = jnp.stack(
        [
            jnp.sum(grad_queries.astype(jnp.float32), axis=0),
            jnp.sum(grad_values.astype(jnp.float32), axis=0),
        ]
    )
    grad_project_in = jnp.einsum(
        "td,te->de", normed_a_low, grad_projected, preferred_element_type=jnp.float32
    )
    grad_normed_a = jnp.einsum(
        "te,de->td", grad_projected, back_in, preferred_element_type=jnp.float32
    )
    grad_from_first, grad_first_gain, grad_first_shift = first_back(grad_normed_a)
    input_grad = grad_middle + grad_from_first
    grad_shift = grad_shift_groups.transpose(1, 2, 3, 0, 4).reshape(2, GRID, GRID, head_count)
    grad_position_table = jnp.einsum(
        "ija,tijh->tah", shift_table, grad_shift, precision=lax.Precision.HIGHEST
    )
    weight_grads = (
        lax.psum_scatter(grad_project_in, "dp", scatter_dimension=0, tiled=True),
        lax.psum_scatter(grad_project_out, "dp", scatter_dimension=0, tiled=True),
        lax.psum_scatter(grad_expand, "dp", scatter_dimension=0, tiled=True),
        lax.psum_scatter(grad_reduce, "dp", scatter_dimension=0, tiled=True),
    )
    weight_grads = lax.psum(
        (weight_grads[0], weight_grads[1], weight_grads[2], weight_grads[3]), "rep"
    )
    small_sums = lax.psum(
        (
            grad_first_gain,
            grad_first_shift,
            grad_query_value_bias,
            grad_output_bias,
            grad_mixer_scale,
            grad_second_gain,
            grad_second_shift,
            grad_hidden_bias,
            grad_return_bias,
            grad_feed_scale,
            grad_position_table,
        ),
        ("dp", "rep"),
    )
    return (
        outputs.astype(jnp.bfloat16),
        input_grad,
        weight_grads[0],
        weight_grads[1],
        weight_grads[2],
        weight_grads[3],
        small_sums[0],
        small_sums[1],
        small_sums[2],
        small_sums[3],
        small_sums[4],
        small_sums[5],
        small_sums[6],
        small_sums[7],
        small_sums[8],
        small_sums[9],
        small_sums[10],
    )


FEATURES = 768
HIDDEN = 3072
SLOTS = 448
MESH = pl.DeviceIdType.MESH
LOW = jnp.bfloat16
FULL = jnp.float32

W_IN = (48, 2304, False, "A")
W_OUT = (48, 768, False, "A")
W_EXPAND = (48, 3072, False, "A")
W_REDUCE = (192, 768, True, "B")
WEIGHTS = (W_IN, W_OUT, W_EXPAND, W_REDUCE)

PARTS = ((0, 0, 1, "A"), (1, 0, 1, "A"), (2, 0, 2, "A"), (2, 1, 2, "A"), (3, 0, 2, "B"), (3, 1, 2, "B"))

CHUNK = 384
CHUNKS = (
    (3, 0, "B"), (3, 1, "A"),
    (2, 0, "A"), (2, 1, "B"), (2, 2, "A"), (2, 3, "A"),
    (1, 0, "B"),
    (0, 0, "A"), (0, 1, "B"), (0, 2, "A"),
)
IN_COLUMNS = ((0, 4), (2, 3), (1, 5))


def aligned(index, step):
    return pl.multiple_of(index, step)


class Net:
    def __init__(self):
        dp, c = lax.axis_index("dp"), lax.axis_index("rep")
        z, y, x = dp // 4, lax.rem(dp // 2, 2), lax.rem(dp, 2)
        self.dp, self.c, self.z, self.y, self.x = dp, c, z, y, x
        self.ma = y * (1 - c) + x * c
        self.mb = x * (1 - c) + y * c
        self.wa, self.wb = 2 - c, 1 + c
        self.to_a = (dp + self.wa * (1 - 2 * self.ma), c)
        self.to_b = (dp + self.wb * (1 - 2 * self.mb), c)
        self.to_z = (lax.rem(dp + 4, 16), c)
        self.from_z = (lax.rem(dp + 12, 16), c)
        self.far_z = (lax.rem(dp + 8, 16), c)
        self.sib = (dp, 1 - c)

    def barrier(self):
        dp = self.dp
        sem = pltpu.get_barrier_semaphore()
        across = (dp - lax.rem(dp, 4) + 3 - lax.rem(dp, 4), self.c)
        for target in (self.to_a, self.to_b, self.to_z, self.from_z, self.far_z, self.sib, across):
            pl.semaphore_signal(sem, inc=1, device_id=target, device_id_type=MESH)
        pl.semaphore_wait(sem, 7)

    def back(self, steps):
        return lax.rem(self.z + 4 - steps, 4)

    def owner(self, z, a, b):
        return 4 * z + self.wa * a + self.wb * b


class Transfers:
    def __init__(self, net, send, recv):
        self.net, self.send, self.recv, self.sent = net, send, recv, []
        self.count = 0

    def push(self, src, dst, slot, to):
        copy = pltpu.make_async_remote_copy(
            src, dst, self.send.at[self.count], self.recv.at[slot], device_id=to, device_id_type=MESH
        )
        copy.start()
        self.sent.append(copy)
        self.count += 1
        return copy

    def sending_done(self, copy):
        copy.wait_send()
        self.sent = [other for other in self.sent if other is not copy]

    def landed(self, dst, slot):
        pltpu.make_async_remote_copy(
            dst, dst, self.send.at[0], self.recv.at[slot], device_id=self.net.sib, device_id_type=MESH
        ).wait_recv()

    def finish(self):
        for copy in self.sent:
            copy.wait_send()


class Gather(Transfers):
    def __init__(self, net, part, buf, send, recv):
        super().__init__(net, send, recv)
        weight, self.part, self.parts, self.order = part
        self.buf = buf
        self.rows, self.cols, self.by_rows, _ = WEIGHTS[weight]

    def span(self, c):
        half = (self.rows if self.by_rows else self.cols) // 2
        size = half // self.parts
        return c * half + self.part * size, size

    def block(self, owner):
        start, size = self.span(self.net.c)
        if self.by_rows:
            return self.buf.at[pl.ds(aligned(owner * self.rows + start, 16), size), :]
        return self.buf.at[pl.ds(aligned(owner * self.rows, 16), self.rows), pl.ds(aligned(start, 128), size)]

    def group(self, z, c):
        start, size = self.span(c)
        if self.by_rows:
            pieces = self.rows // size
            return self.buf.reshape(4, 4, pieces, size, self.cols).at[z, :, c * self.parts + self.part]
        rows = 4 * self.rows
        return self.buf.at[pl.ds(aligned(z * rows, 16), rows), pl.ds(aligned(start, 128), size)]

    def load(self, src, sem):
        start, size = self.span(self.net.c)
        if self.by_rows:
            part = src.at[pl.ds(aligned(start, 16), size), :]
        else:
            part = src.at[:, pl.ds(aligned(start, 128), size)]
        self.copy = pltpu.make_async_copy(part, self.block(self.net.dp), sem)
        self.copy.start()

    def along_z(self, ref, back, other):
        net = self.net
        if back == 0:
            self.push(ref, ref, 2 + other, net.to_z)
            self.push(ref, ref, 6 + other, net.from_z)
        elif back == 1:
            self.push(ref, ref, 4 + other, net.to_z)

    def jobs(self):
        net = self.net
        ma, mb = net.ma, net.mb

        def near(back, other):
            return self.block(net.owner(net.back(back), ma, mb + other * (1 - 2 * mb)))

        def far(back, other):
            return self.block(net.owner(net.back(back), 1 - ma, mb + other * (1 - 2 * mb)))

        def own():
            self.copy.wait()
            ref = near(0, 0)
            self.along_z(ref, 0, 0)
            self.push(ref, ref, 1, net.to_b)
            self.push(ref, ref, 8, net.to_a)

        def relay(back, other):
            def run():
                ref = near(back, other)
                self.landed(ref, back * 2 + other)
                if other == 0 or self.order != "B":
                    self.along_z(ref, back, other)
                if self.order == "B" and other == 0:
                    self.push(ref, ref, back * 2 + 1, net.to_b)
                self.push(ref, ref, 8 + back * 2 + other, net.to_a)

            return run

        def tail(back):
            def run():
                for other in (0, 1):
                    self.landed(far(back, other), 8 + back * 2 + other)
                ref = self.group(net.back(back), net.c)
                self.push(ref, ref, 16 + back, net.sib)

            return run

        def complete():
            for back in range(4):
                self.landed(self.group(net.back(back), 1 - net.c), 16 + back)

        relays = [relay(0, 1)] + [relay(back, other) for back in (1, 3, 2) for other in (0, 1)]
        return [own, *relays, *[tail(back) for back in (0, 1, 3, 2)], complete]


STEPS = (2, 1, 3, 0)


class Scatter(Transfers):
    def __init__(self, net, weight, column, order, refs, stage, send, recv):
        super().__init__(net, send, recv)
        self.order = order
        self.rows, self.cols, self.by_rows, _ = WEIGHTS[weight]
        self.g, self.ra, self.rb, self.rz = refs
        self.stage, self.column = stage, column
        self.rh = self.rows // 2 if self.by_rows else self.rows

    def produced(self, back):
        net = self.net
        self.push(self.g.at[net.back(back), 1 - net.ma], self.ra.at[back], back, net.to_a)

    def along_z(self, step, src):
        net = self.net
        self.push(src, self.rz.at[step], 8 + step, net.from_z if step == 1 else net.to_z)

    def add_into(self, dst, terms):
        total = dst[...].astype(FULL)
        for term in terms:
            total += term[...].astype(FULL)
        dst[...] = total.astype(LOW)

    def part_of_stage(self, c):
        if self.by_rows:
            return self.stage.at[pl.ds(aligned(c * self.rh, 16), self.rh), pl.ds(self.column * CHUNK, CHUNK)]
        return self.stage.at[:, pl.ds(aligned(self.first_column(c), 128), CHUNK)]

    def first_column(self, c):
        if self.cols == 3 * FEATURES:
            first, second = IN_COLUMNS[self.column]
            return (first + c * (second - first)) * CHUNK
        return c * (self.cols // 2) + self.column * CHUNK

    def last(self, terms):
        mine = self.part_of_stage(self.net.c)
        total = terms[0][...].astype(FULL)
        for term in terms[1:]:
            total += term[...].astype(FULL)
        mine[...] = total
        self.push(mine, mine, 11, self.net.sib)

    def got(self):
        self.landed(self.part_of_stage(1 - self.net.c), 11)

    def jobs(self):
        net, g, ra, rb, rz = self.net, self.g, self.ra, self.rb, self.rz
        ma, mb = net.ma, net.mb

        def step_a(s):
            def run():
                back = STEPS[s]
                self.landed(ra.at[back], back)
                terms = [ra.at[back]]
                for k in ((), (), (0,), (1, 2))[s]:
                    self.landed(rz.at[k], 8 + k)
                    terms.append(rz.at[k])
                dst = g.at[net.back(back), ma]
                self.add_into(dst, terms)
                if s < 3:
                    self.along_z(s, dst)
                else:
                    self.push(dst.at[1 - mb], rb.at[0], 4, net.to_b)

            return run

        def final_a():
            self.landed(rb.at[0], 4)
            self.last([g.at[net.z, ma, mb], rb.at[0]])

        def first_b(back):
            def run():
                self.landed(ra.at[back], back)
                dst = g.at[net.back(back), ma]
                self.add_into(dst, [ra.at[back]])
                self.push(dst.at[1 - mb], rb.at[back], 4 + back, net.to_b)

            return run

        def step_b(s):
            def run():
                back = STEPS[s]
                self.landed(rb.at[back], 4 + back)
                terms = [rb.at[back]]
                for k in ((), (), (0,), (1, 2))[s]:
                    self.landed(rz.at[k], 8 + k)
                    terms.append(rz.at[k])
                dst = g.at[net.back(back), ma, mb]
                if s < 3:
                    self.add_into(dst, terms)
                    self.along_z(s, dst)
                else:
                    self.last([dst] + terms)

            return run

        if self.order == "A":
            steps = [step_a(s) for s in range(4)] + [final_a]
        else:
            steps = [first_b(back) for back in STEPS] + [step_b(s) for s in range(4)]
        return steps + [self.got]

    @staticmethod
    def shapes(weight, order):
        rows, _, by_rows, _ = WEIGHTS[weight]
        block = (rows // 2 if by_rows else rows, CHUNK)
        relay = (3,) if order == "B" else (3, 2)
        return [
            pltpu.VMEM((4, 2, 2) + block, LOW),
            pltpu.VMEM((4, 2) + block, LOW),
            pltpu.VMEM((4 if order == "B" else 1,) + block, LOW),
            pltpu.VMEM(relay + block, LOW),
        ]


class SmallSum(Transfers):
    def __init__(self, net, buf, landing, send, recv):
        super().__init__(net, send, recv)
        self.buf, self.landing = buf, landing
        self.place, self.floor = lax.rem(net.dp, 4), net.dp - lax.rem(net.dp, 4)

    def spread(self, first, own, targets):
        ref = self.landing.at[first + own]
        for slot, target in targets:
            self.push(ref, ref, slot, target)

    def gathered(self, first):
        for k in range(1, 4):
            self.landed(self.landing.at[0], first + k)
        return (self.landing[first] + self.landing[first + 1]) + (self.landing[first + 2] + self.landing[first + 3])

    def jobs(self):
        net = self.net

        def start():
            self.push(self.buf.at[0], self.landing.at[0], 0, net.sib)

        def plane():
            self.landed(self.landing.at[0], 0)
            self.landing[1 + self.place] = self.buf[0] + self.landing[0]
            self.spread(
                1, self.place, [(1 + k, (self.floor + lax.rem(self.place + k, 4), net.c)) for k in (1, 2, 3)]
            )

        def line():
            self.landing[5 + net.z] = self.gathered(1)
            self.spread(5, net.z, [(5 + k, (lax.rem(net.dp + 4 * k, 16), net.c)) for k in (1, 2, 3)])

        def last():
            self.buf[1] = self.gathered(5)

        return [start, plane, line, last]


def dot(left, right):
    return jnp.dot(left, right, preferred_element_type=FULL)


def dot_rows(left, right):
    return lax.dot_general(left, right, (((1,), (1,)), ((), ())), preferred_element_type=FULL)


def fold(values):
    return jnp.sum(values.reshape(values.shape[0] // 8, 8, values.shape[1]), axis=0)


def normalised(values):
    centre = values - jnp.mean(values, axis=-1, keepdims=True)
    inverse = lax.rsqrt(jnp.mean(centre * centre, axis=-1, keepdims=True) + EPS)
    return centre * inverse, inverse


BLOCK = 64
ROOT_HALF = 0.7071067811865476
DENSITY = 0.3989422804014327


class Line:
    def __init__(self, ref):
        self.ref = ref

    def __getitem__(self, index):
        cols = slice(None) if index is Ellipsis else index[1]
        return self.ref[cols].reshape(1, -1)


def layer_kernel(
    sizes, tokens_hbm, w_in_hbm, w_out_hbm, w_expand_hbm, w_reduce_hbm, cotangent_hbm,
    first_gain, first_shift, query_value_bias, output_bias, mixer_scale, second_gain, second_shift,
    hidden_bias, return_bias, feed_scale, position_table,
    outputs_hbm, input_grad_hbm, g_in_hbm, g_out_hbm, g_expand_hbm, g_reduce_hbm, small_out,
    w_in, w_out, w_expand, w_reduce,
    stage_in, stage_out, stage_expand, stage_reduce,
    tok, cot, normed_a_t, normed_b_t, blended_t, qkv, place_q, place_k, place_t,
    chances, mixed, branch, middle, act, act_t, act_t_far, slope, g_ret, g_ret_far, g_pre_far,
    g_branch_far, g_qkv_far, work, small, small_landing, table,
    load_sem, out_sem, gather_send, gather_recv, scatter_send, scatter_recv, swap_send, swap_recv,
    small_send, small_recv, *scatter_refs,
):
    net = Net()
    first_gain, first_shift, output_bias, mixer_scale, second_gain, second_shift, hidden_bias, return_bias, feed_scale = map(
        Line,
        (first_gain, first_shift, output_bias, mixer_scale, second_gain, second_shift, hidden_bias, return_bias, feed_scale),
    )
    g_branch = g_ret
    normed = mixed
    c = net.c
    sibling = 1 - c

    weights = [w_in, w_out, w_expand, w_reduce]
    sources = [w_in_hbm, w_out_hbm, w_expand_hbm, w_reduce_hbm]
    jobs = []

    gathers = []
    for i, part in enumerate(PARTS):
        gather = Gather(net, part, weights[part[0]], gather_send.at[i], gather_recv.at[i])
        gather.load(sources[part[0]], load_sem.at[i])
        gathers.append(gather)
        jobs += gather.jobs()
    load_tok = pltpu.make_async_copy(tokens_hbm, tok, load_sem.at[len(PARTS)])
    load_cot = pltpu.make_async_copy(cotangent_hbm, cot, load_sem.at[len(PARTS) + 1])
    load_tok.start()
    load_cot.start()
    net.barrier()

    stages = [stage_in, stage_out, stage_expand, stage_reduce]
    scatters = []
    for i, (weight, column, order) in enumerate(CHUNKS):
        scatters.append(
            Scatter(net, weight, column, order, scatter_refs[4 * i : 4 * i + 4], stages[weight],
                    scatter_send.at[i], scatter_recv.at[i])
        )
    swaps = Transfers(net, swap_send, swap_recv)
    sums = SmallSum(net, small, small_landing, small_send, small_recv)
    for group in scatters + [sums]:
        jobs += group.jobs()

    held = []

    @jobs.append
    def _():
        load_tok.wait()
        load_cot.wait()

        def first_rows(i, carry):
            rows = pl.ds(aligned(i * BLOCK, BLOCK), BLOCK)
            unit, _ = normalised(tok[rows, :].astype(FULL))
            normed[rows, :] = (unit * first_gain[...] + first_shift[...]).astype(LOW)
            returned_grad = (cot[rows, :].astype(FULL) * feed_scale[...]).astype(LOW)
            g_ret[rows, :] = returned_grad
            return carry + fold(returned_grad.astype(FULL))

        total = lax.fori_loop(0, SLOTS // BLOCK, first_rows, jnp.zeros((8, FEATURES), FULL), unroll=True)
        small[0] = jnp.zeros_like(small[0])
        small[0, 12:13, :] = jnp.sum(total, axis=0, keepdims=True)
        held.append(swaps.push(g_ret, g_ret_far, 0, net.sib))

    def turn(source, target):
        for j in range(FEATURES // 128):
            target[0, j * 128 : (j + 1) * 128, :] = source[:, j * 128 : (j + 1) * 128].T

    @jobs.append
    def _():
        turn(normed, normed_a_t)
        swaps.push(normed_a_t.at[0], normed_a_t.at[1], 1, net.sib)

    lane128 = lax.broadcasted_iota(jnp.int32, (128, 128), 1)
    row128 = lax.broadcasted_iota(jnp.int32, (128, 128), 0)
    height, width = sizes[0, 0], sizes[0, 1]
    width_f = width.astype(FULL)
    live = (height * width).astype(FULL)

    def grid_place(slot):
        row = jnp.floor((slot + 0.5) / width_f)
        return row, slot - row * width_f

    @jobs.append
    def _():
        slot = lax.broadcasted_iota(jnp.int32, (SLOTS, 128), 0).astype(FULL)
        lane = lax.broadcasted_iota(jnp.int32, (SLOTS, 128), 1).astype(FULL)
        row, col = grid_place(slot)
        hit = jnp.where(jnp.where(lane < GRID, row, col + GRID) == lane, 1.0, 0.0)
        place_q[...] = hit.astype(LOW)
        place_k[...] = jnp.where(slot < live, hit, jnp.where(lane == GRID - 1, 1.0, 0.0)).astype(LOW)
        slot = lax.broadcasted_iota(jnp.int32, (128, SLOTS), 1).astype(FULL)
        lane = lax.broadcasted_iota(jnp.int32, (128, SLOTS), 0).astype(FULL)
        row, col = grid_place(slot)
        hit = jnp.where(lane < GRID, GRID - 1 - row, 2 * GRID - 1 - col) == lane
        place_t[...] = jnp.where(hit, 1.0, 0.0).astype(LOW)
        mirror = jnp.where(row128 + lane128 == 2 * GRID - 2, 1.0, 0.0).astype(LOW)
        for part in range(2):
            low_table = position_table[:, part, :].astype(LOW)
            table[12 * part : 12 * part + 12, :] = dot(low_table, mirror[: 2 * GRID - 1, :])

    def project(j):
        cols = slice(j * CHUNK, (j + 1) * CHUNK)
        part = dot(normed[...], w_in[:, cols])
        inner = slice((j % 2) * CHUNK, (j % 2 + 1) * CHUNK)
        if j < 2:
            part = (part + query_value_bias[0:1, inner]) * 0.125
        elif j >= 4:
            part = part + query_value_bias[1:2, inner]
        qkv[:, cols] = part.astype(LOW)

    for j in range(6):
        jobs.append(functools.partial(project, j))

    half_lane = lax.broadcasted_iota(jnp.int32, (SLOTS, 128), 1)
    no_key = (lane128 == GRID - 1) & (row128 < GRID) & (jnp.full((128, 128), live) < SLOTS)
    spans = ((0, 256), (256, SLOTS))

    def only(values, e):
        keep = half_lane < 64 if e == 0 else half_lane >= 64
        return jnp.where(keep, values, jnp.zeros_like(values))

    def bias_table(head):
        rows_part = jnp.broadcast_to(table[head : head + 1, :], (GRID, 128))
        cols_part = jnp.broadcast_to(table[12 + head : 13 + head, :], (GRID, 128))
        both = jnp.concatenate(
            [
                pltpu.roll(rows_part, 65, 1, stride=1, stride_axis=0),
                pltpu.roll(cols_part, 1, 1, stride=1, stride_axis=0),
            ],
            axis=0,
        )
        both = jnp.where(lane128 // GRID == row128 // GRID, both, 0.0)
        return jnp.where(no_key, MASKED, both).astype(LOW)

    boards = (work, branch)

    def score(head):
        pair, e = head // 2, head % 2
        keys = jnp.concatenate([qkv[:, 768 + pair * 128 : 896 + pair * 128], place_k[...]], axis=1)
        bias = dot(place_q[...], bias_table(head)).astype(LOW)
        asks = jnp.concatenate([only(qkv[:, pair * 128 : (pair + 1) * 128], e), bias], axis=1)
        boards[e][:, :SLOTS] = dot_rows(keys, asks)

    def attend(head):
        pair, e = head // 2, head % 2
        cols = slice(pair * 128, (pair + 1) * 128)
        if head == 0:
            score(0)
        if head < HEADS - 1:
            score(head + 1)
        for lo, hi in spans:
            scores = boards[e][:, lo:hi]
            raised = jnp.exp(scores - jnp.max(scores, axis=0, keepdims=True))
            chances[head, :, lo:hi] = (raised * (1.0 / jnp.sum(raised, axis=0, keepdims=True))).astype(LOW)
        v_head = qkv[:, 1536 + pair * 128 : 1664 + pair * 128].T[e * 64 : (e + 1) * 64, :]
        blended_t[0, head * 64 : (head + 1) * 64, :] = dot(v_head, chances[head]).astype(LOW)
        if e == 1:
            mixed[:, cols] = blended_t[0, cols, :].T
        if head == HEADS - 1:
            swaps.push(blended_t.at[0], blended_t.at[1], 2, net.sib)

    for head in range(HEADS):
        jobs.append(functools.partial(attend, head))

    @jobs.append
    def _():
        for j in range(2):
            cols = slice(j * CHUNK, (j + 1) * CHUNK)
            branch[:, cols] = dot(mixed[...], w_out[:, cols]) + output_bias[:, cols]

    @jobs.append
    def _():
        def middle_rows(i, carry):
            rows = pl.ds(aligned(i * BLOCK, BLOCK), BLOCK)
            mid = tok[rows, :].astype(FULL) + mixer_scale[...] * branch[rows, :]
            middle[rows, :] = mid
            unit, _ = normalised(mid)
            normed[rows, :] = (unit * second_gain[...] + second_shift[...]).astype(LOW)
            return carry

        lax.fori_loop(0, SLOTS // BLOCK, middle_rows, 0, unroll=True)
        turn(normed, normed_b_t)
        swaps.push(normed_b_t.at[0], normed_b_t.at[1], 3, net.sib)

    act_blocks = act_t.reshape(16, 2, 96, SLOTS)

    def hidden(j):
        cols = slice(j * CHUNK, (j + 1) * CHUNK)
        pre = dot(normed[...], w_expand[:, cols]) + hidden_bias[:, cols]
        share = 0.5 + 0.5 * lax.erf(pre * ROOT_HALF)
        active = (pre * share).astype(LOW)
        act[:, cols] = active
        slope[:, cols] = (share + pre * (DENSITY * jnp.exp(-0.5 * pre * pre))).astype(LOW)
        for k in range(3):
            act_t[j * CHUNK + k * 128 : j * CHUNK + (k + 1) * 128, :] = active[:, k * 128 : (k + 1) * 128].T

    for i, j in enumerate((0, 1, 4, 5, 2, 3, 6, 7)):
        jobs.append(functools.partial(hidden, j))

    @jobs.append
    def _():
        held.append(swaps.push(act_blocks.at[:, sibling], act_t_far, 4, net.sib))

    def place_of(owner):
        oy, ox = owner // 2, owner % 2
        return oy * (1 - c) + ox * c, ox * (1 - c) + oy * c

    def weight_grad(index, order, left, left_far, right, right_far):
        scatter = scatters[index]
        back = STEPS[order]
        z = net.back(back)
        tile = (dot(left(z), right) + dot(left_far(z), right_far)).astype(LOW)
        for owner in range(4):
            pa, pb = place_of(owner)
            scatter.g[z, pa, pb] = tile[owner * scatter.rh : (owner + 1) * scatter.rh, :]
        scatter.produced(back)

    def rows_of(ref, slot):
        return lambda z: ref[slot, pl.ds(aligned(z * 192, 64), 192), :]

    def grad_reduce(j, order):
        cols = slice(j * CHUNK, (j + 1) * CHUNK)
        if (j, order) == (0, 0):
            swaps.landed(g_ret_far, 0)
            swaps.landed(act_t_far, 4)
        weight_grad(
            j, order,
            lambda z: act_blocks[pl.ds(4 * z, 4), c].reshape(384, SLOTS),
            lambda z: act_t_far[pl.ds(4 * z, 4)].reshape(384, SLOTS),
            g_ret[:, cols], g_ret_far[:, cols],
        )

    for j in range(2):
        for order in range(4):
            jobs.append(functools.partial(grad_reduce, j, order))

    def grad_hidden(j):
        half = sibling if j < 4 else c
        cols = pl.ds(aligned(half * 1536 + (j % 4) * CHUNK, 128), CHUNK)
        part = (dot_rows(g_ret[...], w_reduce[cols, :]) * slope[:, cols].astype(FULL)).astype(LOW)
        slope[:, cols] = part
        summed = jnp.sum(part.astype(FULL), axis=0, keepdims=True)
        small[0, pl.ds(8 + 2 * half + (j % 4) // 2, 1), (j % 2) * CHUNK : (j % 2 + 1) * CHUNK] = summed
        if j == 3:
            swaps.push(slope.at[:, pl.ds(aligned(sibling * 1536, 128), 1536)], g_pre_far, 5, net.sib)

    for j in range(8):
        jobs.append(functools.partial(grad_hidden, j))

    def grad_expand(j, order):
        if (j, order) == (0, 0):
            swaps.landed(normed_b_t.at[1], 3)
            swaps.landed(g_pre_far, 5)
        weight_grad(
            2 + j, order, rows_of(normed_b_t, 0), rows_of(normed_b_t, 1),
            slope[:, pl.ds(aligned(c * 1536 + j * CHUNK, 128), CHUNK)], g_pre_far[:, j * CHUNK : (j + 1) * CHUNK],
        )

    for j in range(4):
        for order in range(4):
            jobs.append(functools.partial(grad_expand, j, order))

    def grad_normed_b(j):
        cols = slice(j * CHUNK, (j + 1) * CHUNK)
        work[:, cols] = dot_rows(slope[...], w_expand[cols, :])

    for j in range(2):
        jobs.append(functools.partial(grad_normed_b, j))

    zero = jnp.zeros((8, FEATURES), FULL)

    @jobs.append
    def _():
        swaps.sending_done(held.pop(0))

        def second_back(i, carry):
            gain_sum, shift_sum, mixer_sum, bias_sum = carry
            rows = pl.ds(aligned(i * BLOCK, BLOCK), BLOCK)
            unit, inverse = normalised(middle[rows, :])
            grad = work[rows, :]
            gain_sum += fold(grad * unit)
            shift_sum += fold(grad)
            scaled = grad * second_gain[...]
            moved = scaled - jnp.mean(scaled, axis=-1, keepdims=True)
            moved -= unit * jnp.mean(scaled * unit, axis=-1, keepdims=True)
            grad_middle = cot[rows, :].astype(FULL) + inverse * moved
            work[rows, :] = grad_middle
            mixer_sum += fold(grad_middle * branch[rows, :])
            grad_branch = (grad_middle * mixer_scale[...]).astype(LOW)
            g_branch[rows, :] = grad_branch
            bias_sum += fold(grad_branch.astype(FULL))
            return gain_sum, shift_sum, mixer_sum, bias_sum

        for line, total in zip((6, 7, 5, 4), lax.fori_loop(0, SLOTS // BLOCK, second_back, (zero,) * 4, unroll=True)):
            small[0, line : line + 1, :] = jnp.sum(total, axis=0, keepdims=True)
        swaps.push(g_branch.at[:, pl.ds(aligned(sibling * CHUNK, 128), CHUNK)], g_branch_far, 6, net.sib)

    @jobs.append
    def _():
        for j in range(2):
            cols = slice(j * CHUNK, (j + 1) * CHUNK)
            mixed[:, cols] = dot_rows(g_branch[...], w_out[cols, :]).astype(LOW)

    def grad_out(order):
        if order == 0:
            swaps.landed(blended_t.at[1], 2)
            swaps.landed(g_branch_far, 6)
        weight_grad(
            6, order, rows_of(blended_t, 0), rows_of(blended_t, 1),
            g_branch[:, pl.ds(aligned(c * CHUNK, 128), CHUNK)], g_branch_far[...],
        )

    for order in range(4):
        jobs.append(functools.partial(grad_out, order))

    lane64 = lax.broadcasted_iota(jnp.int32, (GRID, 128), 1)

    grad_boards = (act_t.at[0:SLOTS, :], act_t.at[SLOTS : 2 * SLOTS, :])
    parts = {}

    def grad_chance(head):
        pair, e = head // 2, head % 2
        value_cols = slice(1536 + pair * 128, 1664 + pair * 128)
        g_head = only(mixed[:, pair * 128 : (pair + 1) * 128], e)
        branch[:, :SLOTS] = dot_rows(qkv[:, value_cols], g_head)

    def attend_back(head):
        pair, e = head // 2, head % 2
        cols = slice(pair * 128, (pair + 1) * 128)
        key_cols = slice(768 + pair * 128, 896 + pair * 128)
        value_cols = slice(1536 + pair * 128, 1664 + pair * 128)
        board = grad_boards[e]
        if head == 0:
            swaps.sending_done(held.pop())
            grad_chance(0)
        for lo, hi in spans:
            share = chances[head, :, lo:hi].astype(FULL)
            weighed = share * branch[:, lo:hi]
            board[:, lo:hi] = (weighed - share * jnp.sum(weighed, axis=0, keepdims=True)).astype(LOW)
        if head < HEADS - 1:
            grad_chance(head + 1)
        asks = jnp.concatenate([only(qkv[:, cols], e), place_q[...]], axis=1)
        across = dot(board[...], asks)
        grad_values = dot(chances[head], only(mixed[:, cols], e))
        k_head = qkv[:, key_cols].T[e * 64 : (e + 1) * 64, :]
        grad_queries = dot(k_head, board[...]).astype(LOW).astype(FULL) * 0.125
        marks = across[:, 128:]
        high = marks.astype(LOW)
        low = (marks - high.astype(FULL)).astype(LOW)
        pairs = dot(place_t[...], jnp.concatenate([high, low], axis=1))
        pairs = pairs[:, :128] + pairs[:, 128:]
        rows_part = jnp.where(lane64 < GRID, pairs[:GRID, :], 0.0)
        cols_part = jnp.where(lane64 >= GRID, pairs[GRID:, :], 0.0)
        rows_part = pltpu.roll(rows_part, 0, 1, stride=1, stride_axis=0)
        cols_part = pltpu.roll(cols_part, 64, 1, stride=1, stride_axis=0)
        for line, part in ((head, rows_part), (12 + head, cols_part)):
            spot = (line % 6) * 128
            small[0, 14 + line // 6 : 15 + line // 6, spot : spot + 128] = jnp.sum(part, axis=0, keepdims=True)
        if e == 0:
            parts[pair] = grad_queries, across[:, :128], grad_values
            return
        first_queries, first_keys, first_values = parts.pop(pair)
        grad_queries = jnp.concatenate([first_queries, grad_queries], axis=0).T.astype(LOW)
        grad_values = (first_values + grad_values).astype(LOW)
        qkv[:, cols] = grad_queries
        qkv[:, key_cols] = (first_keys + across[:, :128]).astype(LOW)
        qkv[:, value_cols] = grad_values
        small[0, 2:3, cols] = jnp.sum(grad_queries.astype(FULL), axis=0, keepdims=True)
        small[0, 3:4, cols] = jnp.sum(grad_values.astype(FULL), axis=0, keepdims=True)
        for part in (0,) if pair == 2 else (1, 2) if pair == 5 else ():
            first = aligned(scatters[7 + part].first_column(sibling), 128)
            swaps.push(qkv.at[:, pl.ds(first, CHUNK)], g_qkv_far.at[part], 7 + part, net.sib)

    for head in range(HEADS):
        jobs.append(functools.partial(attend_back, head))

    def grad_in(j, order):
        if (j, order) == (0, 0):
            swaps.landed(normed_a_t.at[1], 1)
        if order == 0:
            swaps.landed(g_qkv_far.at[j], 7 + j)
        weight_grad(
            7 + j, order, rows_of(normed_a_t, 0), rows_of(normed_a_t, 1),
            qkv[:, pl.ds(aligned(scatters[7 + j].first_column(c), 128), CHUNK)], g_qkv_far[j],
        )

    for j in range(3):
        for order in range(4):
            jobs.append(functools.partial(grad_in, j, order))

    def grad_normed_a(j):
        cols = slice(j * CHUNK, (j + 1) * CHUNK)
        branch[:, cols] = dot_rows(qkv[...], w_in[cols, :])

    for j in range(2):
        jobs.append(functools.partial(grad_normed_a, j))

    save_grad = pltpu.make_async_copy(work, input_grad_hbm, out_sem.at[0])
    save_out = pltpu.make_async_copy(mixed, outputs_hbm, out_sem.at[1])

    @jobs.append
    def _():
        def first_back(i, carry):
            gain_sum, shift_sum = carry
            rows = pl.ds(aligned(i * BLOCK, BLOCK), BLOCK)
            unit, inverse = normalised(tok[rows, :].astype(FULL))
            grad = branch[rows, :]
            gain_sum += fold(grad * unit)
            shift_sum += fold(grad)
            scaled = grad * first_gain[...]
            moved = scaled - jnp.mean(scaled, axis=-1, keepdims=True)
            moved -= unit * jnp.mean(scaled * unit, axis=-1, keepdims=True)
            work[rows, :] = work[rows, :] + inverse * moved
            return gain_sum, shift_sum

        for line, total in zip((0, 1), lax.fori_loop(0, SLOTS // BLOCK, first_back, (zero,) * 2, unroll=True)):
            small[0, line : line + 1, :] = jnp.sum(total, axis=0, keepdims=True)
        save_grad.start()

    def finish_rows(j):
        cols = slice(j * CHUNK, (j + 1) * CHUNK)
        returned = dot(act[...], w_reduce[:, cols]) + return_bias[:, cols]
        mixed[:, cols] = (middle[:, cols] + feed_scale[:, cols] * returned).astype(LOW)
        small[0, 13:14, cols] = jnp.sum(cot[:, cols].astype(FULL) * returned, axis=0, keepdims=True)
        if j == 1:
            save_out.start()

    for j in range(2):
        jobs.append(functools.partial(finish_rows, j))

    for key in PLAN:
        jobs[key]()
    small_out[...] = small[1]
    saves = []
    for i, (stage, target) in enumerate(zip(stages, (g_in_hbm, g_out_hbm, g_expand_hbm, g_reduce_hbm))):
        saves.append(pltpu.make_async_copy(stage, target, out_sem.at[2 + i]))
        saves[-1].start()
    for group in gathers + scatters + [swaps, sums]:
        group.finish()
    for save in [save_grad, save_out] + saves:
        save.wait()


PLAN = (
    0, 154, 155, 156, 1, 2, 13, 4, 8, 14, 3, 26, 5, 21, 9, 6, 15, 27, 17, 16, 10, 18, 34, 7, 22, 23, 39, 28, 30, 11,
    19, 40, 29, 12, 157, 158, 159, 160, 161, 31, 162, 163, 20, 47, 164, 35, 165, 41, 166, 167, 36, 168, 24, 43, 52,
    169, 170, 32, 25, 171, 172, 42, 65, 173, 174, 44, 53, 175, 176, 33, 45, 48, 66, 54, 49, 60, 56, 37, 46, 73, 55,
    38, 177, 67, 178, 179, 57, 69, 180, 50, 58, 61, 68, 51, 181, 71, 182, 183, 62, 184, 70, 185, 59, 74, 72, 186, 75,
    187, 63, 188, 189, 76, 190, 191, 64, 192, 193, 77, 194, 78, 195, 196, 79, 197, 198, 199, 80, 200, 201, 218, 81,
    87, 219, 88, 202, 203, 204, 205, 206, 207, 208, 209, 210, 211, 212, 213, 214, 215, 82, 216, 217, 89, 83, 220, 93,
    94, 221, 226, 84, 222, 223, 99, 224, 225, 227, 100, 101, 228, 90, 102, 229, 108, 230, 109, 231, 95, 232, 114, 233,
    115, 238, 239, 240, 241, 234, 85, 235, 110, 120, 121, 236, 86, 103, 122, 237, 123, 250, 91, 96, 104, 242, 243,
    116, 129, 244, 245, 92, 246, 130, 247, 248, 249, 251, 111, 124, 125, 252, 97, 105, 117, 135, 136, 137, 253, 98,
    131, 138, 144, 145, 254, 112, 126, 118, 150, 106, 139, 140, 113, 119, 151, 107, 132, 146, 127, 141, 128, 152, 133,
    147, 134, 142, 143, 148, 149, 153,
)


def one_kernel(
    tokens, project_in, project_out, expand_weight, reduce_weight, first_gain, first_shift, query_value_bias,
    output_bias, mixer_scale, second_gain, second_shift, hidden_bias, return_bias, feed_scale, position_table,
    image_sizes, cotangent,
):
    vector = lambda v: v
    table = jnp.transpose(position_table, (2, 0, 1))
    anywhere = pl.BlockSpec(memory_space=pl.ANY)
    vmem = pl.BlockSpec(memory_space=pltpu.VMEM)
    low = lambda *shape: pltpu.VMEM(shape, LOW)
    full = lambda *shape: pltpu.VMEM(shape, FULL)
    dma = lambda *shape: pltpu.SemaphoreType.DMA(shape)
    like = jax.ShapeDtypeStruct
    scratch = [low(16 * w[0], w[1]) for w in WEIGHTS]
    scratch += [full(w[0], w[1]) for w in WEIGHTS]
    T, D, F = SLOTS, FEATURES, HIDDEN
    scratch += [
        low(T, D), low(T, D), low(2, D, T), low(2, D, T), low(2, D, T), low(T, 3 * D),
        low(T, 128), low(T, 128), low(128, T), low(HEADS, T, T), low(T, D), full(T, D), full(T, D),
        low(T, F), low(F, T), low(16, 96, T), low(T, F), low(T, D), low(T, D), low(T, F // 2),
        low(T, D // 2), low(3, T, CHUNK), full(T, D), full(2, 24, D), full(9, 24, D), full(24, 128),
        dma(len(PARTS) + 2), dma(6), dma(len(PARTS), 24), dma(len(PARTS), 20), dma(len(CHUNKS), 12), dma(len(CHUNKS), 12), dma(10), dma(10),
        dma(7), dma(9),
    ]
    for weight, _, order in CHUNKS:
        scratch += Scatter.shapes(weight, order)
    results = pl.pallas_call(
        layer_kernel,
        out_shape=[
            like((T, D), LOW), like((T, D), FULL), like((48, 3 * D), FULL), like((48, D), FULL), like((48, F), FULL),
            like((192, D), FULL), like((24, D), FULL),
        ],
        in_specs=[pl.BlockSpec(memory_space=pltpu.SMEM)] + [anywhere] * 6 + [vmem] * 11,
        out_specs=[anywhere] * 6 + [vmem],
        scratch_shapes=scratch,
        compiler_params=pltpu.CompilerParams(
            collective_id=0, has_side_effects=True, vmem_limit_bytes=VMEM_BYTES
        ),
    )(
        image_sizes, tokens, project_in, project_out, expand_weight, reduce_weight, cotangent, vector(first_gain),
        vector(first_shift), query_value_bias, vector(output_bias), vector(mixer_scale), vector(second_gain),
        vector(second_shift), vector(hidden_bias), vector(return_bias), vector(feed_scale), table,
    )
    vectors = [(D,), (D,), (2, D), (D,), (D,), (D,), (D,), (F,), (D,), (D,), (HEADS, 2, 2 * GRID - 1)]
    handed = pl.pallas_call(
        handout,
        out_shape=[like(r.shape, r.dtype) for r in results[:6]] + [like(v, FULL) for v in vectors],
        in_specs=[anywhere] * 6 + [vmem],
        out_specs=[anywhere] * 6 + [vmem] * 11,
        scratch_shapes=[pltpu.VMEM(r.shape, r.dtype) for r in results[:6]] + [dma(2, 6)],
    )(*results)
    return (*handed[:16], jnp.transpose(handed[16], (1, 2, 0)))


def handout(*refs):
    large, small, saved, outs, held, sems = refs[:6], refs[6], refs[7:13], refs[13:24], refs[24:30], refs[30]
    loads = [pltpu.make_async_copy(large[i], held[i], sems.at[0, i]) for i in range(6)]
    copies = [pltpu.make_async_copy(held[i], saved[i], sems.at[1, i]) for i in range(6)]
    for load in loads:
        load.start()
    for load, copy in zip(loads, copies):
        load.wait()
        copy.start()
    for line, out in ((0, 0), (1, 1), (4, 3), (5, 4), (6, 5), (7, 6), (12, 8), (13, 9)):
        outs[out][...] = small[line, :]
    outs[2][...] = small[2:4, :]
    for k in range(4):
        outs[7][k * FEATURES : (k + 1) * FEATURES] = small[8 + k, :]
    for n in range(24):
        line = small[14 + n // 6 : 15 + n // 6, (n % 6) * 128 : (n % 6) * 128 + 2 * GRID - 1]
        outs[10][n % 12, n // 12 : n // 12 + 1, :] = line
    for copy in copies:
        copy.wait()


VMEM_BYTES = 64 * 2**20


def solution(mesh):
    placed = (
        P(("dp", "rep"), None),
        P("dp", None),
        P("dp", None),
        P("dp", None),
        P("dp", None),
        P(),
        P(),
        P(),
        P(),
        P(),
        P(),
        P(),
        P(),
        P(),
        P(),
        P(),
        P(("dp", "rep"), None),
        P(("dp", "rep"), None),
    )
    return jax.shard_map(
        one_kernel if tuple(mesh.shape.values()) == (16, 2) else shards,
        mesh=mesh,
        in_specs=placed,
        out_specs=(
            P(("dp", "rep"), None),
            P(("dp", "rep"), None),
            P("dp", None),
            P("dp", None),
            P("dp", None),
            P("dp", None),
            P(),
            P(),
            P(),
            P(),
            P(),
            P(),
            P(),
            P(),
            P(),
            P(),
            P(),
        ),
        check_vma=False,
    )
```

```python
import functools

import jax
import jax.numpy as jnp
from jax import lax
from jax.experimental import pallas as pl
from jax.experimental.pallas import tpu as pltpu
from jax.sharding import PartitionSpec as P

HEADS = 12
HEAD = 64
GRID = 64


EPS = 1e-06
MASKED = -1000000000.0


def layer_norm(values, gain, shift):
    centre = values - jnp.mean(values, axis=-1, keepdims=True)
    spread = jnp.mean(centre * centre, axis=-1, keepdims=True)
    return centre * lax.rsqrt(spread + EPS) * gain + shift


def gelu_exact(values):
    return jax.nn.gelu(values, approximate=False)


def shift_onehot(side):
    first_axis = lax.broadcasted_iota(jnp.int32, (side, side, 2 * side - 1), 0)
    second_axis = lax.broadcasted_iota(jnp.int32, (side, side, 2 * side - 1), 1)
    third_axis = lax.broadcasted_iota(jnp.int32, (side, side, 2 * side - 1), 2)
    return (first_axis - second_axis + side - 1 == third_axis).astype(jnp.float32)


def position_bias(shift_part, picks):
    between = jnp.einsum("tijh,tkj->tihk", shift_part, picks, preferred_element_type=jnp.float32)
    return jnp.einsum(
        "tqi,tihk->hqk", picks, between.astype(jnp.bfloat16), preferred_element_type=jnp.float32
    )


def group_scores(query_part, key_part, shift_part, picks, usable):
    scores = jnp.einsum("qhd,khd->hqk", query_part, key_part, preferred_element_type=jnp.float32)
    scores = scores + position_bias(shift_part, picks)
    return jnp.where(usable[None, None, :], scores, MASKED)


def attend_group(packed, picks, usable):
    query_part, key_part, value_part, shift_part = packed
    scores = group_scores(query_part, key_part, shift_part, picks, usable)
    highest = jnp.max(scores, axis=-1, keepdims=True)
    weights_raw = jnp.exp(scores - highest)
    totals = jnp.sum(weights_raw, axis=-1, keepdims=True)
    chances = (weights_raw / totals).astype(jnp.bfloat16)
    blended = jnp.einsum("hqk,khd->qhd", chances, value_part, preferred_element_type=jnp.float32)
    return (blended.astype(jnp.bfloat16), (highest + jnp.log(totals))[..., 0])


def attend_back(packed, picks, usable):
    query_part, key_part, value_part, grad_part, logsums, shift_part = packed
    scores = group_scores(query_part, key_part, shift_part, picks, usable)
    chances = jnp.exp(scores - logsums[..., None])
    grad_chance = jnp.einsum(
        "qhd,khd->hqk", grad_part, value_part, preferred_element_type=jnp.float32
    )
    row_dot = jnp.sum(chances * grad_chance, axis=-1, keepdims=True)
    grad_scores = (chances * (grad_chance - row_dot)).astype(jnp.bfloat16)
    grad_query = jnp.einsum(
        "hqk,khd->qhd", grad_scores, key_part, preferred_element_type=jnp.float32
    )
    grad_key = jnp.einsum(
        "hqk,qhd->khd", grad_scores, query_part, preferred_element_type=jnp.float32
    )
    grad_value = jnp.einsum(
        "hqk,qhd->khd", chances.astype(jnp.bfloat16), grad_part, preferred_element_type=jnp.float32
    )
    across = jnp.einsum("hqk,tkj->thqj", grad_scores, picks, preferred_element_type=jnp.float32)
    grad_shift = jnp.einsum(
        "tqi,thqj->tijh", picks.astype(jnp.float32), across, precision=lax.Precision.HIGHEST
    )
    return (
        grad_query.astype(jnp.bfloat16),
        grad_key.astype(jnp.bfloat16),
        grad_value.astype(jnp.bfloat16),
        grad_shift,
    )


def shards(
    tokens,
    project_in,
    project_out,
    expand_weight,
    reduce_weight,
    first_gain,
    first_shift,
    query_value_bias,
    output_bias,
    mixer_scale,
    second_gain,
    second_shift,
    hidden_bias,
    return_bias,
    feed_scale,
    position_table,
    image_sizes,
    cotangent,
):
    length = tokens.shape[0]
    width_model = tokens.shape[1]
    head_count = HEADS
    per_group = 4
    groups = head_count // per_group
    full_in, full_out, full_expand, full_reduce = (
        lax.all_gather(project_in, "dp", axis=0, tiled=True),
        lax.all_gather(project_out, "dp", axis=0, tiled=True),
        lax.all_gather(expand_weight, "dp", axis=0, tiled=True),
        lax.all_gather(reduce_weight, "dp", axis=0, tiled=True),
    )
    inputs = tokens.astype(jnp.float32)
    normed_a, first_back = jax.vjp(layer_norm, inputs, first_gain, first_shift)
    normed_a_low = normed_a.astype(jnp.bfloat16)
    projected = jnp.dot(normed_a_low, full_in, preferred_element_type=jnp.float32)
    queries = ((projected[:, :width_model] + query_value_bias[0]) * HEAD ** (-0.5)).astype(
        jnp.bfloat16
    )
    keys_low = projected[:, width_model : 2 * width_model].astype(jnp.bfloat16)
    values_low = (projected[:, 2 * width_model :] + query_value_bias[1]).astype(jnp.bfloat16)
    shift_table = shift_onehot(GRID)
    shifts = jnp.einsum(
        "ija,tah->tijh",
        shift_table.astype(jnp.bfloat16),
        position_table.astype(jnp.bfloat16),
        preferred_element_type=jnp.float32,
    ).astype(jnp.bfloat16)
    shifts_grouped = shifts.reshape(2, GRID, GRID, groups, per_group).transpose(3, 0, 1, 2, 4)
    places = jnp.arange(length, dtype=jnp.int32)
    height = image_sizes[0, 0]
    width_image = image_sizes[0, 1]
    grid_iota = jnp.arange(GRID, dtype=jnp.int32)
    picks = jnp.stack(
        [
            (places // width_image)[:, None] == grid_iota[None, :],
            (places % width_image)[:, None] == grid_iota[None, :],
        ]
    ).astype(jnp.bfloat16)
    usable = places < height * width_image

    def split_heads(matrix):
        return matrix.reshape(length, groups, per_group, HEAD).transpose(1, 0, 2, 3)

    def join_heads(blocks):
        return blocks.transpose(1, 0, 2, 3).reshape(length, width_model)

    query_groups = split_heads(queries)
    key_groups = split_heads(keys_low)
    value_groups = split_heads(values_low)
    blended_groups, logsums = lax.map(
        lambda packed: attend_group(packed, picks, usable),
        (query_groups, key_groups, value_groups, shifts_grouped),
    )
    blended = join_heads(blended_groups)
    branch = jnp.dot(blended, full_out, preferred_element_type=jnp.float32) + output_bias
    middle = inputs + mixer_scale * branch
    normed_b, second_back = jax.vjp(layer_norm, middle, second_gain, second_shift)
    normed_b_low = normed_b.astype(jnp.bfloat16)
    preact = jnp.dot(normed_b_low, full_expand, preferred_element_type=jnp.float32) + hidden_bias
    activated, gelu_back = jax.vjp(gelu_exact, preact)
    activated_low = activated.astype(jnp.bfloat16)
    returned = jnp.dot(activated_low, full_reduce, preferred_element_type=jnp.float32) + return_bias
    outputs = middle + feed_scale * returned
    back_in, back_out, back_expand, back_reduce = (
        lax.all_gather(project_in, "dp", axis=0, tiled=True),
        lax.all_gather(project_out, "dp", axis=0, tiled=True),
        lax.all_gather(expand_weight, "dp", axis=0, tiled=True),
        lax.all_gather(reduce_weight, "dp", axis=0, tiled=True),
    )
    upstream = cotangent.astype(jnp.float32)
    grad_feed_scale = jnp.sum(upstream * returned, axis=0)
    grad_returned = (upstream * feed_scale).astype(jnp.bfloat16)
    grad_return_bias = jnp.sum(grad_returned.astype(jnp.float32), axis=0)
    grad_reduce = jnp.einsum(
        "tf,td->fd", activated_low, grad_returned, preferred_element_type=jnp.float32
    )
    grad_activated = jnp.einsum(
        "td,fd->tf", grad_returned, back_reduce, preferred_element_type=jnp.float32
    )
    grad_preact = gelu_back(grad_activated)[0].astype(jnp.bfloat16)
    grad_hidden_bias = jnp.sum(grad_preact.astype(jnp.float32), axis=0)
    grad_expand = jnp.einsum(
        "td,tf->df", normed_b_low, grad_preact, preferred_element_type=jnp.float32
    )
    grad_normed_b = jnp.einsum(
        "tf,df->td", grad_preact, back_expand, preferred_element_type=jnp.float32
    )
    grad_from_norm, grad_second_gain, grad_second_shift = second_back(grad_normed_b)
    grad_middle = upstream + grad_from_norm
    grad_mixer_scale = jnp.sum(grad_middle * branch, axis=0)
    grad_branch = (grad_middle * mixer_scale).astype(jnp.bfloat16)
    grad_output_bias = jnp.sum(grad_branch.astype(jnp.float32), axis=0)
    grad_project_out = jnp.einsum(
        "td,te->de", blended, grad_branch, preferred_element_type=jnp.float32
    )
    grad_blended = jnp.einsum(
        "te,de->td", grad_branch, back_out, preferred_element_type=jnp.float32
    ).astype(jnp.bfloat16)
    grad_query_groups, grad_key_groups, grad_value_groups, grad_shift_groups = lax.map(
        lambda packed: attend_back(packed, picks, usable),
        (
            query_groups,
            key_groups,
            value_groups,
            split_heads(grad_blended),
            logsums,
            shifts_grouped,
        ),
    )
    grad_queries = join_heads(grad_query_groups) * HEAD ** (-0.5)
    grad_keys = join_heads(grad_key_groups)
    grad_values = join_heads(grad_value_groups)
    grad_projected = jnp.concatenate([grad_queries, grad_keys, grad_values], axis=1)
    grad_query_value_bias = jnp.stack(
        [
            jnp.sum(grad_queries.astype(jnp.float32), axis=0),
            jnp.sum(grad_values.astype(jnp.float32), axis=0),
        ]
    )
    grad_project_in = jnp.einsum(
        "td,te->de", normed_a_low, grad_projected, preferred_element_type=jnp.float32
    )
    grad_normed_a = jnp.einsum(
        "te,de->td", grad_projected, back_in, preferred_element_type=jnp.float32
    )
    grad_from_first, grad_first_gain, grad_first_shift = first_back(grad_normed_a)
    input_grad = grad_middle + grad_from_first
    grad_shift = grad_shift_groups.transpose(1, 2, 3, 0, 4).reshape(2, GRID, GRID, head_count)
    grad_position_table = jnp.einsum(
        "ija,tijh->tah", shift_table, grad_shift, precision=lax.Precision.HIGHEST
    )
    weight_grads = (
        lax.psum_scatter(grad_project_in, "dp", scatter_dimension=0, tiled=True),
        lax.psum_scatter(grad_project_out, "dp", scatter_dimension=0, tiled=True),
        lax.psum_scatter(grad_expand, "dp", scatter_dimension=0, tiled=True),
        lax.psum_scatter(grad_reduce, "dp", scatter_dimension=0, tiled=True),
    )
    weight_grads = lax.psum(
        (weight_grads[0], weight_grads[1], weight_grads[2], weight_grads[3]), "rep"
    )
    small_sums = lax.psum(
        (
            grad_first_gain,
            grad_first_shift,
            grad_query_value_bias,
            grad_output_bias,
            grad_mixer_scale,
            grad_second_gain,
            grad_second_shift,
            grad_hidden_bias,
            grad_return_bias,
            grad_feed_scale,
            grad_position_table,
        ),
        ("dp", "rep"),
    )
    return (
        outputs.astype(jnp.bfloat16),
        input_grad,
        weight_grads[0],
        weight_grads[1],
        weight_grads[2],
        weight_grads[3],
        small_sums[0],
        small_sums[1],
        small_sums[2],
        small_sums[3],
        small_sums[4],
        small_sums[5],
        small_sums[6],
        small_sums[7],
        small_sums[8],
        small_sums[9],
        small_sums[10],
    )


FEATURES = 768
HIDDEN = 3072
SLOTS = 448
MESH = pl.DeviceIdType.MESH
LOW = jnp.bfloat16
FULL = jnp.float32

W_IN = (48, 2304, False, "A")
W_OUT = (48, 768, False, "A")
W_EXPAND = (48, 3072, False, "A")
W_REDUCE = (192, 768, True, "B")
WEIGHTS = (W_IN, W_OUT, W_EXPAND, W_REDUCE)

PARTS = ((0, 0, 1, "B"), (1, 0, 1, "A"), (2, 0, 2, "A"), (2, 1, 2, "A"), (3, 0, 2, "B"), (3, 1, 2, "A"))

CHUNK = 384
WIDE = 256
CHUNKS = (
    (3, 0, "A"), (3, 1, "A"), (2, 0, "A"), (2, 1, "A"), (2, 2, "B"), (2, 3, "A"), (1, 0, "A"), (0, 0, "B"), (0, 1, "B"), (0, 2, "B")
)
IN_COLUMNS = ((0, 4), (2, 3), (1, 5))


def aligned(index, step):
    return pl.multiple_of(index, step)


class Net:
    def __init__(self):
        dp, c = lax.axis_index("dp"), lax.axis_index("rep")
        z, y, x = dp // 4, lax.rem(dp // 2, 2), lax.rem(dp, 2)
        self.dp, self.c, self.z, self.y, self.x = dp, c, z, y, x
        self.ma = y * (1 - c) + x * c
        self.mb = x * (1 - c) + y * c
        self.wa, self.wb = 2 - c, 1 + c
        self.to_a = (dp + self.wa * (1 - 2 * self.ma), c)
        self.to_b = (dp + self.wb * (1 - 2 * self.mb), c)
        self.to_z = (lax.rem(dp + 4, 16), c)
        self.from_z = (lax.rem(dp + 12, 16), c)
        self.far_z = (lax.rem(dp + 8, 16), c)
        self.sib = (dp, 1 - c)

    def barrier(self):
        dp = self.dp
        sem = pltpu.get_barrier_semaphore()
        across = (dp - lax.rem(dp, 4) + 3 - lax.rem(dp, 4), self.c)
        for target in (self.to_a, self.to_b, self.to_z, self.from_z, self.far_z, self.sib, across):
            pl.semaphore_signal(sem, inc=1, device_id=target, device_id_type=MESH)
        pl.semaphore_wait(sem, 7)

    def back(self, steps):
        return lax.rem(self.z + 4 - steps, 4)

    def owner(self, z, a, b):
        return 4 * z + self.wa * a + self.wb * b


class Transfers:
    def __init__(self, net, send, recv):
        self.net, self.send, self.recv, self.sent = net, send, recv, []
        self.count = 0

    def push(self, src, dst, slot, to):
        copy = pltpu.make_async_remote_copy(
            src, dst, self.send.at[self.count], self.recv.at[slot], device_id=to, device_id_type=MESH
        )
        copy.start()
        self.sent.append(copy)
        self.count += 1
        return copy

    def sending_done(self, copy):
        copy.wait_send()
        self.sent = [other for other in self.sent if other is not copy]

    def landed(self, dst, slot):
        pltpu.make_async_remote_copy(
            dst, dst, self.send.at[0], self.recv.at[slot], device_id=self.net.sib, device_id_type=MESH
        ).wait_recv()

    def finish(self):
        for copy in self.sent:
            copy.wait_send()


class Gather(Transfers):
    def __init__(self, net, part, buf, send, recv):
        super().__init__(net, send, recv)
        weight, self.part, self.parts, self.order = part
        self.buf = buf
        self.rows, self.cols, self.by_rows, _ = WEIGHTS[weight]

    def span(self, c):
        half = (self.rows if self.by_rows else self.cols) // 2
        size = half // self.parts
        return c * half + self.part * size, size

    def block(self, owner):
        start, size = self.span(self.net.c)
        if self.by_rows:
            return self.buf.at[pl.ds(aligned(owner * self.rows + start, 16), size), :]
        return self.buf.at[pl.ds(aligned(owner * self.rows, 16), self.rows), pl.ds(aligned(start, 128), size)]

    def group(self, z, c):
        start, size = self.span(c)
        if self.by_rows:
            pieces = self.rows // size
            return self.buf.reshape(4, 4, pieces, size, self.cols).at[z, :, c * self.parts + self.part]
        rows = 4 * self.rows
        return self.buf.at[pl.ds(aligned(z * rows, 16), rows), pl.ds(aligned(start, 128), size)]

    def load(self, src, sem):
        start, size = self.span(self.net.c)
        if self.by_rows:
            part = src.at[pl.ds(aligned(start, 16), size), :]
        else:
            part = src.at[:, pl.ds(aligned(start, 128), size)]
        self.copy = pltpu.make_async_copy(part, self.block(self.net.dp), sem)
        self.copy.start()

    def along_z(self, ref, back, other):
        net = self.net
        if back == 0:
            self.push(ref, ref, 2 + other, net.to_z)
            self.push(ref, ref, 6 + other, net.from_z)
        elif back == 1:
            self.push(ref, ref, 4 + other, net.to_z)

    def jobs(self):
        net = self.net
        ma, mb = net.ma, net.mb

        def near(back, other):
            return self.block(net.owner(net.back(back), ma, mb + other * (1 - 2 * mb)))

        def far(back, other):
            return self.block(net.owner(net.back(back), 1 - ma, mb + other * (1 - 2 * mb)))

        def own():
            self.copy.wait()
            ref = near(0, 0)
            self.along_z(ref, 0, 0)
            self.push(ref, ref, 1, net.to_b)
            self.push(ref, ref, 8, net.to_a)

        def relay(back, other):
            def run():
                ref = near(back, other)
                self.landed(ref, back * 2 + other)
                if other == 0 or self.order != "B":
                    self.along_z(ref, back, other)
                if self.order == "B" and other == 0:
                    self.push(ref, ref, back * 2 + 1, net.to_b)
                self.push(ref, ref, 8 + back * 2 + other, net.to_a)

            return run

        def tail(back):
            def run():
                for other in (0, 1):
                    self.landed(far(back, other), 8 + back * 2 + other)
                ref = self.group(net.back(back), net.c)
                self.push(ref, ref, 16 + back, net.sib)

            return run

        def complete():
            for back in range(4):
                self.landed(self.group(net.back(back), 1 - net.c), 16 + back)

        relays = [relay(0, 1)] + [relay(back, other) for back in (1, 3, 2) for other in (0, 1)]
        return [own, *relays, *[tail(back) for back in (0, 1, 3, 2)], complete]


STEPS = (2, 1, 3, 0)


class Scatter(Transfers):
    def __init__(self, net, weight, column, order, refs, stage, send, recv):
        super().__init__(net, send, recv)
        self.order, self.weight, self.done = order, weight, False
        self.rows, self.cols, self.by_rows, _ = WEIGHTS[weight]
        self.g, self.ra, self.rb, self.rz = refs
        self.stage, self.column = stage, column
        self.rh = self.rows // 2 if self.by_rows else self.rows

    def produced(self, back):
        net = self.net
        self.push(self.g.at[net.back(back), 1 - net.ma], self.ra.at[back], back, net.to_a)

    def along_z(self, step, src):
        net = self.net
        self.push(src, self.rz.at[step], 8 + step, net.from_z if step == 1 else net.to_z)

    def add_into(self, dst, terms):
        total = dst[...].astype(FULL)
        for term in terms:
            total += term[...].astype(FULL)
        dst[...] = total.astype(LOW)

    def part_of_stage(self, c):
        if self.by_rows:
            return self.stage.at[pl.ds(aligned(c * self.rh, 16), self.rh), pl.ds(self.column * CHUNK, CHUNK)]
        return self.stage.at[:, pl.ds(aligned(self.first_column(c), 128), CHUNK)]

    def first_column(self, c):
        if self.cols == 3 * FEATURES:
            first, second = IN_COLUMNS[self.column]
            return (first + c * (second - first)) * CHUNK
        return c * (self.cols // 2) + self.column * CHUNK

    def last(self, terms):
        mine = self.part_of_stage(self.net.c)
        total = terms[0][...].astype(FULL)
        for term in terms[1:]:
            total += term[...].astype(FULL)
        mine[...] = total
        self.push(mine, mine, 11, self.net.sib)

    def got(self):
        self.landed(self.part_of_stage(1 - self.net.c), 11)
        self.done = True

    def jobs(self):
        net, g, ra, rb, rz = self.net, self.g, self.ra, self.rb, self.rz
        ma, mb = net.ma, net.mb

        def step_a(s):
            def run():
                back = STEPS[s]
                self.landed(ra.at[back], back)
                terms = [ra.at[back]]
                for k in ((), (), (0,), (1, 2))[s]:
                    self.landed(rz.at[k], 8 + k)
                    terms.append(rz.at[k])
                dst = g.at[net.back(back), ma]
                self.add_into(dst, terms)
                if s < 3:
                    self.along_z(s, dst)
                else:
                    self.push(dst.at[1 - mb], rb.at[0], 4, net.to_b)

            return run

        def final_a():
            self.landed(rb.at[0], 4)
            self.last([g.at[net.z, ma, mb], rb.at[0]])

        def first_b(back):
            def run():
                self.landed(ra.at[back], back)
                dst = g.at[net.back(back), ma]
                self.add_into(dst, [ra.at[back]])
                self.push(dst.at[1 - mb], rb.at[back], 4 + back, net.to_b)

            return run

        def step_b(s):
            def run():
                back = STEPS[s]
                self.landed(rb.at[back], 4 + back)
                terms = [rb.at[back]]
                for k in ((), (), (0,), (1, 2))[s]:
                    self.landed(rz.at[k], 8 + k)
                    terms.append(rz.at[k])
                dst = g.at[net.back(back), ma, mb]
                if s < 3:
                    self.add_into(dst, terms)
                    self.along_z(s, dst)
                else:
                    self.last([dst] + terms)

            return run

        if self.order == "A":
            steps = [step_a(s) for s in range(4)] + [final_a]
        else:
            steps = [first_b(back) for back in STEPS] + [step_b(s) for s in range(4)]
        return steps + [self.got]

    @staticmethod
    def shapes(weight, order):
        rows, _, by_rows, _ = WEIGHTS[weight]
        block = (rows // 2 if by_rows else rows, CHUNK)
        relay = (3,) if order == "B" else (3, 2)
        return [
            pltpu.VMEM((4, 2, 2) + block, LOW),
            pltpu.VMEM((4, 2) + block, LOW),
            pltpu.VMEM((4 if order == "B" else 1,) + block, LOW),
            pltpu.VMEM(relay + block, LOW),
        ]


class SmallSum(Transfers):
    def __init__(self, net, buf, landing, send, recv):
        super().__init__(net, send, recv)
        self.buf, self.landing = buf, landing
        self.place, self.floor = lax.rem(net.dp, 4), net.dp - lax.rem(net.dp, 4)

    def spread(self, first, own, targets):
        ref = self.landing.at[first + own]
        for slot, target in targets:
            self.push(ref, ref, slot, target)

    def gathered(self, first):
        for k in range(1, 4):
            self.landed(self.landing.at[0], first + k)
        return (self.landing[first] + self.landing[first + 1]) + (self.landing[first + 2] + self.landing[first + 3])

    def jobs(self):
        net = self.net

        def start():
            self.push(self.buf.at[0], self.landing.at[0], 0, net.sib)

        def plane():
            self.landed(self.landing.at[0], 0)
            self.landing[1 + self.place] = self.buf[0] + self.landing[0]
            self.spread(
                1, self.place, [(1 + k, (self.floor + lax.rem(self.place + k, 4), net.c)) for k in (1, 2, 3)]
            )

        def line():
            self.landing[5 + net.z] = self.gathered(1)
            self.spread(5, net.z, [(5 + k, (lax.rem(net.dp + 4 * k, 16), net.c)) for k in (1, 2, 3)])

        def last():
            self.buf[1] = self.gathered(5)

        return [start, plane, line, last]


def dot(left, right):
    return jnp.dot(left, right, preferred_element_type=FULL)


def dot_rows(left, right):
    return lax.dot_general(left, right, (((1,), (1,)), ((), ())), preferred_element_type=FULL)


def fold(values):
    return jnp.sum(values.reshape(values.shape[0] // 8, 8, values.shape[1]), axis=0)


def normalised(values):
    centre = values - jnp.mean(values, axis=-1, keepdims=True)
    inverse = lax.rsqrt(jnp.mean(centre * centre, axis=-1, keepdims=True) + EPS)
    return centre * inverse, inverse


BLOCK = 64
ROOT_HALF = 0.7071067811865476
DENSITY = 0.3989422804014327


class Line:
    def __init__(self, ref):
        self.ref = ref

    def __getitem__(self, index):
        cols = slice(None) if index is Ellipsis else index[1]
        return self.ref[cols].reshape(1, -1)


def layer_kernel(
    sizes, tokens_hbm, w_in_hbm, w_out_hbm, w_expand_hbm, w_reduce_hbm, cotangent_hbm,
    first_gain, first_shift, query_value_bias, output_bias, mixer_scale, second_gain, second_shift,
    hidden_bias, return_bias, feed_scale, position_table,
    outputs_hbm, input_grad_hbm, g_in_hbm, g_out_hbm, g_expand_hbm, g_reduce_hbm, small_out,
    w_in, w_out, w_expand, w_reduce,
    stage_in, stage_out, stage_expand, stage_reduce,
    tok, cot, normed_a_t, normed_b_t, blended_t, qkv, place_q, place_k, place_t,
    chances, mixed, branch, middle, act, act_t, act_t_far, slope, g_ret, g_ret_far, g_pre_far,
    g_branch_far, work, small, small_landing, table,
    load_sem, out_sem, gather_send, gather_recv, scatter_send, scatter_recv, swap_send, swap_recv,
    small_send, small_recv, free_sem, *scatter_refs,
):
    net = Net()
    first_gain, first_shift, output_bias, mixer_scale, second_gain, second_shift, hidden_bias, return_bias, feed_scale = map(
        Line,
        (first_gain, first_shift, output_bias, mixer_scale, second_gain, second_shift, hidden_bias, return_bias, feed_scale),
    )
    g_branch = g_ret
    normed = mixed
    c = net.c
    sibling = 1 - c

    weights = [w_in, w_out, w_expand, w_reduce]
    sources = [w_in_hbm, w_out_hbm, w_expand_hbm, w_reduce_hbm]
    jobs = []

    gathers = []
    for i, part in enumerate(PARTS):
        gather = Gather(net, part, weights[part[0]], gather_send.at[i], gather_recv.at[i])
        gather.load(sources[part[0]], load_sem.at[i])
        gathers.append(gather)
        jobs += gather.jobs()
    load_tok = pltpu.make_async_copy(tokens_hbm, tok, load_sem.at[len(PARTS)])
    load_cot = pltpu.make_async_copy(cotangent_hbm, cot, load_sem.at[len(PARTS) + 1])
    load_tok.start()
    load_cot.start()
    net.barrier()

    stages = [stage_in, stage_out, stage_expand, stage_reduce]
    scatters = []
    for i, (weight, column, order) in enumerate(CHUNKS):
        scatters.append(
            Scatter(net, weight, column, order, scatter_refs[4 * i : 4 * i + 4], stages[weight],
                    scatter_send.at[i], scatter_recv.at[i])
        )
    swaps = Transfers(net, swap_send, swap_recv)
    sums = SmallSum(net, small, small_landing, small_send, small_recv)
    for group in scatters + [sums]:
        jobs += group.jobs()

    held = []

    @jobs.append
    def _():
        load_tok.wait()
        load_cot.wait()

        def first_rows(i, carry):
            rows = pl.ds(aligned(i * BLOCK, BLOCK), BLOCK)
            unit, _ = normalised(tok[rows, :].astype(FULL))
            normed[rows, :] = (unit * first_gain[...] + first_shift[...]).astype(LOW)
            returned_grad = (cot[rows, :].astype(FULL) * feed_scale[...]).astype(LOW)
            g_ret[rows, :] = returned_grad
            return carry + fold(returned_grad.astype(FULL))

        total = lax.fori_loop(0, SLOTS // BLOCK, first_rows, jnp.zeros((8, FEATURES), FULL), unroll=True)
        small[0] = jnp.zeros_like(small[0])
        small[0, 12:13, :] = jnp.sum(total, axis=0, keepdims=True)
        held.append(swaps.push(g_ret, g_ret_far, 0, net.sib))

    def turn(source, target):
        for j in range(FEATURES // 128):
            target[0, j * 128 : (j + 1) * 128, :] = source[:, j * 128 : (j + 1) * 128].T

    @jobs.append
    def _():
        turn(normed, normed_a_t)
        swaps.push(normed_a_t.at[0], normed_a_t.at[1], 1, net.sib)

    lane128 = lax.broadcasted_iota(jnp.int32, (128, 128), 1)
    row128 = lax.broadcasted_iota(jnp.int32, (128, 128), 0)
    height, width = sizes[0, 0], sizes[0, 1]
    width_f = width.astype(FULL)
    live = (height * width).astype(FULL)

    def grid_place(slot):
        row = jnp.floor((slot + 0.5) / width_f)
        return row, slot - row * width_f

    @jobs.append
    def _():
        slot = lax.broadcasted_iota(jnp.int32, (SLOTS, 128), 0).astype(FULL)
        lane = lax.broadcasted_iota(jnp.int32, (SLOTS, 128), 1).astype(FULL)
        row, col = grid_place(slot)
        hit = jnp.where(jnp.where(lane < GRID, row, col + GRID) == lane, 1.0, 0.0)
        place_q[...] = hit.astype(LOW)
        place_k[...] = jnp.where(slot < live, hit, jnp.where(lane == GRID - 1, 1.0, 0.0)).astype(LOW)
        slot = lax.broadcasted_iota(jnp.int32, (128, SLOTS), 1).astype(FULL)
        lane = lax.broadcasted_iota(jnp.int32, (128, SLOTS), 0).astype(FULL)
        row, col = grid_place(slot)
        hit = jnp.where(lane < GRID, GRID - 1 - row, 2 * GRID - 1 - col) == lane
        place_t[...] = jnp.where(hit, 1.0, 0.0).astype(LOW)
        mirror = jnp.where(row128 + lane128 == 2 * GRID - 2, 1.0, 0.0).astype(LOW)
        for part in range(2):
            low_table = position_table[:, part, :].astype(LOW)
            table[12 * part : 12 * part + 12, :] = dot(low_table, mirror[: 2 * GRID - 1, :])

    def project(j):
        cols = slice(j * WIDE, (j + 1) * WIDE)
        part = dot(normed[...], w_in[:, cols])
        inner = slice((j % 3) * WIDE, (j % 3 + 1) * WIDE)
        if j < 3:
            part = (part + query_value_bias[0:1, inner]) * 0.125
        elif j >= 6:
            part = part + query_value_bias[1:2, inner]
        qkv[:, cols] = part.astype(LOW)

    for j in range(9):
        jobs.append(functools.partial(project, j))

    half_lane = lax.broadcasted_iota(jnp.int32, (SLOTS, 128), 1)
    no_key = (lane128 == GRID - 1) & (row128 < GRID) & (jnp.full((128, 128), live) < SLOTS)
    spans = ((0, 256), (256, SLOTS))

    def only(values, e):
        keep = half_lane < 64 if e == 0 else half_lane >= 64
        return jnp.where(keep, values, jnp.zeros_like(values))

    def bias_table(head):
        rows_part = jnp.broadcast_to(table[head : head + 1, :], (GRID, 128))
        cols_part = jnp.broadcast_to(table[12 + head : 13 + head, :], (GRID, 128))
        both = jnp.concatenate(
            [
                pltpu.roll(rows_part, 65, 1, stride=1, stride_axis=0),
                pltpu.roll(cols_part, 1, 1, stride=1, stride_axis=0),
            ],
            axis=0,
        )
        both = jnp.where(lane128 // GRID == row128 // GRID, both, 0.0)
        return jnp.where(no_key, MASKED, both).astype(LOW)

    boards = (work, branch)

    def score(head):
        pair, e = head // 2, head % 2
        keys = jnp.concatenate([qkv[:, 768 + pair * 128 : 896 + pair * 128], place_k[...]], axis=1)
        bias = dot(place_q[...], bias_table(head)).astype(LOW)
        asks = jnp.concatenate([only(qkv[:, pair * 128 : (pair + 1) * 128], e), bias], axis=1)
        boards[e][:, :SLOTS] = dot_rows(keys, asks)

    def attend(head):
        pair, e = head // 2, head % 2
        cols = slice(pair * 128, (pair + 1) * 128)
        if head == 0:
            score(0)
        if head < HEADS - 1:
            score(head + 1)
        for lo, hi in spans:
            scores = boards[e][:, lo:hi]
            raised = jnp.exp(scores - jnp.max(scores, axis=0, keepdims=True))
            chances[head, :, lo:hi] = (raised * (1.0 / jnp.sum(raised, axis=0, keepdims=True))).astype(LOW)
        v_head = qkv[:, 1536 + pair * 128 : 1664 + pair * 128].T[e * 64 : (e + 1) * 64, :]
        blended_t[0, head * 64 : (head + 1) * 64, :] = dot(v_head, chances[head]).astype(LOW)
        if e == 1:
            mixed[:, cols] = blended_t[0, cols, :].T
        if head == HEADS - 1:
            swaps.push(blended_t.at[0], blended_t.at[1], 2, net.sib)

    for head in range(HEADS):
        jobs.append(functools.partial(attend, head))

    @jobs.append
    def _():
        for j in range(3):
            cols = slice(j * WIDE, (j + 1) * WIDE)
            branch[:, cols] = dot(mixed[...], w_out[:, cols]) + output_bias[:, cols]

    @jobs.append
    def _():
        def middle_rows(i, carry):
            rows = pl.ds(aligned(i * BLOCK, BLOCK), BLOCK)
            mid = tok[rows, :].astype(FULL) + mixer_scale[...] * branch[rows, :]
            middle[rows, :] = mid
            unit, _ = normalised(mid)
            normed[rows, :] = (unit * second_gain[...] + second_shift[...]).astype(LOW)
            return carry

        lax.fori_loop(0, SLOTS // BLOCK, middle_rows, 0, unroll=True)
        turn(normed, normed_b_t)
        swaps.push(normed_b_t.at[0], normed_b_t.at[1], 3, net.sib)

    act_blocks = act_t.reshape(16, 2, 96, SLOTS)

    def hidden(j):
        cols = slice(j * WIDE, (j + 1) * WIDE)
        pre = dot(normed[...], w_expand[:, cols]) + hidden_bias[:, cols]
        share = 0.5 + 0.5 * lax.erf(pre * ROOT_HALF)
        active = (pre * share).astype(LOW)
        act[:, cols] = active
        slope[:, cols] = (share + pre * (DENSITY * jnp.exp(-0.5 * pre * pre))).astype(LOW)
        for k in range(2):
            act_t[j * WIDE + k * 128 : j * WIDE + (k + 1) * 128, :] = active[:, k * 128 : (k + 1) * 128].T

    for j in (0, 1, 2, 6, 7, 8, 3, 4, 5, 9, 10, 11):
        jobs.append(functools.partial(hidden, j))

    @jobs.append
    def _():
        held.append(swaps.push(act_blocks.at[:, sibling], act_t_far, 4, net.sib))

    def place_of(owner):
        oy, ox = owner // 2, owner % 2
        return oy * (1 - c) + ox * c, ox * (1 - c) + oy * c

    def weight_grad(index, order, left, left_far, right, right_far, chunks=1):
        back = STEPS[order]
        z = net.back(back)
        tile = (dot(left(z), right) + dot(left_far(z), right_far)).astype(LOW)
        for chunk in range(chunks):
            scatter = scatters[index + chunk]
            for owner in range(4):
                pa, pb = place_of(owner)
                rows = slice(owner * scatter.rh, (owner + 1) * scatter.rh)
                scatter.g[z, pa, pb] = tile[rows, chunk * CHUNK : (chunk + 1) * CHUNK]
            scatter.produced(back)

    def rows_of(ref, slot):
        return lambda z: ref[slot, pl.ds(aligned(z * 192, 64), 192), :]

    def grad_reduce(j, order):
        cols = slice(j * CHUNK, (j + 1) * CHUNK)
        if (j, order) == (0, 0):
            swaps.landed(g_ret_far, 0)
            swaps.landed(act_t_far, 4)
        weight_grad(
            j, order,
            lambda z: act_blocks[pl.ds(4 * z, 4), c].reshape(384, SLOTS),
            lambda z: act_t_far[pl.ds(4 * z, 4)].reshape(384, SLOTS),
            g_ret[:, cols], g_ret_far[:, cols],
        )

    for j in range(2):
        for order in range(4):
            jobs.append(functools.partial(grad_reduce, j, order))

    def grad_hidden(j):
        half = sibling if j < 6 else c
        cols = pl.ds(aligned(half * 1536 + (j % 6) * WIDE, 128), WIDE)
        part = (dot_rows(g_ret[...], w_reduce[cols, :]) * slope[:, cols].astype(FULL)).astype(LOW)
        slope[:, cols] = part
        summed = jnp.sum(part.astype(FULL), axis=0, keepdims=True)
        small[0, pl.ds(8 + 2 * half + (j % 6) // 3, 1), (j % 3) * WIDE : (j % 3 + 1) * WIDE] = summed
        if j == 5:
            swaps.push(slope.at[:, pl.ds(aligned(sibling * 1536, 128), 1536)], g_pre_far, 5, net.sib)

    for j in range(12):
        jobs.append(functools.partial(grad_hidden, j))

    def grad_expand(j, order):
        if (j, order) == (0, 0):
            swaps.landed(normed_b_t.at[1], 3)
            swaps.landed(g_pre_far, 5)
        weight_grad(
            2 + 2 * j, order, rows_of(normed_b_t, 0), rows_of(normed_b_t, 1),
            slope[:, pl.ds(aligned(c * 1536 + 2 * j * CHUNK, 128), 2 * CHUNK)],
            g_pre_far[:, 2 * j * CHUNK : 2 * (j + 1) * CHUNK], 2,
        )
        if (j, order) == (1, 3):
            pl.semaphore_signal(free_sem, inc=1, device_id=net.sib, device_id_type=MESH)

    def g_qkv_far(part):
        return g_pre_far.at[:, part * CHUNK : (part + 1) * CHUNK]

    for j in range(2):
        for order in range(4):
            jobs.append(functools.partial(grad_expand, j, order))

    def grad_normed_b(j):
        cols = slice(j * WIDE, (j + 1) * WIDE)
        work[:, cols] = dot_rows(slope[...], w_expand[cols, :])

    for j in range(3):
        jobs.append(functools.partial(grad_normed_b, j))

    zero = jnp.zeros((8, FEATURES), FULL)

    @jobs.append
    def _():
        swaps.sending_done(held.pop(0))

        def second_back(i, carry):
            gain_sum, shift_sum, mixer_sum, bias_sum = carry
            rows = pl.ds(aligned(i * BLOCK, BLOCK), BLOCK)
            unit, inverse = normalised(middle[rows, :])
            grad = work[rows, :]
            gain_sum += fold(grad * unit)
            shift_sum += fold(grad)
            scaled = grad * second_gain[...]
            moved = scaled - jnp.mean(scaled, axis=-1, keepdims=True)
            moved -= unit * jnp.mean(scaled * unit, axis=-1, keepdims=True)
            grad_middle = cot[rows, :].astype(FULL) + inverse * moved
            work[rows, :] = grad_middle
            mixer_sum += fold(grad_middle * branch[rows, :])
            grad_branch = (grad_middle * mixer_scale[...]).astype(LOW)
            g_branch[rows, :] = grad_branch
            bias_sum += fold(grad_branch.astype(FULL))
            return gain_sum, shift_sum, mixer_sum, bias_sum

        for line, total in zip((6, 7, 5, 4), lax.fori_loop(0, SLOTS // BLOCK, second_back, (zero,) * 4, unroll=True)):
            small[0, line : line + 1, :] = jnp.sum(total, axis=0, keepdims=True)
        swaps.push(g_branch.at[:, pl.ds(aligned(sibling * CHUNK, 128), CHUNK)], g_branch_far, 6, net.sib)

    @jobs.append
    def _():
        for j in range(3):
            cols = slice(j * WIDE, (j + 1) * WIDE)
            mixed[:, cols] = dot_rows(g_branch[...], w_out[cols, :]).astype(LOW)

    def grad_out(order):
        if order == 0:
            swaps.landed(blended_t.at[1], 2)
            swaps.landed(g_branch_far, 6)
        weight_grad(
            6, order, rows_of(blended_t, 0), rows_of(blended_t, 1),
            g_branch[:, pl.ds(aligned(c * CHUNK, 128), CHUNK)], g_branch_far[...],
        )

    for order in range(4):
        jobs.append(functools.partial(grad_out, order))

    lane64 = lax.broadcasted_iota(jnp.int32, (GRID, 128), 1)

    grad_boards = (act_t.at[0:SLOTS, :], act_t.at[SLOTS : 2 * SLOTS, :])
    parts = {}

    def grad_chance(head):
        pair, e = head // 2, head % 2
        value_cols = slice(1536 + pair * 128, 1664 + pair * 128)
        g_head = only(mixed[:, pair * 128 : (pair + 1) * 128], e)
        branch[:, :SLOTS] = dot_rows(qkv[:, value_cols], g_head)

    def attend_back(head):
        pair, e = head // 2, head % 2
        cols = slice(pair * 128, (pair + 1) * 128)
        key_cols = slice(768 + pair * 128, 896 + pair * 128)
        value_cols = slice(1536 + pair * 128, 1664 + pair * 128)
        board = grad_boards[e]
        if head == 0:
            swaps.sending_done(held.pop())
            grad_chance(0)
        for lo, hi in spans:
            share = chances[head, :, lo:hi].astype(FULL)
            weighed = share * branch[:, lo:hi]
            board[:, lo:hi] = (weighed - share * jnp.sum(weighed, axis=0, keepdims=True)).astype(LOW)
        if head < HEADS - 1:
            grad_chance(head + 1)
        asks = jnp.concatenate([only(qkv[:, cols], e), place_q[...]], axis=1)
        across = dot(board[...], asks)
        grad_values = dot(chances[head], only(mixed[:, cols], e))
        k_head = qkv[:, key_cols].T[e * 64 : (e + 1) * 64, :]
        grad_queries = dot(k_head, board[...]).astype(LOW).astype(FULL) * 0.125
        marks = across[:, 128:]
        high = marks.astype(LOW)
        low = (marks - high.astype(FULL)).astype(LOW)
        pairs = dot(place_t[...], jnp.concatenate([high, low], axis=1))
        pairs = pairs[:, :128] + pairs[:, 128:]
        rows_part = jnp.where(lane64 < GRID, pairs[:GRID, :], 0.0)
        cols_part = jnp.where(lane64 >= GRID, pairs[GRID:, :], 0.0)
        rows_part = pltpu.roll(rows_part, 0, 1, stride=1, stride_axis=0)
        cols_part = pltpu.roll(cols_part, 64, 1, stride=1, stride_axis=0)
        for line, part in ((head, rows_part), (12 + head, cols_part)):
            spot = (line % 6) * 128
            small[0, 14 + line // 6 : 15 + line // 6, spot : spot + 128] = jnp.sum(part, axis=0, keepdims=True)
        if e == 0:
            parts[pair] = grad_queries, across[:, :128], grad_values
            return
        first_queries, first_keys, first_values = parts.pop(pair)
        grad_queries = jnp.concatenate([first_queries, grad_queries], axis=0).T.astype(LOW)
        grad_values = (first_values + grad_values).astype(LOW)
        qkv[:, cols] = grad_queries
        qkv[:, key_cols] = (first_keys + across[:, :128]).astype(LOW)
        qkv[:, value_cols] = grad_values
        small[0, 2:3, cols] = jnp.sum(grad_queries.astype(FULL), axis=0, keepdims=True)
        small[0, 3:4, cols] = jnp.sum(grad_values.astype(FULL), axis=0, keepdims=True)
        for part in (0,) if pair == 2 else (1, 2) if pair == 5 else ():
            first = aligned(scatters[7 + part].first_column(sibling), 128)
            if part == 0:
                pl.semaphore_wait(free_sem, 1)
            swaps.push(qkv.at[:, pl.ds(first, CHUNK)], g_qkv_far(part), 7 + part, net.sib)

    for head in range(HEADS):
        jobs.append(functools.partial(attend_back, head))

    def grad_in(j, order):
        parts = (0,) if j == 0 else (1, 2)
        if (j, order) == (0, 0):
            swaps.landed(normed_a_t.at[1], 1)
        if order == 0:
            for part in parts:
                swaps.landed(g_qkv_far(part), 7 + part)
        own = [qkv[:, pl.ds(aligned(scatters[7 + part].first_column(c), 128), CHUNK)] for part in parts]
        far = [g_qkv_far(part)[...] for part in parts]
        weight_grad(
            7 + j, order, rows_of(normed_a_t, 0), rows_of(normed_a_t, 1),
            jnp.concatenate(own, axis=1), jnp.concatenate(far, axis=1), len(parts),
        )

    for j in range(2):
        for order in range(4):
            jobs.append(functools.partial(grad_in, j, order))

    def grad_normed_a(j):
        cols = slice(j * WIDE, (j + 1) * WIDE)
        branch[:, cols] = dot_rows(qkv[...], w_in[cols, :])

    for j in range(3):
        jobs.append(functools.partial(grad_normed_a, j))

    save_grad = pltpu.make_async_copy(work, input_grad_hbm, out_sem.at[0])
    save_out = pltpu.make_async_copy(mixed, outputs_hbm, out_sem.at[1])

    @jobs.append
    def _():
        def first_back(i, carry):
            gain_sum, shift_sum = carry
            rows = pl.ds(aligned(i * BLOCK, BLOCK), BLOCK)
            unit, inverse = normalised(tok[rows, :].astype(FULL))
            grad = branch[rows, :]
            gain_sum += fold(grad * unit)
            shift_sum += fold(grad)
            scaled = grad * first_gain[...]
            moved = scaled - jnp.mean(scaled, axis=-1, keepdims=True)
            moved -= unit * jnp.mean(scaled * unit, axis=-1, keepdims=True)
            work[rows, :] = work[rows, :] + inverse * moved
            return gain_sum, shift_sum

        for line, total in zip((0, 1), lax.fori_loop(0, SLOTS // BLOCK, first_back, (zero,) * 2, unroll=True)):
            small[0, line : line + 1, :] = jnp.sum(total, axis=0, keepdims=True)
        save_grad.start()

    def finish_rows(j):
        cols = slice(j * WIDE, (j + 1) * WIDE)
        returned = dot(act[...], w_reduce[:, cols]) + return_bias[:, cols]
        mixed[:, cols] = (middle[:, cols] + feed_scale[:, cols] * returned).astype(LOW)
        small[0, 13:14, cols] = jnp.sum(cot[:, cols].astype(FULL) * returned, axis=0, keepdims=True)
        if j == 2:
            save_out.start()

    for j in range(3):
        jobs.append(functools.partial(finish_rows, j))

    saves = {}
    for key in PLAN:
        jobs[key]()
        for weight, target in enumerate((g_in_hbm, g_out_hbm, g_expand_hbm, g_reduce_hbm)):
            if weight not in saves and all(scatter.done for scatter in scatters if scatter.weight == weight):
                saves[weight] = pltpu.make_async_copy(stages[weight], target, out_sem.at[2 + weight])
                saves[weight].start()
    small_out[...] = small[1]
    for group in gathers + scatters + [swaps, sums]:
        group.finish()
    for save in [save_grad, save_out, *saves.values()]:
        save.wait()


PLAN = (
    0, 154, 155, 13, 156, 1, 2, 14, 4, 26, 8, 15, 17, 3, 21, 6, 5, 16, 18, 27, 28, 30, 9, 19, 20, 7, 39, 29, 10, 22,
    31, 23, 34, 32, 41, 24, 11, 25, 43, 40, 33, 12, 157, 158, 35, 159, 160, 161, 36, 162, 45, 163, 164, 165, 166, 167,
    42, 168, 169, 47, 52, 44, 170, 37, 171, 172, 65, 48, 173, 38, 46, 174, 53, 175, 176, 54, 49, 177, 178, 56, 66,
    179, 50, 67, 180, 60, 181, 182, 55, 69, 183, 184, 185, 57, 58, 51, 186, 187, 188, 68, 73, 189, 190, 191, 61, 70,
    192, 62, 71, 59, 72, 74, 75, 193, 194, 195, 63, 196, 76, 197, 198, 199, 64, 200, 77, 201, 202, 203, 204, 78, 205,
    206, 207, 208, 209, 79, 210, 211, 212, 221, 222, 223, 213, 214, 84, 80, 215, 216, 85, 217, 218, 219, 220, 224,
    225, 90, 230, 96, 86, 91, 226, 227, 97, 228, 229, 231, 81, 232, 233, 234, 102, 111, 235, 103, 236, 112, 104, 92,
    242, 243, 98, 244, 105, 245, 237, 238, 117, 87, 118, 239, 240, 82, 241, 106, 107, 83, 250, 123, 113, 124, 251,
    125, 246, 247, 126, 248, 88, 93, 127, 128, 249, 99, 89, 252, 132, 253, 141, 119, 133, 254, 108, 142, 255, 143,
    134, 94, 256, 150, 114, 144, 135, 100, 95, 129, 151, 145, 136, 137, 101, 146, 120, 109, 115, 110, 116, 130, 147,
    131, 138, 152, 121, 122, 148, 139, 149, 140, 153,
)


def one_kernel(
    tokens, project_in, project_out, expand_weight, reduce_weight, first_gain, first_shift, query_value_bias,
    output_bias, mixer_scale, second_gain, second_shift, hidden_bias, return_bias, feed_scale, position_table,
    image_sizes, cotangent,
):
    vector = lambda v: v
    table = jnp.transpose(position_table, (2, 0, 1))
    anywhere = pl.BlockSpec(memory_space=pl.ANY)
    vmem = pl.BlockSpec(memory_space=pltpu.VMEM)
    low = lambda *shape: pltpu.VMEM(shape, LOW)
    full = lambda *shape: pltpu.VMEM(shape, FULL)
    dma = lambda *shape: pltpu.SemaphoreType.DMA(shape)
    like = jax.ShapeDtypeStruct
    scratch = [low(16 * w[0], w[1]) for w in WEIGHTS]
    scratch += [full(w[0], w[1]) for w in WEIGHTS]
    T, D, F = SLOTS, FEATURES, HIDDEN
    scratch += [
        low(T, D), low(T, D), low(2, D, T), low(2, D, T), low(2, D, T), low(T, 3 * D),
        low(T, 128), low(T, 128), low(128, T), low(HEADS, T, T), low(T, D), full(T, D), full(T, D),
        low(T, F), low(F, T), low(16, 96, T), low(T, F), low(T, D), low(T, D), low(T, F // 2),
        low(T, D // 2), full(T, D), full(2, 24, D), full(9, 24, D), full(24, 128),
        dma(len(PARTS) + 2), dma(6), dma(len(PARTS), 24), dma(len(PARTS), 20), dma(len(CHUNKS), 12), dma(len(CHUNKS), 12), dma(10), dma(10),
        dma(7), dma(9), pltpu.SemaphoreType.REGULAR,
    ]
    for weight, _, order in CHUNKS:
        scratch += Scatter.shapes(weight, order)
    results = pl.pallas_call(
        layer_kernel,
        out_shape=[
            like((T, D), LOW), like((T, D), FULL), like((48, 3 * D), FULL), like((48, D), FULL), like((48, F), FULL),
            like((192, D), FULL), like((24, D), FULL),
        ],
        in_specs=[pl.BlockSpec(memory_space=pltpu.SMEM)] + [anywhere] * 6 + [vmem] * 11,
        out_specs=[anywhere] * 6 + [vmem],
        scratch_shapes=scratch,
        compiler_params=pltpu.CompilerParams(
            collective_id=0, has_side_effects=True, vmem_limit_bytes=VMEM_BYTES
        ),
    )(
        image_sizes, tokens, project_in, project_out, expand_weight, reduce_weight, cotangent, vector(first_gain),
        vector(first_shift), query_value_bias, vector(output_bias), vector(mixer_scale), vector(second_gain),
        vector(second_shift), vector(hidden_bias), vector(return_bias), vector(feed_scale), table,
    )
    vectors = [(D,), (D,), (2, D), (D,), (D,), (D,), (D,), (F,), (D,), (D,), (HEADS, 2, 2 * GRID - 1)]
    handed = pl.pallas_call(
        handout,
        out_shape=[like(r.shape, r.dtype) for r in results[:6]] + [like(v, FULL) for v in vectors],
        in_specs=[anywhere] * 6 + [vmem],
        out_specs=[anywhere] * 6 + [vmem] * 11,
        scratch_shapes=[pltpu.VMEM(r.shape, r.dtype) for r in results[:6]] + [dma(2, 6)],
    )(*results)
    return (*handed[:16], jnp.transpose(handed[16], (1, 2, 0)))


def handout(*refs):
    large, small, saved, outs, held, sems = refs[:6], refs[6], refs[7:13], refs[13:24], refs[24:30], refs[30]
    loads = [pltpu.make_async_copy(large[i], held[i], sems.at[0, i]) for i in range(6)]
    copies = [pltpu.make_async_copy(held[i], saved[i], sems.at[1, i]) for i in range(6)]
    for load in loads:
        load.start()
    for load, copy in zip(loads, copies):
        load.wait()
        copy.start()
    for line, out in ((0, 0), (1, 1), (4, 3), (5, 4), (6, 5), (7, 6), (12, 8), (13, 9)):
        outs[out][...] = small[line, :]
    outs[2][...] = small[2:4, :]
    for k in range(4):
        outs[7][k * FEATURES : (k + 1) * FEATURES] = small[8 + k, :]
    for n in range(24):
        line = small[14 + n // 6 : 15 + n // 6, (n % 6) * 128 : (n % 6) * 128 + 2 * GRID - 1]
        outs[10][n % 12, n // 12 : n // 12 + 1, :] = line
    for copy in copies:
        copy.wait()


VMEM_BYTES = 64 * 2**20


def solution(mesh):
    placed = (
        P(("dp", "rep"), None),
        P("dp", None),
        P("dp", None),
        P("dp", None),
        P("dp", None),
        P(),
        P(),
        P(),
        P(),
        P(),
        P(),
        P(),
        P(),
        P(),
        P(),
        P(),
        P(("dp", "rep"), None),
        P(("dp", "rep"), None),
    )
    return jax.shard_map(
        one_kernel if tuple(mesh.shape.values()) == (16, 2) else shards,
        mesh=mesh,
        in_specs=placed,
        out_specs=(
            P(("dp", "rep"), None),
            P(("dp", "rep"), None),
            P("dp", None),
            P("dp", None),
            P("dp", None),
            P("dp", None),
            P(),
            P(),
            P(),
            P(),
            P(),
            P(),
            P(),
            P(),
            P(),
            P(),
            P(),
        ),
        check_vma=False,
    )
```

```python
import functools

import jax
import jax.numpy as jnp
from jax import lax
from jax.experimental import pallas as pl
from jax.experimental.pallas import tpu as pltpu
from jax.sharding import PartitionSpec as P

HEADS = 12
HEAD = 64
GRID = 64


EPS = 1e-06
MASKED = -1000000000.0


def layer_norm(values, gain, shift):
    centre = values - jnp.mean(values, axis=-1, keepdims=True)
    spread = jnp.mean(centre * centre, axis=-1, keepdims=True)
    return centre * lax.rsqrt(spread + EPS) * gain + shift


def gelu_exact(values):
    return jax.nn.gelu(values, approximate=False)


def shift_onehot(side):
    first_axis = lax.broadcasted_iota(jnp.int32, (side, side, 2 * side - 1), 0)
    second_axis = lax.broadcasted_iota(jnp.int32, (side, side, 2 * side - 1), 1)
    third_axis = lax.broadcasted_iota(jnp.int32, (side, side, 2 * side - 1), 2)
    return (first_axis - second_axis + side - 1 == third_axis).astype(jnp.float32)


def position_bias(shift_part, picks):
    between = jnp.einsum("tijh,tkj->tihk", shift_part, picks, preferred_element_type=jnp.float32)
    return jnp.einsum(
        "tqi,tihk->hqk", picks, between.astype(jnp.bfloat16), preferred_element_type=jnp.float32
    )


def group_scores(query_part, key_part, shift_part, picks, usable):
    scores = jnp.einsum("qhd,khd->hqk", query_part, key_part, preferred_element_type=jnp.float32)
    scores = scores + position_bias(shift_part, picks)
    return jnp.where(usable[None, None, :], scores, MASKED)


def attend_group(packed, picks, usable):
    query_part, key_part, value_part, shift_part = packed
    scores = group_scores(query_part, key_part, shift_part, picks, usable)
    highest = jnp.max(scores, axis=-1, keepdims=True)
    weights_raw = jnp.exp(scores - highest)
    totals = jnp.sum(weights_raw, axis=-1, keepdims=True)
    chances = (weights_raw / totals).astype(jnp.bfloat16)
    blended = jnp.einsum("hqk,khd->qhd", chances, value_part, preferred_element_type=jnp.float32)
    return (blended.astype(jnp.bfloat16), (highest + jnp.log(totals))[..., 0])


def attend_back(packed, picks, usable):
    query_part, key_part, value_part, grad_part, logsums, shift_part = packed
    scores = group_scores(query_part, key_part, shift_part, picks, usable)
    chances = jnp.exp(scores - logsums[..., None])
    grad_chance = jnp.einsum(
        "qhd,khd->hqk", grad_part, value_part, preferred_element_type=jnp.float32
    )
    row_dot = jnp.sum(chances * grad_chance, axis=-1, keepdims=True)
    grad_scores = (chances * (grad_chance - row_dot)).astype(jnp.bfloat16)
    grad_query = jnp.einsum(
        "hqk,khd->qhd", grad_scores, key_part, preferred_element_type=jnp.float32
    )
    grad_key = jnp.einsum(
        "hqk,qhd->khd", grad_scores, query_part, preferred_element_type=jnp.float32
    )
    grad_value = jnp.einsum(
        "hqk,qhd->khd", chances.astype(jnp.bfloat16), grad_part, preferred_element_type=jnp.float32
    )
    across = jnp.einsum("hqk,tkj->thqj", grad_scores, picks, preferred_element_type=jnp.float32)
    grad_shift = jnp.einsum(
        "tqi,thqj->tijh", picks.astype(jnp.float32), across, precision=lax.Precision.HIGHEST
    )
    return (
        grad_query.astype(jnp.bfloat16),
        grad_key.astype(jnp.bfloat16),
        grad_value.astype(jnp.bfloat16),
        grad_shift,
    )


def shards(
    tokens,
    project_in,
    project_out,
    expand_weight,
    reduce_weight,
    first_gain,
    first_shift,
    query_value_bias,
    output_bias,
    mixer_scale,
    second_gain,
    second_shift,
    hidden_bias,
    return_bias,
    feed_scale,
    position_table,
    image_sizes,
    cotangent,
):
    length = tokens.shape[0]
    width_model = tokens.shape[1]
    head_count = HEADS
    per_group = 4
    groups = head_count // per_group
    full_in, full_out, full_expand, full_reduce = (
        lax.all_gather(project_in, "dp", axis=0, tiled=True),
        lax.all_gather(project_out, "dp", axis=0, tiled=True),
        lax.all_gather(expand_weight, "dp", axis=0, tiled=True),
        lax.all_gather(reduce_weight, "dp", axis=0, tiled=True),
    )
    inputs = tokens.astype(jnp.float32)
    normed_a, first_back = jax.vjp(layer_norm, inputs, first_gain, first_shift)
    normed_a_low = normed_a.astype(jnp.bfloat16)
    projected = jnp.dot(normed_a_low, full_in, preferred_element_type=jnp.float32)
    queries = ((projected[:, :width_model] + query_value_bias[0]) * HEAD ** (-0.5)).astype(
        jnp.bfloat16
    )
    keys_low = projected[:, width_model : 2 * width_model].astype(jnp.bfloat16)
    values_low = (projected[:, 2 * width_model :] + query_value_bias[1]).astype(jnp.bfloat16)
    shift_table = shift_onehot(GRID)
    shifts = jnp.einsum(
        "ija,tah->tijh",
        shift_table.astype(jnp.bfloat16),
        position_table.astype(jnp.bfloat16),
        preferred_element_type=jnp.float32,
    ).astype(jnp.bfloat16)
    shifts_grouped = shifts.reshape(2, GRID, GRID, groups, per_group).transpose(3, 0, 1, 2, 4)
    places = jnp.arange(length, dtype=jnp.int32)
    height = image_sizes[0, 0]
    width_image = image_sizes[0, 1]
    grid_iota = jnp.arange(GRID, dtype=jnp.int32)
    picks = jnp.stack(
        [
            (places // width_image)[:, None] == grid_iota[None, :],
            (places % width_image)[:, None] == grid_iota[None, :],
        ]
    ).astype(jnp.bfloat16)
    usable = places < height * width_image

    def split_heads(matrix):
        return matrix.reshape(length, groups, per_group, HEAD).transpose(1, 0, 2, 3)

    def join_heads(blocks):
        return blocks.transpose(1, 0, 2, 3).reshape(length, width_model)

    query_groups = split_heads(queries)
    key_groups = split_heads(keys_low)
    value_groups = split_heads(values_low)
    blended_groups, logsums = lax.map(
        lambda packed: attend_group(packed, picks, usable),
        (query_groups, key_groups, value_groups, shifts_grouped),
    )
    blended = join_heads(blended_groups)
    branch = jnp.dot(blended, full_out, preferred_element_type=jnp.float32) + output_bias
    middle = inputs + mixer_scale * branch
    normed_b, second_back = jax.vjp(layer_norm, middle, second_gain, second_shift)
    normed_b_low = normed_b.astype(jnp.bfloat16)
    preact = jnp.dot(normed_b_low, full_expand, preferred_element_type=jnp.float32) + hidden_bias
    activated, gelu_back = jax.vjp(gelu_exact, preact)
    activated_low = activated.astype(jnp.bfloat16)
    returned = jnp.dot(activated_low, full_reduce, preferred_element_type=jnp.float32) + return_bias
    outputs = middle + feed_scale * returned
    back_in, back_out, back_expand, back_reduce = (
        lax.all_gather(project_in, "dp", axis=0, tiled=True),
        lax.all_gather(project_out, "dp", axis=0, tiled=True),
        lax.all_gather(expand_weight, "dp", axis=0, tiled=True),
        lax.all_gather(reduce_weight, "dp", axis=0, tiled=True),
    )
    upstream = cotangent.astype(jnp.float32)
    grad_feed_scale = jnp.sum(upstream * returned, axis=0)
    grad_returned = (upstream * feed_scale).astype(jnp.bfloat16)
    grad_return_bias = jnp.sum(grad_returned.astype(jnp.float32), axis=0)
    grad_reduce = jnp.einsum(
        "tf,td->fd", activated_low, grad_returned, preferred_element_type=jnp.float32
    )
    grad_activated = jnp.einsum(
        "td,fd->tf", grad_returned, back_reduce, preferred_element_type=jnp.float32
    )
    grad_preact = gelu_back(grad_activated)[0].astype(jnp.bfloat16)
    grad_hidden_bias = jnp.sum(grad_preact.astype(jnp.float32), axis=0)
    grad_expand = jnp.einsum(
        "td,tf->df", normed_b_low, grad_preact, preferred_element_type=jnp.float32
    )
    grad_normed_b = jnp.einsum(
        "tf,df->td", grad_preact, back_expand, preferred_element_type=jnp.float32
    )
    grad_from_norm, grad_second_gain, grad_second_shift = second_back(grad_normed_b)
    grad_middle = upstream + grad_from_norm
    grad_mixer_scale = jnp.sum(grad_middle * branch, axis=0)
    grad_branch = (grad_middle * mixer_scale).astype(jnp.bfloat16)
    grad_output_bias = jnp.sum(grad_branch.astype(jnp.float32), axis=0)
    grad_project_out = jnp.einsum(
        "td,te->de", blended, grad_branch, preferred_element_type=jnp.float32
    )
    grad_blended = jnp.einsum(
        "te,de->td", grad_branch, back_out, preferred_element_type=jnp.float32
    ).astype(jnp.bfloat16)
    grad_query_groups, grad_key_groups, grad_value_groups, grad_shift_groups = lax.map(
        lambda packed: attend_back(packed, picks, usable),
        (
            query_groups,
            key_groups,
            value_groups,
            split_heads(grad_blended),
            logsums,
            shifts_grouped,
        ),
    )
    grad_queries = join_heads(grad_query_groups) * HEAD ** (-0.5)
    grad_keys = join_heads(grad_key_groups)
    grad_values = join_heads(grad_value_groups)
    grad_projected = jnp.concatenate([grad_queries, grad_keys, grad_values], axis=1)
    grad_query_value_bias = jnp.stack(
        [
            jnp.sum(grad_queries.astype(jnp.float32), axis=0),
            jnp.sum(grad_values.astype(jnp.float32), axis=0),
        ]
    )
    grad_project_in = jnp.einsum(
        "td,te->de", normed_a_low, grad_projected, preferred_element_type=jnp.float32
    )
    grad_normed_a = jnp.einsum(
        "te,de->td", grad_projected, back_in, preferred_element_type=jnp.float32
    )
    grad_from_first, grad_first_gain, grad_first_shift = first_back(grad_normed_a)
    input_grad = grad_middle + grad_from_first
    grad_shift = grad_shift_groups.transpose(1, 2, 3, 0, 4).reshape(2, GRID, GRID, head_count)
    grad_position_table = jnp.einsum(
        "ija,tijh->tah", shift_table, grad_shift, precision=lax.Precision.HIGHEST
    )
    weight_grads = (
        lax.psum_scatter(grad_project_in, "dp", scatter_dimension=0, tiled=True),
        lax.psum_scatter(grad_project_out, "dp", scatter_dimension=0, tiled=True),
        lax.psum_scatter(grad_expand, "dp", scatter_dimension=0, tiled=True),
        lax.psum_scatter(grad_reduce, "dp", scatter_dimension=0, tiled=True),
    )
    weight_grads = lax.psum(
        (weight_grads[0], weight_grads[1], weight_grads[2], weight_grads[3]), "rep"
    )
    small_sums = lax.psum(
        (
            grad_first_gain,
            grad_first_shift,
            grad_query_value_bias,
            grad_output_bias,
            grad_mixer_scale,
            grad_second_gain,
            grad_second_shift,
            grad_hidden_bias,
            grad_return_bias,
            grad_feed_scale,
            grad_position_table,
        ),
        ("dp", "rep"),
    )
    return (
        outputs.astype(jnp.bfloat16),
        input_grad,
        weight_grads[0],
        weight_grads[1],
        weight_grads[2],
        weight_grads[3],
        small_sums[0],
        small_sums[1],
        small_sums[2],
        small_sums[3],
        small_sums[4],
        small_sums[5],
        small_sums[6],
        small_sums[7],
        small_sums[8],
        small_sums[9],
        small_sums[10],
    )


FEATURES = 768
HIDDEN = 3072
SLOTS = 448
MESH = pl.DeviceIdType.MESH
LOW = jnp.bfloat16
FULL = jnp.float32

W_IN = (48, 2304, False, "A")
W_OUT = (48, 768, False, "A")
W_EXPAND = (48, 3072, False, "A")
W_REDUCE = (192, 768, True, "B")
WEIGHTS = (W_IN, W_OUT, W_EXPAND, W_REDUCE)

PARTS = ((0, 0, 1, "B"), (1, 0, 1, "A"), (2, 0, 2, "A"), (2, 1, 2, "A"), (3, 0, 2, "B"), (3, 1, 2, "A"))

CHUNK = 384
WIDE = 256
CHUNKS = (
    (3, 0, "A"), (3, 1, "A"), (2, 0, "A"), (2, 1, "A"), (2, 2, "A"), (2, 3, "B"), (1, 0, "A"), (0, 0, "B"), (0, 1, "B"), (0, 2, "B")
)
IN_COLUMNS = ((0, 4), (2, 3), (1, 5))


def aligned(index, step):
    return pl.multiple_of(index, step)


class Net:
    def __init__(self):
        dp, c = lax.axis_index("dp"), lax.axis_index("rep")
        z, y, x = dp // 4, lax.rem(dp // 2, 2), lax.rem(dp, 2)
        self.dp, self.c, self.z, self.y, self.x = dp, c, z, y, x
        self.ma = y * (1 - c) + x * c
        self.mb = x * (1 - c) + y * c
        self.wa, self.wb = 2 - c, 1 + c
        self.to_a = (dp + self.wa * (1 - 2 * self.ma), c)
        self.to_b = (dp + self.wb * (1 - 2 * self.mb), c)
        self.to_z = (lax.rem(dp + 4, 16), c)
        self.from_z = (lax.rem(dp + 12, 16), c)
        self.far_z = (lax.rem(dp + 8, 16), c)
        self.sib = (dp, 1 - c)

    def barrier(self):
        dp = self.dp
        sem = pltpu.get_barrier_semaphore()
        across = (dp - lax.rem(dp, 4) + 3 - lax.rem(dp, 4), self.c)
        for target in (self.to_a, self.to_b, self.to_z, self.from_z, self.far_z, self.sib, across):
            pl.semaphore_signal(sem, inc=1, device_id=target, device_id_type=MESH)
        pl.semaphore_wait(sem, 7)

    def back(self, steps):
        return lax.rem(self.z + 4 - steps, 4)

    def owner(self, z, a, b):
        return 4 * z + self.wa * a + self.wb * b


class Transfers:
    def __init__(self, net, send, recv):
        self.net, self.send, self.recv, self.sent = net, send, recv, []
        self.count = 0

    def push(self, src, dst, slot, to):
        copy = pltpu.make_async_remote_copy(
            src, dst, self.send.at[self.count], self.recv.at[slot], device_id=to, device_id_type=MESH
        )
        copy.start()
        self.sent.append(copy)
        self.count += 1
        return copy

    def sending_done(self, copy):
        copy.wait_send()
        self.sent = [other for other in self.sent if other is not copy]

    def landed(self, dst, slot):
        pltpu.make_async_remote_copy(
            dst, dst, self.send.at[0], self.recv.at[slot], device_id=self.net.sib, device_id_type=MESH
        ).wait_recv()

    def finish(self):
        for copy in self.sent:
            copy.wait_send()


class Gather(Transfers):
    def __init__(self, net, part, buf, send, recv):
        super().__init__(net, send, recv)
        weight, self.part, self.parts, self.order = part
        self.buf = buf
        self.rows, self.cols, self.by_rows, _ = WEIGHTS[weight]

    def span(self, c):
        half = (self.rows if self.by_rows else self.cols) // 2
        size = half // self.parts
        return c * half + self.part * size, size

    def block(self, owner):
        start, size = self.span(self.net.c)
        if self.by_rows:
            return self.buf.at[pl.ds(aligned(owner * self.rows + start, 16), size), :]
        return self.buf.at[pl.ds(aligned(owner * self.rows, 16), self.rows), pl.ds(aligned(start, 128), size)]

    def group(self, z, c):
        start, size = self.span(c)
        if self.by_rows:
            pieces = self.rows // size
            return self.buf.reshape(4, 4, pieces, size, self.cols).at[z, :, c * self.parts + self.part]
        rows = 4 * self.rows
        return self.buf.at[pl.ds(aligned(z * rows, 16), rows), pl.ds(aligned(start, 128), size)]

    def load(self, src, sem):
        start, size = self.span(self.net.c)
        if self.by_rows:
            part = src.at[pl.ds(aligned(start, 16), size), :]
        else:
            part = src.at[:, pl.ds(aligned(start, 128), size)]
        self.copy = pltpu.make_async_copy(part, self.block(self.net.dp), sem)
        self.copy.start()

    def along_z(self, ref, back, other):
        net = self.net
        if back == 0:
            self.push(ref, ref, 2 + other, net.to_z)
            self.push(ref, ref, 6 + other, net.from_z)
        elif back == 1:
            self.push(ref, ref, 4 + other, net.to_z)

    def jobs(self):
        net = self.net
        ma, mb = net.ma, net.mb

        def near(back, other):
            return self.block(net.owner(net.back(back), ma, mb + other * (1 - 2 * mb)))

        def far(back, other):
            return self.block(net.owner(net.back(back), 1 - ma, mb + other * (1 - 2 * mb)))

        def own():
            self.copy.wait()
            ref = near(0, 0)
            self.along_z(ref, 0, 0)
            self.push(ref, ref, 1, net.to_b)
            self.push(ref, ref, 8, net.to_a)

        def relay(back, other):
            def run():
                ref = near(back, other)
                self.landed(ref, back * 2 + other)
                if other == 0 or self.order != "B":
                    self.along_z(ref, back, other)
                if self.order == "B" and other == 0:
                    self.push(ref, ref, back * 2 + 1, net.to_b)
                self.push(ref, ref, 8 + back * 2 + other, net.to_a)

            return run

        def tail(back):
            def run():
                for other in (0, 1):
                    self.landed(far(back, other), 8 + back * 2 + other)
                ref = self.group(net.back(back), net.c)
                self.push(ref, ref, 16 + back, net.sib)

            return run

        def complete():
            for back in range(4):
                self.landed(self.group(net.back(back), 1 - net.c), 16 + back)

        relays = [relay(0, 1)] + [relay(back, other) for back in (1, 3, 2) for other in (0, 1)]
        return [own, *relays, *[tail(back) for back in (0, 1, 3, 2)], complete]


STEPS = (2, 1, 3, 0)


class Scatter(Transfers):
    def __init__(self, net, weight, column, order, refs, stage, send, recv):
        super().__init__(net, send, recv)
        self.order, self.weight, self.done = order, weight, False
        self.rows, self.cols, self.by_rows, _ = WEIGHTS[weight]
        self.g, self.ra, self.rb, self.rz = refs
        self.stage, self.column = stage, column
        self.rh = self.rows // 2 if self.by_rows else self.rows

    def produced(self, back):
        net = self.net
        self.push(self.g.at[net.back(back), 1 - net.ma], self.ra.at[back], back, net.to_a)

    def along_z(self, step, src):
        net = self.net
        self.push(src, self.rz.at[step], 8 + step, net.from_z if step == 1 else net.to_z)

    def add_into(self, dst, terms):
        total = dst[...].astype(FULL)
        for term in terms:
            total += term[...].astype(FULL)
        dst[...] = total.astype(LOW)

    def part_of_stage(self, c):
        if self.by_rows:
            return self.stage.at[pl.ds(aligned(c * self.rh, 16), self.rh), pl.ds(self.column * CHUNK, CHUNK)]
        return self.stage.at[:, pl.ds(aligned(self.first_column(c), 128), CHUNK)]

    def first_column(self, c):
        if self.cols == 3 * FEATURES:
            first, second = IN_COLUMNS[self.column]
            return (first + c * (second - first)) * CHUNK
        return c * (self.cols // 2) + self.column * CHUNK

    def last(self, terms):
        mine = self.part_of_stage(self.net.c)
        total = terms[0][...].astype(FULL)
        for term in terms[1:]:
            total += term[...].astype(FULL)
        mine[...] = total
        self.push(mine, mine, 11, self.net.sib)

    def got(self):
        self.landed(self.part_of_stage(1 - self.net.c), 11)
        self.done = True

    def jobs(self):
        net, g, ra, rb, rz = self.net, self.g, self.ra, self.rb, self.rz
        ma, mb = net.ma, net.mb

        def step_a(s):
            def run():
                back = STEPS[s]
                self.landed(ra.at[back], back)
                terms = [ra.at[back]]
                for k in ((), (), (0,), (1, 2))[s]:
                    self.landed(rz.at[k], 8 + k)
                    terms.append(rz.at[k])
                dst = g.at[net.back(back), ma]
                self.add_into(dst, terms)
                if s < 3:
                    self.along_z(s, dst)
                else:
                    self.push(dst.at[1 - mb], rb.at[0], 4, net.to_b)

            return run

        def final_a():
            self.landed(rb.at[0], 4)
            self.last([g.at[net.z, ma, mb], rb.at[0]])

        def first_b(back):
            def run():
                self.landed(ra.at[back], back)
                dst = g.at[net.back(back), ma]
                self.add_into(dst, [ra.at[back]])
                self.push(dst.at[1 - mb], rb.at[back], 4 + back, net.to_b)

            return run

        def step_b(s):
            def run():
                back = STEPS[s]
                self.landed(rb.at[back], 4 + back)
                terms = [rb.at[back]]
                for k in ((), (), (0,), (1, 2))[s]:
                    self.landed(rz.at[k], 8 + k)
                    terms.append(rz.at[k])
                dst = g.at[net.back(back), ma, mb]
                if s < 3:
                    self.add_into(dst, terms)
                    self.along_z(s, dst)
                else:
                    self.last([dst] + terms)

            return run

        if self.order == "A":
            steps = [step_a(s) for s in range(4)] + [final_a]
        else:
            steps = [first_b(back) for back in STEPS] + [step_b(s) for s in range(4)]
        return steps + [self.got]

    @staticmethod
    def shapes(weight, order):
        rows, _, by_rows, _ = WEIGHTS[weight]
        block = (rows // 2 if by_rows else rows, CHUNK)
        relay = (3,) if order == "B" else (3, 2)
        return [
            pltpu.VMEM((4, 2, 2) + block, LOW),
            pltpu.VMEM((4, 2) + block, LOW),
            pltpu.VMEM((4 if order == "B" else 1,) + block, LOW),
            pltpu.VMEM(relay + block, LOW),
        ]


class SmallSum(Transfers):
    def __init__(self, net, buf, landing, send, recv):
        super().__init__(net, send, recv)
        self.buf, self.landing = buf, landing
        self.place, self.floor = lax.rem(net.dp, 4), net.dp - lax.rem(net.dp, 4)

    def spread(self, first, own, targets):
        ref = self.landing.at[first + own]
        for slot, target in targets:
            self.push(ref, ref, slot, target)

    def gathered(self, first):
        for k in range(1, 4):
            self.landed(self.landing.at[0], first + k)
        return (self.landing[first] + self.landing[first + 1]) + (self.landing[first + 2] + self.landing[first + 3])

    def jobs(self):
        net = self.net

        def start():
            self.push(self.buf.at[0], self.landing.at[0], 0, net.sib)

        def plane():
            self.landed(self.landing.at[0], 0)
            self.landing[1 + self.place] = self.buf[0] + self.landing[0]
            self.spread(
                1, self.place, [(1 + k, (self.floor + lax.rem(self.place + k, 4), net.c)) for k in (1, 2, 3)]
            )

        def line():
            self.landing[5 + net.z] = self.gathered(1)
            self.spread(5, net.z, [(5 + k, (lax.rem(net.dp + 4 * k, 16), net.c)) for k in (1, 2, 3)])

        def last():
            self.buf[1] = self.gathered(5)

        return [start, plane, line, last]


def dot(left, right):
    return jnp.dot(left, right, preferred_element_type=FULL)


def dot_rows(left, right):
    return lax.dot_general(left, right, (((1,), (1,)), ((), ())), preferred_element_type=FULL)


def fold(values):
    return jnp.sum(values.reshape(values.shape[0] // 8, 8, values.shape[1]), axis=0)


def normalised(values):
    centre = values - jnp.mean(values, axis=-1, keepdims=True)
    inverse = lax.rsqrt(jnp.mean(centre * centre, axis=-1, keepdims=True) + EPS)
    return centre * inverse, inverse


BLOCK = 64
ROOT_HALF = 0.7071067811865476
DENSITY = 0.3989422804014327


class Line:
    def __init__(self, ref):
        self.ref = ref

    def __getitem__(self, index):
        cols = slice(None) if index is Ellipsis else index[1]
        return self.ref[cols].reshape(1, -1)


def layer_kernel(
    sizes, tokens_hbm, w_in_hbm, w_out_hbm, w_expand_hbm, w_reduce_hbm, cotangent_hbm,
    first_gain, first_shift, query_value_bias, output_bias, mixer_scale, second_gain, second_shift,
    hidden_bias, return_bias, feed_scale, position_table,
    outputs_hbm, input_grad_hbm, g_in_hbm, g_out_hbm, g_expand_hbm, g_reduce_hbm, small_out,
    w_in, w_out, w_expand, w_reduce,
    stage_in, stage_out, stage_expand, stage_reduce,
    tok, cot, normed_a_t, normed_b_t, blended_t, qkv, place_q, place_k, place_t,
    chances, mixed, branch, middle, act, act_t, act_t_far, slope, g_ret, g_ret_far, g_pre_far,
    g_branch_far, work, small, small_landing, table,
    load_sem, out_sem, gather_send, gather_recv, scatter_send, scatter_recv, swap_send, swap_recv,
    small_send, small_recv, free_sem, *scatter_refs,
):
    net = Net()
    first_gain, first_shift, output_bias, mixer_scale, second_gain, second_shift, hidden_bias, return_bias, feed_scale = map(
        Line,
        (first_gain, first_shift, output_bias, mixer_scale, second_gain, second_shift, hidden_bias, return_bias, feed_scale),
    )
    g_branch = g_ret
    normed = mixed
    c = net.c
    sibling = 1 - c

    weights = [w_in, w_out, w_expand, w_reduce]
    sources = [w_in_hbm, w_out_hbm, w_expand_hbm, w_reduce_hbm]
    jobs = []

    gathers = []
    for i, part in enumerate(PARTS):
        gather = Gather(net, part, weights[part[0]], gather_send.at[i], gather_recv.at[i])
        gather.load(sources[part[0]], load_sem.at[i])
        gathers.append(gather)
        jobs += gather.jobs()
    load_tok = pltpu.make_async_copy(tokens_hbm, tok, load_sem.at[len(PARTS)])
    load_cot = pltpu.make_async_copy(cotangent_hbm, cot, load_sem.at[len(PARTS) + 1])
    load_tok.start()
    load_cot.start()
    net.barrier()

    stages = [stage_in, stage_out, stage_expand, stage_reduce]
    scatters = []
    for i, (weight, column, order) in enumerate(CHUNKS):
        scatters.append(
            Scatter(net, weight, column, order, scatter_refs[4 * i : 4 * i + 4], stages[weight],
                    scatter_send.at[i], scatter_recv.at[i])
        )
    swaps = Transfers(net, swap_send, swap_recv)
    sums = SmallSum(net, small, small_landing, small_send, small_recv)
    for group in scatters + [sums]:
        jobs += group.jobs()

    held = []

    @jobs.append
    def _():
        load_tok.wait()
        load_cot.wait()

        def first_rows(i, carry):
            rows = pl.ds(aligned(i * BLOCK, BLOCK), BLOCK)
            unit, _ = normalised(tok[rows, :].astype(FULL))
            normed[rows, :] = (unit * first_gain[...] + first_shift[...]).astype(LOW)
            returned_grad = (cot[rows, :].astype(FULL) * feed_scale[...]).astype(LOW)
            g_ret[rows, :] = returned_grad
            return carry + fold(returned_grad.astype(FULL))

        total = lax.fori_loop(0, SLOTS // BLOCK, first_rows, jnp.zeros((8, FEATURES), FULL), unroll=True)
        small[0] = jnp.zeros_like(small[0])
        small[0, 12:13, :] = jnp.sum(total, axis=0, keepdims=True)
        held.append(swaps.push(g_ret, g_ret_far, 0, net.sib))

    def turn(source, target):
        for j in range(FEATURES // 128):
            target[0, j * 128 : (j + 1) * 128, :] = source[:, j * 128 : (j + 1) * 128].T

    @jobs.append
    def _():
        turn(normed, normed_a_t)
        swaps.push(normed_a_t.at[0], normed_a_t.at[1], 1, net.sib)

    lane128 = lax.broadcasted_iota(jnp.int32, (128, 128), 1)
    row128 = lax.broadcasted_iota(jnp.int32, (128, 128), 0)
    height, width = sizes[0, 0], sizes[0, 1]
    width_f = width.astype(FULL)
    live = (height * width).astype(FULL)

    def grid_place(slot):
        row = jnp.floor((slot + 0.5) / width_f)
        return row, slot - row * width_f

    @jobs.append
    def _():
        slot = lax.broadcasted_iota(jnp.int32, (SLOTS, 128), 0).astype(FULL)
        lane = lax.broadcasted_iota(jnp.int32, (SLOTS, 128), 1).astype(FULL)
        row, col = grid_place(slot)
        hit = jnp.where(jnp.where(lane < GRID, row, col + GRID) == lane, 1.0, 0.0)
        place_q[...] = hit.astype(LOW)
        place_k[...] = jnp.where(slot < live, hit, jnp.where(lane == GRID - 1, 1.0, 0.0)).astype(LOW)
        slot = lax.broadcasted_iota(jnp.int32, (128, SLOTS), 1).astype(FULL)
        lane = lax.broadcasted_iota(jnp.int32, (128, SLOTS), 0).astype(FULL)
        row, col = grid_place(slot)
        hit = jnp.where(lane < GRID, GRID - 1 - row, 2 * GRID - 1 - col) == lane
        place_t[...] = jnp.where(hit, 1.0, 0.0).astype(LOW)
        mirror = jnp.where(row128 + lane128 == 2 * GRID - 2, 1.0, 0.0).astype(LOW)
        for part in range(2):
            low_table = position_table[:, part, :].astype(LOW)
            table[12 * part : 12 * part + 12, :] = dot(low_table, mirror[: 2 * GRID - 1, :])

    def project(j):
        cols = slice(j * WIDE, (j + 1) * WIDE)
        part = dot(normed[...], w_in[:, cols])
        inner = slice((j % 3) * WIDE, (j % 3 + 1) * WIDE)
        if j < 3:
            part = (part + query_value_bias[0:1, inner]) * 0.125
        elif j >= 6:
            part = part + query_value_bias[1:2, inner]
        qkv[:, cols] = part.astype(LOW)

    for j in range(9):
        jobs.append(functools.partial(project, j))

    half_lane = lax.broadcasted_iota(jnp.int32, (SLOTS, 128), 1)
    no_key = (lane128 == GRID - 1) & (row128 < GRID) & (jnp.full((128, 128), live) < SLOTS)
    spans = ((0, 256), (256, SLOTS))

    def only(values, e):
        keep = half_lane < 64 if e == 0 else half_lane >= 64
        return jnp.where(keep, values, jnp.zeros_like(values))

    def bias_table(head):
        rows_part = jnp.broadcast_to(table[head : head + 1, :], (GRID, 128))
        cols_part = jnp.broadcast_to(table[12 + head : 13 + head, :], (GRID, 128))
        both = jnp.concatenate(
            [
                pltpu.roll(rows_part, 65, 1, stride=1, stride_axis=0),
                pltpu.roll(cols_part, 1, 1, stride=1, stride_axis=0),
            ],
            axis=0,
        )
        both = jnp.where(lane128 // GRID == row128 // GRID, both, 0.0)
        return jnp.where(no_key, MASKED, both).astype(LOW)

    boards = (work, branch)

    def score(head):
        pair, e = head // 2, head % 2
        keys = jnp.concatenate([qkv[:, 768 + pair * 128 : 896 + pair * 128], place_k[...]], axis=1)
        bias = dot(place_q[...], bias_table(head)).astype(LOW)
        asks = jnp.concatenate([only(qkv[:, pair * 128 : (pair + 1) * 128], e), bias], axis=1)
        boards[e][:, :SLOTS] = dot_rows(keys, asks)

    def attend(head):
        pair, e = head // 2, head % 2
        cols = slice(pair * 128, (pair + 1) * 128)
        if head == 0:
            score(0)
        if head < HEADS - 1:
            score(head + 1)
        for lo, hi in spans:
            scores = boards[e][:, lo:hi]
            raised = jnp.exp(scores - jnp.max(scores, axis=0, keepdims=True))
            chances[head, :, lo:hi] = (raised * (1.0 / jnp.sum(raised, axis=0, keepdims=True))).astype(LOW)
        v_head = qkv[:, 1536 + pair * 128 : 1664 + pair * 128].T[e * 64 : (e + 1) * 64, :]
        blended_t[0, head * 64 : (head + 1) * 64, :] = dot(v_head, chances[head]).astype(LOW)
        if e == 1:
            mixed[:, cols] = blended_t[0, cols, :].T
        if head == HEADS - 1:
            swaps.push(blended_t.at[0], blended_t.at[1], 2, net.sib)

    for head in range(HEADS):
        jobs.append(functools.partial(attend, head))

    @jobs.append
    def _():
        for j in range(3):
            cols = slice(j * WIDE, (j + 1) * WIDE)
            branch[:, cols] = dot(mixed[...], w_out[:, cols]) + output_bias[:, cols]

    @jobs.append
    def _():
        def middle_rows(i, carry):
            rows = pl.ds(aligned(i * BLOCK, BLOCK), BLOCK)
            mid = tok[rows, :].astype(FULL) + mixer_scale[...] * branch[rows, :]
            middle[rows, :] = mid
            unit, _ = normalised(mid)
            normed[rows, :] = (unit * second_gain[...] + second_shift[...]).astype(LOW)
            return carry

        lax.fori_loop(0, SLOTS // BLOCK, middle_rows, 0, unroll=True)
        turn(normed, normed_b_t)
        swaps.push(normed_b_t.at[0], normed_b_t.at[1], 3, net.sib)

    act_blocks = act_t.reshape(16, 2, 96, SLOTS)

    def hidden(j):
        cols = slice(j * WIDE, (j + 1) * WIDE)
        pre = dot(normed[...], w_expand[:, cols]) + hidden_bias[:, cols]
        share = 0.5 + 0.5 * lax.erf(pre * ROOT_HALF)
        active = (pre * share).astype(LOW)
        act[:, cols] = active
        slope[:, cols] = (share + pre * (DENSITY * jnp.exp(-0.5 * pre * pre))).astype(LOW)
        for k in range(2):
            act_t[j * WIDE + k * 128 : j * WIDE + (k + 1) * 128, :] = active[:, k * 128 : (k + 1) * 128].T

    for j in (0, 1, 2, 6, 7, 8, 3, 4, 5, 9, 10, 11):
        jobs.append(functools.partial(hidden, j))

    @jobs.append
    def _():
        held.append(swaps.push(act_blocks.at[:, sibling], act_t_far, 4, net.sib))

    def place_of(owner):
        oy, ox = owner // 2, owner % 2
        return oy * (1 - c) + ox * c, ox * (1 - c) + oy * c

    def weight_grad(index, order, left, left_far, right, right_far, chunks=1):
        back = STEPS[order]
        z = net.back(back)
        tile = (dot(left(z), right) + dot(left_far(z), right_far)).astype(LOW)
        for chunk in range(chunks):
            scatter = scatters[index + chunk]
            for owner in range(4):
                pa, pb = place_of(owner)
                rows = slice(owner * scatter.rh, (owner + 1) * scatter.rh)
                scatter.g[z, pa, pb] = tile[rows, chunk * CHUNK : (chunk + 1) * CHUNK]
            scatter.produced(back)

    def rows_of(ref, slot):
        return lambda z: ref[slot, pl.ds(aligned(z * 192, 64), 192), :]

    def grad_reduce(j, order):
        cols = slice(j * CHUNK, (j + 1) * CHUNK)
        if (j, order) == (0, 0):
            swaps.landed(g_ret_far, 0)
            swaps.landed(act_t_far, 4)
        weight_grad(
            j, order,
            lambda z: act_blocks[pl.ds(4 * z, 4), c].reshape(384, SLOTS),
            lambda z: act_t_far[pl.ds(4 * z, 4)].reshape(384, SLOTS),
            g_ret[:, cols], g_ret_far[:, cols],
        )

    for j in range(2):
        for order in range(4):
            jobs.append(functools.partial(grad_reduce, j, order))

    def grad_hidden(j):
        half = sibling if j < 6 else c
        cols = pl.ds(aligned(half * 1536 + (j % 6) * WIDE, 128), WIDE)
        part = (dot_rows(g_ret[...], w_reduce[cols, :]) * slope[:, cols].astype(FULL)).astype(LOW)
        slope[:, cols] = part
        summed = jnp.sum(part.astype(FULL), axis=0, keepdims=True)
        small[0, pl.ds(8 + 2 * half + (j % 6) // 3, 1), (j % 3) * WIDE : (j % 3 + 1) * WIDE] = summed
        if j == 5:
            swaps.push(slope.at[:, pl.ds(aligned(sibling * 1536, 128), 1536)], g_pre_far, 5, net.sib)

    for j in range(12):
        jobs.append(functools.partial(grad_hidden, j))

    def grad_expand(j, order):
        if (j, order) == (0, 0):
            swaps.landed(normed_b_t.at[1], 3)
            swaps.landed(g_pre_far, 5)
        weight_grad(
            2 + 2 * j, order, rows_of(normed_b_t, 0), rows_of(normed_b_t, 1),
            slope[:, pl.ds(aligned(c * 1536 + 2 * j * CHUNK, 128), 2 * CHUNK)],
            g_pre_far[:, 2 * j * CHUNK : 2 * (j + 1) * CHUNK], 2,
        )
        if (j, order) == (1, 3):
            pl.semaphore_signal(free_sem, inc=1, device_id=net.sib, device_id_type=MESH)

    def g_qkv_far(part):
        return g_pre_far.at[:, part * CHUNK : (part + 1) * CHUNK]

    for j in range(2):
        for order in range(4):
            jobs.append(functools.partial(grad_expand, j, order))

    def grad_normed_b(j):
        cols = slice(j * WIDE, (j + 1) * WIDE)
        work[:, cols] = dot_rows(slope[...], w_expand[cols, :])

    for j in range(3):
        jobs.append(functools.partial(grad_normed_b, j))

    zero = jnp.zeros((8, FEATURES), FULL)

    @jobs.append
    def _():
        swaps.sending_done(held.pop(0))

        def second_back(i, carry):
            gain_sum, shift_sum, mixer_sum, bias_sum = carry
            rows = pl.ds(aligned(i * BLOCK, BLOCK), BLOCK)
            unit, inverse = normalised(middle[rows, :])
            grad = work[rows, :]
            gain_sum += fold(grad * unit)
            shift_sum += fold(grad)
            scaled = grad * second_gain[...]
            moved = scaled - jnp.mean(scaled, axis=-1, keepdims=True)
            moved -= unit * jnp.mean(scaled * unit, axis=-1, keepdims=True)
            grad_middle = cot[rows, :].astype(FULL) + inverse * moved
            work[rows, :] = grad_middle
            mixer_sum += fold(grad_middle * branch[rows, :])
            grad_branch = (grad_middle * mixer_scale[...]).astype(LOW)
            g_branch[rows, :] = grad_branch
            bias_sum += fold(grad_branch.astype(FULL))
            return gain_sum, shift_sum, mixer_sum, bias_sum

        for line, total in zip((6, 7, 5, 4), lax.fori_loop(0, SLOTS // BLOCK, second_back, (zero,) * 4, unroll=True)):
            small[0, line : line + 1, :] = jnp.sum(total, axis=0, keepdims=True)
        swaps.push(g_branch.at[:, pl.ds(aligned(sibling * CHUNK, 128), CHUNK)], g_branch_far, 6, net.sib)

    @jobs.append
    def _():
        for j in range(3):
            cols = slice(j * WIDE, (j + 1) * WIDE)
            mixed[:, cols] = dot_rows(g_branch[...], w_out[cols, :]).astype(LOW)

    def grad_out(order):
        if order == 0:
            swaps.landed(blended_t.at[1], 2)
            swaps.landed(g_branch_far, 6)
        weight_grad(
            6, order, rows_of(blended_t, 0), rows_of(blended_t, 1),
            g_branch[:, pl.ds(aligned(c * CHUNK, 128), CHUNK)], g_branch_far[...],
        )

    for order in range(4):
        jobs.append(functools.partial(grad_out, order))

    lane64 = lax.broadcasted_iota(jnp.int32, (GRID, 128), 1)

    grad_boards = (act_t.at[0:SLOTS, :], act_t.at[SLOTS : 2 * SLOTS, :])
    parts = {}

    def grad_chance(head):
        pair, e = head // 2, head % 2
        value_cols = slice(1536 + pair * 128, 1664 + pair * 128)
        g_head = only(mixed[:, pair * 128 : (pair + 1) * 128], e)
        branch[:, :SLOTS] = dot_rows(qkv[:, value_cols], g_head)

    def attend_back(head):
        pair, e = head // 2, head % 2
        cols = slice(pair * 128, (pair + 1) * 128)
        key_cols = slice(768 + pair * 128, 896 + pair * 128)
        value_cols = slice(1536 + pair * 128, 1664 + pair * 128)
        board = grad_boards[e]
        if head == 0:
            swaps.sending_done(held.pop())
            grad_chance(0)
        for lo, hi in spans:
            share = chances[head, :, lo:hi].astype(FULL)
            weighed = share * branch[:, lo:hi]
            board[:, lo:hi] = (weighed - share * jnp.sum(weighed, axis=0, keepdims=True)).astype(LOW)
        if head < HEADS - 1:
            grad_chance(head + 1)
        asks = jnp.concatenate([only(qkv[:, cols], e), place_q[...]], axis=1)
        across = dot(board[...], asks)
        grad_values = dot(chances[head], only(mixed[:, cols], e))
        k_head = qkv[:, key_cols].T[e * 64 : (e + 1) * 64, :]
        grad_queries = dot(k_head, board[...]).astype(LOW).astype(FULL) * 0.125
        marks = across[:, 128:]
        high = marks.astype(LOW)
        low = (marks - high.astype(FULL)).astype(LOW)
        pairs = dot(place_t[...], jnp.concatenate([high, low], axis=1))
        pairs = pairs[:, :128] + pairs[:, 128:]
        rows_part = jnp.where(lane64 < GRID, pairs[:GRID, :], 0.0)
        cols_part = jnp.where(lane64 >= GRID, pairs[GRID:, :], 0.0)
        rows_part = pltpu.roll(rows_part, 0, 1, stride=1, stride_axis=0)
        cols_part = pltpu.roll(cols_part, 64, 1, stride=1, stride_axis=0)
        for line, part in ((head, rows_part), (12 + head, cols_part)):
            spot = (line % 6) * 128
            small[0, 14 + line // 6 : 15 + line // 6, spot : spot + 128] = jnp.sum(part, axis=0, keepdims=True)
        if e == 0:
            parts[pair] = grad_queries, across[:, :128], grad_values
            return
        first_queries, first_keys, first_values = parts.pop(pair)
        grad_queries = jnp.concatenate([first_queries, grad_queries], axis=0).T.astype(LOW)
        grad_values = (first_values + grad_values).astype(LOW)
        qkv[:, cols] = grad_queries
        qkv[:, key_cols] = (first_keys + across[:, :128]).astype(LOW)
        qkv[:, value_cols] = grad_values
        small[0, 2:3, cols] = jnp.sum(grad_queries.astype(FULL), axis=0, keepdims=True)
        small[0, 3:4, cols] = jnp.sum(grad_values.astype(FULL), axis=0, keepdims=True)
        for part in (0,) if pair == 2 else (1, 2) if pair == 5 else ():
            first = aligned(scatters[7 + part].first_column(sibling), 128)
            if part == 0:
                pl.semaphore_wait(free_sem, 1)
            swaps.push(qkv.at[:, pl.ds(first, CHUNK)], g_qkv_far(part), 7 + part, net.sib)

    for head in range(HEADS):
        jobs.append(functools.partial(attend_back, head))

    def grad_in(j, order):
        parts = (0,) if j == 0 else (1, 2)
        if (j, order) == (0, 0):
            swaps.landed(normed_a_t.at[1], 1)
        if order == 0:
            for part in parts:
                swaps.landed(g_qkv_far(part), 7 + part)
        own = [qkv[:, pl.ds(aligned(scatters[7 + part].first_column(c), 128), CHUNK)] for part in parts]
        far = [g_qkv_far(part)[...] for part in parts]
        weight_grad(
            7 + j, order, rows_of(normed_a_t, 0), rows_of(normed_a_t, 1),
            jnp.concatenate(own, axis=1), jnp.concatenate(far, axis=1), len(parts),
        )

    for j in range(2):
        for order in range(4):
            jobs.append(functools.partial(grad_in, j, order))

    def grad_normed_a(j):
        cols = slice(j * WIDE, (j + 1) * WIDE)
        branch[:, cols] = dot_rows(qkv[...], w_in[cols, :])

    for j in range(3):
        jobs.append(functools.partial(grad_normed_a, j))

    save_grad = pltpu.make_async_copy(work, input_grad_hbm, out_sem.at[0])
    save_out = pltpu.make_async_copy(mixed, outputs_hbm, out_sem.at[1])

    @jobs.append
    def _():
        def first_back(i, carry):
            gain_sum, shift_sum = carry
            rows = pl.ds(aligned(i * BLOCK, BLOCK), BLOCK)
            unit, inverse = normalised(tok[rows, :].astype(FULL))
            grad = branch[rows, :]
            gain_sum += fold(grad * unit)
            shift_sum += fold(grad)
            scaled = grad * first_gain[...]
            moved = scaled - jnp.mean(scaled, axis=-1, keepdims=True)
            moved -= unit * jnp.mean(scaled * unit, axis=-1, keepdims=True)
            work[rows, :] = work[rows, :] + inverse * moved
            return gain_sum, shift_sum

        for line, total in zip((0, 1), lax.fori_loop(0, SLOTS // BLOCK, first_back, (zero,) * 2, unroll=True)):
            small[0, line : line + 1, :] = jnp.sum(total, axis=0, keepdims=True)
        save_grad.start()

    def finish_rows(j):
        cols = slice(j * WIDE, (j + 1) * WIDE)
        returned = dot(act[...], w_reduce[:, cols]) + return_bias[:, cols]
        mixed[:, cols] = (middle[:, cols] + feed_scale[:, cols] * returned).astype(LOW)
        small[0, 13:14, cols] = jnp.sum(cot[:, cols].astype(FULL) * returned, axis=0, keepdims=True)
        if j == 2:
            save_out.start()

    for j in range(3):
        jobs.append(functools.partial(finish_rows, j))

    saves = {}
    for key in PLAN:
        jobs[key]()
        for weight, target in enumerate((g_in_hbm, g_out_hbm, g_expand_hbm, g_reduce_hbm)):
            if weight not in saves and all(scatter.done for scatter in scatters if scatter.weight == weight):
                saves[weight] = pltpu.make_async_copy(stages[weight], target, out_sem.at[2 + weight])
                saves[weight].start()
    small_out[...] = small[1]
    for group in gathers + scatters + [swaps, sums]:
        group.finish()
    for save in [save_grad, save_out, *saves.values()]:
        save.wait()


PLAN = (
    0, 13, 154, 26, 155, 156, 1, 14, 2, 27, 4, 8, 21, 15, 17, 3, 28, 34, 30, 5, 16, 18, 9, 6, 39, 29, 10, 22, 23, 31,
    19, 7, 32, 40, 20, 35, 41, 36, 43, 11, 33, 47, 24, 12, 157, 158, 42, 159, 160, 161, 162, 163, 164, 25, 165, 166,
    37, 44, 52, 167, 168, 45, 48, 169, 38, 170, 171, 46, 65, 49, 172, 53, 173, 174, 54, 175, 176, 50, 56, 177, 66,
    178, 179, 67, 51, 60, 180, 55, 69, 181, 182, 183, 184, 57, 58, 185, 186, 187, 188, 68, 73, 189, 190, 191, 192, 61,
    70, 62, 71, 59, 72, 74, 75, 193, 194, 195, 196, 63, 197, 198, 76, 199, 200, 64, 78, 77, 201, 202, 203, 204, 205,
    79, 206, 207, 208, 209, 210, 211, 212, 221, 222, 223, 84, 213, 80, 214, 215, 85, 216, 217, 218, 219, 220, 224, 90,
    225, 96, 230, 86, 91, 226, 97, 227, 228, 229, 231, 81, 232, 233, 102, 234, 108, 235, 103, 109, 236, 92, 237, 110,
    98, 242, 243, 244, 111, 245, 238, 117, 118, 239, 87, 240, 241, 112, 113, 82, 250, 123, 251, 104, 124, 246, 83,
    125, 247, 126, 248, 249, 88, 93, 127, 128, 252, 132, 89, 99, 141, 253, 133, 119, 254, 142, 255, 114, 134, 143,
    256, 135, 150, 144, 94, 105, 136, 151, 100, 129, 145, 95, 137, 146, 101, 120, 106, 115, 138, 107, 116, 130, 147,
    131, 152, 121, 122, 139, 140, 148, 149, 153,
)


def one_kernel(
    tokens, project_in, project_out, expand_weight, reduce_weight, first_gain, first_shift, query_value_bias,
    output_bias, mixer_scale, second_gain, second_shift, hidden_bias, return_bias, feed_scale, position_table,
    image_sizes, cotangent,
):
    vector = lambda v: v
    table = jnp.transpose(position_table, (2, 0, 1))
    anywhere = pl.BlockSpec(memory_space=pl.ANY)
    vmem = pl.BlockSpec(memory_space=pltpu.VMEM)
    low = lambda *shape: pltpu.VMEM(shape, LOW)
    full = lambda *shape: pltpu.VMEM(shape, FULL)
    dma = lambda *shape: pltpu.SemaphoreType.DMA(shape)
    like = jax.ShapeDtypeStruct
    scratch = [low(16 * w[0], w[1]) for w in WEIGHTS]
    scratch += [full(w[0], w[1]) for w in WEIGHTS]
    T, D, F = SLOTS, FEATURES, HIDDEN
    scratch += [
        low(T, D), low(T, D), low(2, D, T), low(2, D, T), low(2, D, T), low(T, 3 * D),
        low(T, 128), low(T, 128), low(128, T), low(HEADS, T, T), low(T, D), full(T, D), full(T, D),
        low(T, F), low(F, T), low(16, 96, T), low(T, F), low(T, D), low(T, D), low(T, F // 2),
        low(T, D // 2), full(T, D), full(2, 24, D), full(9, 24, D), full(24, 128),
        dma(len(PARTS) + 2), dma(6), dma(len(PARTS), 24), dma(len(PARTS), 20), dma(len(CHUNKS), 12), dma(len(CHUNKS), 12), dma(10), dma(10),
        dma(7), dma(9), pltpu.SemaphoreType.REGULAR,
    ]
    for weight, _, order in CHUNKS:
        scratch += Scatter.shapes(weight, order)
    results = pl.pallas_call(
        layer_kernel,
        out_shape=[
            like((T, D), LOW), like((T, D), FULL), like((48, 3 * D), FULL), like((48, D), FULL), like((48, F), FULL),
            like((192, D), FULL), like((24, D), FULL),
        ],
        in_specs=[pl.BlockSpec(memory_space=pltpu.SMEM)] + [anywhere] * 6 + [vmem] * 11,
        out_specs=[anywhere] * 6 + [vmem],
        scratch_shapes=scratch,
        compiler_params=pltpu.CompilerParams(
            collective_id=0, has_side_effects=True, vmem_limit_bytes=VMEM_BYTES
        ),
    )(
        image_sizes, tokens, project_in, project_out, expand_weight, reduce_weight, cotangent, vector(first_gain),
        vector(first_shift), query_value_bias, vector(output_bias), vector(mixer_scale), vector(second_gain),
        vector(second_shift), vector(hidden_bias), vector(return_bias), vector(feed_scale), table,
    )
    vectors = [(D,), (D,), (2, D), (D,), (D,), (D,), (D,), (F,), (D,), (D,), (HEADS, 2, 2 * GRID - 1)]
    handed = pl.pallas_call(
        handout,
        out_shape=[like(r.shape, r.dtype) for r in results[:6]] + [like(v, FULL) for v in vectors],
        in_specs=[anywhere] * 6 + [vmem],
        out_specs=[anywhere] * 6 + [vmem] * 11,
        scratch_shapes=[pltpu.VMEM(r.shape, r.dtype) for r in results[:6]] + [dma(2, 6)],
    )(*results)
    return (*handed[:16], jnp.transpose(handed[16], (1, 2, 0)))


def handout(*refs):
    large, small, saved, outs, held, sems = refs[:6], refs[6], refs[7:13], refs[13:24], refs[24:30], refs[30]
    loads = [pltpu.make_async_copy(large[i], held[i], sems.at[0, i]) for i in range(6)]
    copies = [pltpu.make_async_copy(held[i], saved[i], sems.at[1, i]) for i in range(6)]
    for load in loads:
        load.start()
    for load, copy in zip(loads, copies):
        load.wait()
        copy.start()
    for line, out in ((0, 0), (1, 1), (4, 3), (5, 4), (6, 5), (7, 6), (12, 8), (13, 9)):
        outs[out][...] = small[line, :]
    outs[2][...] = small[2:4, :]
    for k in range(4):
        outs[7][k * FEATURES : (k + 1) * FEATURES] = small[8 + k, :]
    for n in range(24):
        line = small[14 + n // 6 : 15 + n // 6, (n % 6) * 128 : (n % 6) * 128 + 2 * GRID - 1]
        outs[10][n % 12, n // 12 : n // 12 + 1, :] = line
    for copy in copies:
        copy.wait()


VMEM_BYTES = 64 * 2**20


def solution(mesh):
    placed = (
        P(("dp", "rep"), None),
        P("dp", None),
        P("dp", None),
        P("dp", None),
        P("dp", None),
        P(),
        P(),
        P(),
        P(),
        P(),
        P(),
        P(),
        P(),
        P(),
        P(),
        P(),
        P(("dp", "rep"), None),
        P(("dp", "rep"), None),
    )
    return jax.shard_map(
        one_kernel if tuple(mesh.shape.values()) == (16, 2) else shards,
        mesh=mesh,
        in_specs=placed,
        out_specs=(
            P(("dp", "rep"), None),
            P(("dp", "rep"), None),
            P("dp", None),
            P("dp", None),
            P("dp", None),
            P("dp", None),
            P(),
            P(),
            P(),
            P(),
            P(),
            P(),
            P(),
            P(),
            P(),
            P(),
            P(),
        ),
        check_vma=False,
    )
```
